512 devices in a mesh: gy: 32 (over z, core), gz: 16 (over y, x).
Axes of the slice: x: 4, y: 4, z: 16, core: 2. Of those that a mesh axis runs over, the one named last changes fastest.
Arguments:
- measured: float32 [16, 1024, 1024], P('gz', 'gy'), may hold values from -20 to 20
- point_spread: float32 [1024, 1024], P('gy'), may hold values from -0.005859375 to 0.005859375
- stencil_weights: float32 [3, 3, 3], replicated, may hold values from -0.9 to 0.9
- upstream: float32 [16, 1024, 1024], P('gz', 'gy'), may hold values from -6 to 6
Outputs:
- grad_measured: float32 [16, 1024, 1024], P('gz', 'gy')
- grad_stencil: float32 [3, 3, 3], replicated
The draws below stay inside these ranges and needn't reach their ends.
All inputs are finite; a program needn't handle non-finite values.
Results may differ from the reference program's by a relative error of at most 0.00021.
Values sent between devices are 32-bit elements; how exact they have to be, the bound alone decides.
No kernel may reach another device: no remote copies, remote signals or barrier semaphores. Data moves between devices by JAX's collectives and lax.ppermute only.
A program may use at most 64 MiB of HBM per device.

```python
import math
import jax
import jax.numpy as jnp

X = 1024
Y = 1024
ITERS = 2
Z = 16


def draw_measured(key, part):
    subkeys = jax.random.split(jax.random.fold_in(key, 11), 1)
    plane_index = jnp.arange(Z, dtype=jnp.float32)[:, None, None]
    attenuation = jnp.exp(-math.log(3.0) * plane_index / max(Z - 1, 1))
    return jnp.clip(jax.random.normal(subkeys[0], (Z, Y, X), jnp.float32), -6.0, 6.0) * attenuation


def block_levels(key, shape, cuts, smallest, largest):
    gain, own = 1.0, jax.random.fold_in(key, 6)
    for dim, blocks in cuts:
        heights = jnp.exp(jax.random.uniform(jax.random.fold_in(own, dim), (blocks,), jnp.float32, smallest / len(cuts), largest / len(cuts)))
        gain = gain * jnp.repeat(heights, shape[dim] // blocks).reshape([-1 if axis == dim else 1 for axis in range(len(shape))])
    return gain


def normal_values(own_key, extent, deviation, bound, pieces=(), kind=jnp.bfloat16):
    values = deviation * jax.random.normal(own_key, extent, jnp.float32)
    if pieces:
        values = values * block_levels(own_key, extent, pieces, -0.22, 0.18)
    return jnp.clip(values, -bound, bound).astype(kind)


def setup_inputs(seed: int = 0) -> dict:
    key_of = jax.random.split(jax.random.key(seed), 5)
    measured = draw_measured(jax.random.fold_in(key_of[4], 71), 0)
    point_spread = normal_values(key_of[1], (Y, X), (X * Y) ** -0.5, 0.005859375, ((0, 32),), jnp.float32)
    stencil_weights = normal_values(key_of[2], (3, 3, 3), 0.15, 0.9, (), jnp.float32)
    upstream = normal_values(key_of[3], (Z, Y, X), 1.0, 6.0, ((0, 16), (1, 32)), jnp.float32)
    return dict(measured=measured, point_spread=point_spread, stencil_weights=stencil_weights, upstream=upstream)


def apply_stencil(volume, kernel):
    planes, row_count, columns = volume.shape
    padded = jnp.pad(volume, 1)
    summed = jnp.zeros(volume.shape, jnp.float32)
    for shift_z in range(3):
        for shift_y in range(3):
            for shift_x in range(3):
                summed = summed + kernel[shift_z, shift_y, shift_x] * padded[shift_z:shift_z + planes, shift_y:shift_y + row_count, shift_x:shift_x + columns]
    return summed

def regularize(volume, kernel):
    mapped = apply_stencil(volume, kernel)
    return apply_stencil(mapped, kernel[::-1, ::-1, ::-1])

def filtered(volume, response):
    spectrum = jnp.fft.fft2(volume, axes=(1, 2))
    return jnp.real(jnp.fft.ifft2(spectrum * response, axes=(1, 2))).astype(jnp.float32)

def restore(measured, kernel, transfer):
    power_gain = jnp.real(transfer) ** 2 + jnp.imag(transfer) ** 2
    right_side = filtered(measured, jnp.conj(transfer))
    solution = jnp.zeros_like(right_side)
    residual = right_side
    direction = right_side
    norm_now = jnp.sum(residual * residual)
    for iteration in range(ITERS):
        applied = filtered(direction, power_gain) + regularize(direction, kernel)
        step_size = norm_now / jnp.sum(direction * applied)
        solution = solution + step_size * direction
        if iteration + 1 < ITERS:
            residual = residual - step_size * applied
            norm_next = jnp.sum(residual * residual)
            direction = residual + norm_next / norm_now * direction
            norm_now = norm_next
    return solution

def reference(measured, point_spread, stencil_weights, upstream):
    transfer = jnp.fft.fft2(point_spread)

    def forward(values, weights):
        return restore(values, weights, transfer)
    unused, pullback = jax.vjp(forward, measured, stencil_weights)
    grad_measured, grad_weights = pullback(upstream)
    return (grad_measured, grad_weights / math.sqrt(X * Y * Z))
```

```python
import functools
import math

import jax
import jax.numpy as jnp
import ml_dtypes
import numpy as np
from jax import lax
from jax.experimental import pallas as pl
from jax.experimental.pallas import tpu as pltpu
from jax.sharding import PartitionSpec as P

ROWS = 32
COLS = 1024
FRAME = 48
BLOCKS = 9
F32 = jnp.float32
BF16 = jnp.bfloat16
VMEM = 40 * 1024 * 1024


def split_table(table):
    high = table.astype(ml_dtypes.bfloat16)
    low = (table - high.astype(np.float64)).astype(ml_dtypes.bfloat16)
    return high, low


def x_tables():
    part, half, device, i = np.meshgrid(
        np.arange(2), np.arange(2), np.arange(32), np.arange(8), indexing="ij"
    )
    part, kx = part.reshape(-1, 1), (16 * device + 8 * half + i).reshape(-1, 1)
    x = np.arange(COLS)[None, :]
    angle = 2.0 * np.pi * ((kx * x) % COLS) / COLS
    flip = 1.0 - 2.0 * (x % 2)
    nyquist = (kx == 0) & (part == 1)
    wave = np.where(part == 0, np.cos(angle), -np.sin(angle))
    forward = np.where(nyquist, flip, wave)
    weight = np.where(kx == 0, 1.0, 2.0) / (COLS * 1024.0)
    return forward, forward * weight


def y_tables():
    q = np.arange(32)[:, None]
    s = np.arange(32)[None, :]
    angle = 2.0 * np.pi * ((q * s) % 32) / 32
    first = np.concatenate([np.cos(angle), np.sin(angle)], 0)
    lane = np.arange(128)
    part, half, t = lane // 64, lane // 32 % 2, lane % 32
    turn = 2.0 * np.pi * q * t[None, :] / 1024
    sign = np.where(part == 0, 1.0, -1.0)[None, :]
    turn_cos, turn_sin = np.cos(turn), np.sin(turn) * sign
    angle = 2.0 * np.pi * ((t[:, None] * t[None, :]) % 32) / 32
    pi, po = part[:, None], part[None, :]
    block = np.where(pi == po, np.cos(angle), np.where(pi > po, np.sin(angle), -np.sin(angle)))
    second = np.where(half[:, None] == half[None, :], block, 0.0)
    return first, turn_cos, turn_sin, second


X_FORWARD, X_INVERSE = x_tables()
Y_FIRST, TURN_COS, TURN_SIN, Y_SECOND = y_tables()


def halves(value):
    high = value.astype(BF16)
    return high, (value - high.astype(F32)).astype(BF16)


def dot(left, right):
    return lax.dot_general(left, right, (((1,), (0,)), ((), ())), preferred_element_type=F32)


def dot_nt(left, right):
    return lax.dot_general(left, right, (((1,), (1,)), ((), ())), preferred_element_type=F32)


def swap(value):
    return pltpu.roll(value, 64, 1)


def lanes(shape):
    return lax.broadcasted_iota(jnp.int32, shape, 1)


def sublanes(shape):
    return lax.broadcasted_iota(jnp.int32, shape, 0)


def x_forward(value, high_ref, low_ref):
    high, low = halves(value)
    both = jnp.concatenate([high] * 4 + [low] * 4, 0)
    group = lanes((256, 128)) // 32
    out = None
    for h in range(4):
        rows = slice(256 * h, 256 * h + 256)
        first = dot_nt(high_ref[rows, :], both)
        piece = first[:, :128] + first[:, 128:] + dot_nt(low_ref[rows, :], both[:128])
        out = piece if out is None else jnp.where(group == h, piece, out)
    return out


def x_inverse(spectra, high_ref, low_ref):
    lefts = []
    for value in spectra:
        turned = value.T
        lefts.append(jnp.concatenate([turned[32 * h : 32 * h + 32] for h in range(4)], 1))
    left = lefts[0] if len(lefts) == 1 else jnp.concatenate(lefts, 0)
    count = left.shape[0]
    high, low = halves(left)
    first = dot(jnp.concatenate([high, low], 0), high_ref[...])
    return first[:count] + first[count:] + dot(high, low_ref[...])


class Lateral:
    def __init__(self, refs):
        self.first_high, self.first_low, self.cos, self.sin, second_high, second_low, back_high, back_low = refs
        self.second = (second_high, second_low)
        self.back = (back_high, back_low)
        self.sign = jnp.where(lanes((32, 128)) < 64, 1.0, -1.0)

    def over_s(self, blocks, direction):
        high, low = halves(jnp.concatenate(blocks, 1))
        first_high, first_low = self.first_high[...], self.first_low[...]
        both = dot(first_high, high) + dot(first_high, low) + dot(first_low, high)
        out = []
        for i in range(len(blocks)):
            cols = slice(128 * i, 128 * i + 128)
            out.append(both[:32, cols] + direction * self.sign * swap(both[32:, cols]))
        return out

    def over_t(self, blocks, tables):
        high, low = halves(jnp.concatenate(blocks, 0))
        table_high, table_low = tables[0][...], tables[1][...]
        return dot(high, table_high) + dot(low, table_high) + dot(high, table_low)

    def forward(self, ref, offset, is_first):
        blocks = [ref[:, offset + i, :] for i in range(8)]
        lane = lanes((32, 128))
        nyquist = (lane >= 64) & (lane < 96)
        blocks.append(jnp.where(lane < 32, swap(blocks[0]), 0.0) * is_first)
        blocks[0] = jnp.where(nyquist, blocks[0] * (1.0 - is_first), blocks[0])
        blocks = self.over_s(blocks, 1.0)
        blocks = [z * self.cos[...] + swap(z) * self.sin[...] for z in blocks]
        return self.over_t(blocks, self.second)

    def inverse(self, spectrum, ref, offset, halo):
        all_rows = self.over_t([spectrum], self.back)
        blocks = [all_rows[32 * i : 32 * i + 32] for i in range(BLOCKS)]
        blocks = [z * self.cos[...] - swap(z) * self.sin[...] for z in blocks]
        blocks = self.over_s(blocks, -1.0)
        lane = lanes((32, 128))
        nyquist = (lane >= 64) & (lane < 96)
        blocks[0] = blocks[0] + jnp.where(nyquist, swap(blocks[8]), 0.0)
        t = lane % 32
        row = sublanes((32, 128))
        for i in range(8):
            ref[:, offset + i, :] = blocks[i]
            if halo:
                after = jnp.where((t < 8) & (row < 31), pltpu.roll(blocks[i], 31, 0), 0.0)
                before = jnp.where((t >= 24) & (row > 0), pltpu.roll(blocks[i], 1, 0), 0.0)
                ref[:, offset + 8 + i, :] = after + before


def product(real, imaginary, value):
    return real * value + imaginary * swap(value)


def spread_kernel(fields, high_ref, low_ref, *refs):
    out_ref = refs[fields]
    for f in range(fields):
        out_ref[:, 8 * f : 8 * f + 8, :] = x_forward(refs[f][...], high_ref, low_ref).reshape(32, 8, 128)


def first_filter_kernel(*refs):
    lateral = Lateral(refs[:8])
    is_first_ref, arrived, right, image, real_ref, imaginary_ref, power_ref, spectrum_ref = refs[8:]
    is_first = is_first_ref[0]
    transfer = lateral.forward(arrived, 8, is_first)
    observed = lateral.forward(arrived, 0, is_first)
    turned = swap(transfer)
    left = lanes(transfer.shape) < 64
    real = jnp.where(left, transfer, turned)
    imaginary = jnp.where(left, turned, -transfer)
    power = real * real + imaginary * imaginary
    spectrum = product(real, imaginary, observed)
    lateral.inverse(spectrum, right, 0, True)
    lateral.inverse(spectrum * power, image, 0, True)
    real_ref[...] = real
    imaginary_ref[...] = imaginary
    power_ref[...] = power
    spectrum_ref[...] = spectrum


def second_filter_kernel(*refs):
    lateral = Lateral(refs[:8])
    is_first_ref, arrived, power_ref, spectrum_ref, out_ref, image_ref = refs[8:]
    power = power_ref[...]
    image = power * spectrum_ref[...] + lateral.forward(arrived, 0, is_first_ref[0])
    lateral.inverse(power * image, out_ref, 0, True)
    image_ref[...] = image


def last_filter_kernel(*refs):
    lateral = Lateral(refs[:8])
    (is_first_ref, factor_ref, third, second, upstream, real_ref, imaginary_ref, power_ref, spectrum_ref, image_ref, out_ref) = refs[8:]
    is_first = is_first_ref[0]
    power = power_ref[...]
    image = image_ref[...]
    further = power * image + lateral.forward(second, 0, is_first)
    last = power * further + lateral.forward(third, 0, is_first)
    weights = lateral.forward(upstream, 0, is_first)
    total = factor_ref[0] * weights + factor_ref[1] * (power * weights + lateral.forward(upstream, 8, is_first))
    total = total + factor_ref[2] * spectrum_ref[...] + factor_ref[3] * image
    total = total + factor_ref[4] * further + factor_ref[5] * last
    lateral.inverse(product(real_ref[...], -imaginary_ref[...], total), out_ref, 0, False)


def gather_kernel(high_ref, low_ref, arrived, out_ref):
    main = arrived[:, 0:8, :].reshape(256, 128)
    halo = arrived[:, 8:16, :].reshape(256, 128)
    value = x_inverse([main, halo], high_ref, low_ref)
    out_ref[0:8, :] = value[56:64]
    out_ref[8:40, :] = value[0:32]
    out_ref[40:48, :] = value[32:40]


def final_kernel(high_ref, low_ref, arrived, out_ref):
    out_ref[...] = x_inverse([arrived[...].reshape(256, 128)], high_ref, low_ref)


def shifted_columns(value):
    column = lanes(value.shape)
    left = jnp.where(column >= 1, pltpu.roll(value, 1, 1), 0.0)
    right = jnp.where(column < COLS - 1, pltpu.roll(value, COLS - 1, 1), 0.0)
    return left, right


def stencil_sum(weight, source, start, cols):
    total = None
    for b in range(3):
        part = None
        for a in range(3):
            for c in range(3):
                term = weight(a, b, c) * source[c, start + a, :, cols]
                part = term if part is None else part + term
        if b == 0:
            part = pltpu.roll(part, 1, 0)
        elif b == 2:
            part = pltpu.roll(part, FRAME - 1, 0)
        total = part if total is None else total + part
    return total


def stencil_kernel(mode, place_ref, weights_ref, high_ref, low_ref, own, up1, up2, down1, down2, *refs):
    refs = list(refs)
    base = refs.pop(0) if mode == "add" else None
    back_ref = None if mode == "both" else refs.pop(0)
    mapped_ref, out_ref, source, middle = refs
    device, plane, planes = place_ref[0], place_ref[1], place_ref[2]
    for p, ref in enumerate((up2, up1, own, down1, down2)):
        value = ref[...]
        left, right = shifted_columns(value)
        source[0, p], source[1, p], source[2, p] = left, value, right
    row = sublanes((FRAME, 128))
    lowest = jnp.where(device > 0, 0, 8)
    highest = jnp.where(device < 31, FRAME, 40)
    inside = (row >= lowest) & (row < highest)

    def weight(a, b, c):
        return weights_ref[9 * a + 3 * b + c]

    def flipped(a, b, c):
        return weights_ref[26 - 9 * a - 3 * b - c]

    for p in range(3):
        here = plane + (p - 1)
        end = jnp.where((here >= 0) & (here < planes), highest, 0)
        valid = (row >= lowest) & (row < end)
        for k in range(8):
            cols = slice(128 * k, 128 * k + 128)
            value = stencil_sum(weight, source, p, cols)
            middle[1, p, :, cols] = jnp.where(valid, value, 0.0)
    for p in range(3):
        value = middle[1, p]
        left, right = shifted_columns(value)
        middle[0, p], middle[2, p] = left, right
    mapped_ref[...] = middle[1, 1]
    for k in range(8):
        cols = slice(128 * k, 128 * k + 128)
        value = jnp.where(inside, stencil_sum(flipped, middle, 0, cols), 0.0)
        source[1, 0, :, cols] = value
        if mode == "add":
            back_ref[:, cols] = base[:, cols] + value
    if mode == "both":
        out_ref[:, 0:8, :] = x_forward(own[8:40, :], high_ref, low_ref).reshape(32, 8, 128)
        out_ref[:, 8:16, :] = x_forward(source[1, 0, 8:40, :], high_ref, low_ref).reshape(32, 8, 128)
    else:
        out_ref[...] = x_forward(source[1, 0, 8:40, :], high_ref, low_ref).reshape(32, 8, 128)
    if mode == "plain":
        back_ref[...] = source[1, 0]


def moments_kernel(right, image, further, upstream, out_ref):
    b, ab, aab, u = (ref[8:40, :] for ref in (right, image, further, upstream))
    lane = lanes((1, 128))
    out = jnp.zeros((1, 128), F32)
    for k, value in enumerate((b * b, b * ab, ab * ab, ab * aab, u * b, u * ab)):
        out = jnp.where(lane == k, jnp.sum(value), out)
    out_ref[...] = out


def correlate_kernel(factor_ref, *refs):
    out_ref, scaled, mapped = refs[-3:]
    right, image, further, upstream = refs[0:3], refs[3:6], refs[6:9], refs[9:12]
    right_map, image_map, further_map, upstream_map = refs[12:16]
    f = [factor_ref[k] for k in range(6)]
    for p in range(3):
        scaled[p] = f[0] * upstream[p][...] + f[1] * right[p][...] + f[2] * image[p][...] + f[3] * further[p][...]
    mapped[0] = (
        f[0] * upstream_map[8:40, :] + f[1] * right_map[8:40, :] + f[2] * image_map[8:40, :] + f[3] * further_map[8:40, :]
    )
    mapped[1] = right_map[8:40, :]
    mapped[2] = f[4] * image_map[8:40, :]
    lane = lanes((1, 128))
    out = jnp.zeros((1, 128), F32)
    column = lanes((ROWS, COLS))
    left_edge, right_edge = column < COLS - 1, column >= 1
    for c in range(3):
        parts = []
        for k in range(3):
            value = mapped[k]
            if c == 0:
                value = jnp.where(left_edge, pltpu.roll(value, COLS - 1, 1), 0.0)
            elif c == 2:
                value = jnp.where(right_edge, pltpu.roll(value, 1, 1), 0.0)
            parts.append(value)
        for a in range(3):
            for b in range(3):
                rows = slice(7 + b, 39 + b)
                total = parts[0] * right[a][rows, :] + parts[1] * scaled[a, rows, :] + parts[2] * image[a][rows, :]
                out = jnp.where(lane == 9 * a + 3 * b + c, jnp.sum(total), out)
    out_ref[...] = out


def shape(*dims):
    return jax.ShapeDtypeStruct(dims, F32)


def call(body, out_shape, operands, scalars=0, scratch=(), flops=200_000_000):
    memory = [pl.BlockSpec(memory_space=pltpu.SMEM)] * scalars
    memory = memory + [pl.BlockSpec(memory_space=pltpu.VMEM)] * (len(operands) - scalars)
    return pl.pallas_call(
        body,
        out_shape=out_shape,
        in_specs=memory,
        out_specs=jax.tree.map(lambda _: pl.BlockSpec(memory_space=pltpu.VMEM), out_shape),
        scratch_shapes=list(scratch),
        compiler_params=pltpu.CompilerParams(vmem_limit_bytes=VMEM),
        cost_estimate=pl.CostEstimate(flops=flops, bytes_accessed=8_000_000, transcendentals=0),
    )(*operands)


def exchange(value):
    return lax.all_to_all(value, "gy", 0, 0, tiled=True)


def neighbours(value):
    size = lax.axis_size("gz")

    def moved(by):
        pairs = [(i, i + by) for i in range(size) if 0 <= i + by < size]
        return lax.ppermute(value, "gz", pairs)

    return value, moved(1), moved(2), moved(-1), moved(-2)


def summed(row):
    for axis in ("gy", "gz"):
        size = lax.axis_size(axis)
        copies = jnp.broadcast_to(row[None], (size, 1, 128))
        row = jnp.sum(lax.all_to_all(copies, axis, 0, 0, tiled=True), 0)
    return row[0]


def factors(m0, m1, m2, m3, u0, u1):
    def pair(m0, m1, m2, m3):
        step0 = m0 / m1
        norm1 = m0 - 2.0 * step0 * m1 + step0 * step0 * m2
        ratio = norm1 / m0
        keep = 1.0 + ratio
        curvature = keep * keep * m1 - 2.0 * keep * step0 * m2 + step0 * step0 * m3
        step1 = norm1 / curvature
        return step0 + step1 * keep, -step1 * step0

    (alpha, gamma), back = jax.vjp(pair, m0, m1, m2, m3)
    return (alpha, gamma, *back((u0, u1)))


def local(measured, point_spread, stencil_weights, upstream):
    cells = measured.size * lax.axis_size("gy") * lax.axis_size("gz")
    device, plane = lax.axis_index("gy"), lax.axis_index("gz")
    is_first = jnp.where(device == 0, 1.0, 0.0).astype(F32).reshape(1)
    place = jnp.stack([device, plane, jnp.int32(lax.axis_size("gz"))]).astype(jnp.int32)
    weights = stencil_weights.reshape(27)
    to_x = [jnp.asarray(table) for table in split_table(X_FORWARD)]
    from_x = [jnp.asarray(table) for table in split_table(X_INVERSE)]
    along_y = [jnp.asarray(table) for table in split_table(Y_FIRST)]
    along_y += [jnp.asarray(TURN_COS, F32), jnp.asarray(TURN_SIN, F32)]
    along_y += [jnp.asarray(table) for table in split_table(Y_SECOND)]
    along_y += [jnp.asarray(table) for table in split_table(Y_SECOND.T)]
    measured, upstream = measured[0], upstream[0]
    tile = (32, 8, 128)
    tiles = (32, 16, 128)
    spectral = (32 * BLOCKS, 128)
    frame = (FRAME, COLS)

    def stencil(mode, parts, *base):
        frames = (shape(*frame), shape(*frame)) if mode != "both" else (shape(*frame),)
        outs = (*frames, shape(*(tiles if mode == "both" else tile)))
        scratch = (pltpu.VMEM((3, 5, FRAME, COLS), F32), pltpu.VMEM((3, 3, FRAME, COLS), F32))
        operands = [place, weights, *to_x, *parts, *base]
        return call(functools.partial(stencil_kernel, mode), outs, operands, 2, scratch)

    def filter_call(body, outs, scalars, operands):
        count, end = len(scalars), len(scalars) + len(along_y)

        def ordered(*refs):
            body(*refs[count:end], *refs[:count], *refs[end:])

        return call(ordered, outs, [*scalars, *along_y, *operands], count)

    first = exchange(
        call(functools.partial(spread_kernel, 2), shape(*tiles), [*to_x, measured, point_spread])
    )

    size = lax.axis_size("gy")
    below = lax.ppermute(upstream[24:32], "gy", [(i, i + 1) for i in range(size - 1)])
    above = lax.ppermute(upstream[0:8], "gy", [(i + 1, i) for i in range(size - 1)])
    loss_parts = neighbours(jnp.concatenate([below, upstream, above], 0))
    loss_map, loss_out = stencil("both", loss_parts)
    loss_arrived = exchange(loss_out)

    right_out, image_out, real, imaginary, power, spectrum = filter_call(
        first_filter_kernel,
        (shape(*tiles), shape(*tiles), shape(*spectral), shape(*spectral), shape(*spectral), shape(*spectral)),
        [is_first],
        [first],
    )
    right = call(gather_kernel, shape(*frame), [*from_x, exchange(right_out)])
    blurred = call(gather_kernel, shape(*frame), [*from_x, exchange(image_out)])
    right_parts = neighbours(right)
    image, right_map, image_send = stencil("add", right_parts, blurred)
    further_out, image_spectrum = filter_call(
        second_filter_kernel,
        (shape(*tiles), shape(*spectral)),
        [is_first],
        [exchange(image_send), power, spectrum],
    )
    image_parts = neighbours(image)
    image_back, image_map, further_send = stencil("plain", image_parts)
    further_arrived = exchange(further_send)
    further = call(gather_kernel, shape(*frame), [*from_x, exchange(further_out)]) + image_back
    further_parts = neighbours(further)
    unused, further_map, last_send = stencil("plain", further_parts)
    last_arrived = exchange(last_send)

    moments = summed(call(moments_kernel, shape(1, 128), [right, image, further, loss_parts[0]]))
    alpha, gamma, g0, g1, g2, g3 = factors(*(moments[k] for k in range(6)))
    filter_factors = jnp.stack([alpha, gamma, 2.0 * g0, 2.0 * g1, 2.0 * g2, 2.0 * g3])
    result_out = filter_call(
        last_filter_kernel,
        shape(*tile),
        [is_first, filter_factors],
        [last_arrived, further_arrived, loss_arrived, real, imaginary, power, spectrum, image_spectrum],
    )
    grad_measured = call(final_kernel, shape(ROWS, COLS), [*from_x, exchange(result_out)])

    stencil_factors = jnp.stack([gamma, g1, 2.0 * g2, 2.0 * g3, 2.0 * g3, g3])
    operands = [stencil_factors]
    for parts in (right_parts, image_parts, further_parts, loss_parts):
        operands += [parts[1], parts[0], parts[3]]
    operands += [right_map, image_map, further_map, loss_map]
    scratch = (pltpu.VMEM((3, FRAME, COLS), F32), pltpu.VMEM((3, ROWS, COLS), F32))
    terms = summed(call(correlate_kernel, shape(1, 128), operands, 1, scratch))
    grad_stencil = terms[:27].reshape(3, 3, 3) / math.sqrt(cells)
    return grad_measured[None], grad_stencil


def solution(mesh):
    return jax.shard_map(
        local,
        mesh=mesh,
        in_specs=(P("gz", "gy", None), P("gy", None), P(), P("gz", "gy", None)),
        out_specs=(P("gz", "gy", None), P()),
        check_vma=False,
    )
```

```python
import functools
import math

import jax
import jax.numpy as jnp
import ml_dtypes
import numpy as np
from jax import lax
from jax.experimental import pallas as pl
from jax.experimental.pallas import tpu as pltpu
from jax.sharding import Mesh
from jax.sharding import PartitionSpec as P

GY = ("gy_0", "gy_1")
GZ = ("gz_0", "gz_1")
ROWS = 32
COLS = 1024
FRAME = 48
BLOCKS = 9
F32 = jnp.float32
BF16 = jnp.bfloat16
VMEM = 14 * 1024 * 1024


def split_table(table):
    high = table.astype(ml_dtypes.bfloat16)
    low = (table - high.astype(np.float64)).astype(ml_dtypes.bfloat16)
    return high, low


def x_table():
    part, half, device, i = np.meshgrid(
        np.arange(2), np.arange(2), np.arange(32), np.arange(8), indexing="ij"
    )
    kx = 2 * (16 * (device % 16) + 8 * half + i) + device // 16
    part, kx = part.reshape(-1, 1), kx.reshape(-1, 1)
    x = np.arange(COLS // 2)[None, :]
    angle = 2.0 * np.pi * ((kx * x) % COLS) / COLS
    flip = 1.0 - 2.0 * (x % 2)
    wave = np.where(part == 0, np.cos(angle), -np.sin(angle))
    return np.where((kx == 0) & (part == 1), flip, wave)


def y_tables():
    q = np.arange(32)[:, None]
    s = np.arange(32)[None, :]
    angle = 2.0 * np.pi * ((q * s) % 32) / 32
    first = np.concatenate([np.cos(angle), np.sin(angle)], 0)
    lane = np.arange(128)
    part, half, t = lane // 64, lane // 32 % 2, lane % 32
    turn = 2.0 * np.pi * q * t[None, :] / 1024
    sign = np.where(part == 0, 1.0, -1.0)[None, :]
    turn_cos, turn_sin = np.cos(turn), np.sin(turn) * sign
    angle = 2.0 * np.pi * ((t[:, None] * t[None, :]) % 32) / 32
    pi, po = part[:, None], part[None, :]
    block = np.where(pi == po, np.cos(angle), np.where(pi > po, np.sin(angle), -np.sin(angle)))
    second = np.where(half[:, None] == half[None, :], block, 0.0)
    return first, turn_cos, turn_sin, second


def packed_tables():
    first, turn_cos, turn_sin, second = y_tables()
    first = np.pad(first, ((0, 0), (0, 96)))
    tables = [*split_table(second), *split_table(second.T), *split_table(first)]
    turns = np.concatenate([turn_cos, turn_sin], 0).astype(np.float32)
    return np.concatenate(tables, 0), turns


X_TABLE = np.concatenate(split_table(x_table()), 0)
Y_TABLE, Y_TURNS = packed_tables()
SCALE = 2.0 / (COLS * 1024.0)


def halves(value):
    high = value.astype(BF16)
    return high, (value - high.astype(F32)).astype(BF16)


def dot(left, right):
    return lax.dot_general(left, right, (((1,), (0,)), ((), ())), preferred_element_type=F32)


def dot_nt(left, right):
    return lax.dot_general(left, right, (((1,), (1,)), ((), ())), preferred_element_type=F32)


def swap(value):
    return pltpu.roll(value, 64, 1)


def lanes(shape):
    return lax.broadcasted_iota(jnp.int32, shape, 1)


def sublanes(shape):
    return lax.broadcasted_iota(jnp.int32, shape, 0)


def x_forward(value, table_ref):
    left, right = value[:, : COLS // 2], value[:, COLS // 2 :]
    group = lanes((128, 128)) // 32
    outs = []
    for parity, folded in enumerate((left + right, left - right)):
        high, low = halves(folded)
        both = jnp.concatenate([high] * 4 + [low] * 4, 0)
        out = None
        for h in range(4):
            start = 256 * h + 128 * parity
            first = dot_nt(table_ref[start : start + 128, :], both)
            piece = first[:, :128] + first[:, 128:]
            piece = piece + dot_nt(table_ref[1024 + start : 1152 + start, :], both[:128])
            out = piece if out is None else jnp.where(group == h, piece, out)
        outs.append(out)
    return jnp.concatenate(outs, 0)


def x_inverse(spectra, table_ref):
    turned = [value.T for value in spectra]
    sums = []
    for parity in range(2):
        cols = slice(128 * parity, 128 * parity + 128)
        rows = [jnp.concatenate([v[32 * h : 32 * h + 32, cols] for h in range(4)], 1) for v in turned]
        left = rows[0] if len(rows) == 1 else jnp.concatenate(rows, 0)
        count = left.shape[0]
        high, low = halves(left)
        both = jnp.concatenate([high, low], 0)
        total = None
        for h in range(4):
            start = 256 * h + 128 * parity
            k = slice(128 * h, 128 * h + 128)
            first = dot(both[:, k], table_ref[start : start + 128, :])
            piece = first[:count] + first[count:] + dot(high[:, k], table_ref[1024 + start : 1152 + start, :])
            total = piece if total is None else total + piece
        sums.append(total)
    return jnp.concatenate([sums[0] + sums[1], sums[0] - sums[1]], 1)


class Lateral:
    def __init__(self, table, turns, is_first):
        self.second = (table[0:128, :], table[128:256, :])
        self.back = (table[256:384, :], table[384:512, :])
        self.first = (table[512:576, 0:32], table[576:640, 0:32])
        self.cos, self.sin = turns[0:32, :], turns[32:64, :]
        self.is_first = is_first
        self.sign = jnp.where(lanes((32, 128)) < 64, 1.0, -1.0)

    def over_s(self, blocks, direction):
        high, low = halves(jnp.concatenate(blocks, 1))
        both = dot(self.first[0], high) + dot(self.first[0], low) + dot(self.first[1], high)
        out = []
        for i in range(len(blocks)):
            cols = slice(128 * i, 128 * i + 128)
            out.append(both[:32, cols] + direction * self.sign * swap(both[32:, cols]))
        return out

    def over_t(self, value, tables):
        high, low = halves(value)
        return dot(high, tables[0]) + dot(low, tables[0]) + dot(high, tables[1])

    def forward(self, ref, offset):
        blocks = [ref[:, offset + i, :] for i in range(8)]
        lane = lanes((32, 128))
        nyquist = (lane >= 64) & (lane < 96)
        blocks.append(jnp.where(lane < 32, swap(blocks[0]), 0.0) * self.is_first)
        blocks[0] = jnp.where(nyquist, blocks[0] * (1.0 - self.is_first), blocks[0])
        blocks = self.over_s(blocks, 1.0)
        blocks = [z * self.cos + swap(z) * self.sin for z in blocks]
        return self.over_t(jnp.concatenate(blocks, 0), self.second)

    def inverse(self, spectrum):
        all_rows = self.over_t(spectrum, self.back)
        blocks = [all_rows[32 * i : 32 * i + 32] for i in range(BLOCKS)]
        blocks = [z * self.cos - swap(z) * self.sin for z in blocks]
        blocks = self.over_s(blocks, -1.0)
        lane = lanes((32, 128))
        nyquist = (lane >= 64) & (lane < 96)
        own = jnp.where(lane // 32 % 2 == 0, SCALE * (1.0 - 0.5 * self.is_first), SCALE)
        blocks[0] = (blocks[0] + jnp.where(nyquist, swap(blocks[8]), 0.0)) * own
        return [blocks[0]] + [z * SCALE for z in blocks[1:8]]

    def weighted_sum(self, value):
        lane, row = lanes(value.shape), sublanes(value.shape)
        weight = jnp.where((row < 32) & (lane // 32 % 2 == 0), 2.0 - self.is_first, 2.0)
        weight = jnp.where(row >= 256, 1.0, weight)
        return jnp.sum(value * weight) * (1.0 / (COLS * 1024.0))


def halo_rows(block):
    lane, row = lanes((32, 128)) % 32, sublanes((32, 128))
    after = jnp.where((lane < 8) & (row < 31), pltpu.roll(block, 31, 0), 0.0)
    before = jnp.where((lane >= 24) & (row > 0), pltpu.roll(block, 1, 0), 0.0)
    return after, before


def product(real, imaginary, value):
    return real * value + imaginary * swap(value)


def spread_kernel(table_ref, measured, point_spread, out_ref):
    for f, ref in enumerate((measured, point_spread)):
        out_ref[:, 8 * f : 8 * f + 8, :] = x_forward(ref[...], table_ref).reshape(32, 8, 128)


def first_filter_kernel(is_first_ref, table, turns, arrived, out_ref, real_ref, imaginary_ref, power_ref, spectrum_ref):
    lateral = Lateral(table, turns, is_first_ref[0])
    transfer = lateral.forward(arrived, 8)
    observed = lateral.forward(arrived, 0)
    turned = swap(transfer)
    left = lanes(transfer.shape) < 64
    real = jnp.where(left, transfer, turned)
    imaginary = jnp.where(left, turned, -transfer)
    power = real * real + imaginary * imaginary
    spectrum = product(real, imaginary, observed)
    right = lateral.inverse(spectrum)
    image = lateral.inverse(spectrum * power)
    for i in range(8):
        out_ref[:, i, :] = right[i]
        out_ref[:, 8 + i, :] = image[i]
        after, before = halo_rows(right[i])
        image_after, image_before = halo_rows(image[i])
        image_after, image_before = pltpu.roll(image_after, 8, 1), pltpu.roll(image_before, 120, 1)
        out_ref[:, 16 + i, :] = after + before + image_after + image_before
    real_ref[...] = real
    imaginary_ref[...] = imaginary
    power_ref[...] = power
    spectrum_ref[...] = spectrum


def second_filter_kernel(is_first_ref, table, turns, arrived, power_ref, spectrum_ref, row_b, row_ab, out_ref, image_ref):
    lateral = Lateral(table, turns, is_first_ref[0])
    power = power_ref[...]
    image = power * spectrum_ref[...] + lateral.forward(arrived, 0)
    filtered = power * image
    blocks = lateral.inverse(filtered)
    for i in range(8):
        out_ref[:, i, :] = blocks[i]
        after, before = halo_rows(blocks[i])
        out_ref[:, 8 + i, :] = after + before
    image_ref[...] = image
    row = row_b[...] + row_ab[...]
    row = row + jnp.where(lanes((1, 128)) == 3, lateral.weighted_sum(image * filtered), 0.0)
    out_ref[:, 8, :] = out_ref[:, 8, :] + pltpu.roll(jnp.broadcast_to(row, (32, 128)), 8, 1)


def last_filter_kernel(
    is_first_ref, factor_ref, table, turns, arrived, real_ref, imaginary_ref, power_ref, spectrum_ref, image_ref, out_ref
):
    lateral = Lateral(table, turns, is_first_ref[0])
    power = power_ref[...]
    image = image_ref[...]
    total = factor_ref[4] * image + factor_ref[5] * (power * image) + lateral.forward(arrived, 8)
    total = power * total + factor_ref[2] * spectrum_ref[...] + factor_ref[3] * image
    total = total + lateral.forward(arrived, 0)
    blocks = lateral.inverse(product(real_ref[...], -imaginary_ref[...], total))
    for i in range(8):
        out_ref[:, i, :] = blocks[i]


def gather_two_kernel(table_ref, arrived, right_ref, image_ref):
    tiles = [arrived[:, 8 * f : 8 * f + 8, :].reshape(256, 128) for f in range(3)]
    value = x_inverse(tiles, table_ref)
    right_ref[0:8, :] = value[88:96]
    right_ref[8:40, :] = value[0:32]
    right_ref[40:48, :] = value[64:72]
    image_ref[0:8, :] = value[80:88]
    image_ref[8:40, :] = value[32:64]
    image_ref[40:48, :] = value[72:80]


def gather_sum_kernel(table_ref, arrived, base, out_ref, row_ref):
    row = pltpu.roll(jnp.broadcast_to(jnp.sum(arrived[:, 8, :], 0, keepdims=True), (8, 128)), 120, 1)
    row_ref[...] = jnp.where(lanes((1, 128)) < 6, row[0:1], 0.0)
    tiles = [arrived[:, 8 * f : 8 * f + 8, :].reshape(256, 128) for f in range(2)]
    value = x_inverse(tiles, table_ref)
    out_ref[0:8, :] = base[0:8, :] + value[56:64]
    out_ref[8:40, :] = base[8:40, :] + value[0:32]
    out_ref[40:48, :] = base[40:48, :] + value[32:40]


def final_kernel(table_ref, arrived, out_ref):
    out_ref[...] = x_inverse([arrived[...].reshape(256, 128)], table_ref)


def shifted_columns(value):
    column = lanes(value.shape)
    left = jnp.where(column >= 1, pltpu.roll(value, 1, 1), 0.0)
    right = jnp.where(column < COLS - 1, pltpu.roll(value, COLS - 1, 1), 0.0)
    return left, right


def stencil_sum(weight, source, start, cols):
    total = None
    for b in range(3):
        part = None
        for a in range(3):
            for c in range(3):
                term = weight(a, b, c) * source[c, start + a, :, cols]
                part = term if part is None else part + term
        if b == 0:
            part = pltpu.roll(part, 1, 0)
        elif b == 2:
            part = pltpu.roll(part, FRAME - 1, 0)
        total = part if total is None else total + part
    return total


def apply_stencils(place_ref, weights_ref, parts, source, middle, back_ref):
    device, plane, planes = place_ref[0], place_ref[1], place_ref[2]
    own, up1, up2, down1, down2 = parts
    for p, ref in enumerate((up2, up1, own, down1, down2)):
        value = ref[...]
        left, right = shifted_columns(value)
        source[0, p], source[1, p], source[2, p] = left, value, right
    row = sublanes((FRAME, 128))
    lowest = jnp.where(device > 0, 0, 8)
    highest = jnp.where(device < 31, FRAME, 40)

    def weight(a, b, c):
        return weights_ref[9 * a + 3 * b + c]

    def flipped(a, b, c):
        return weights_ref[26 - 9 * a - 3 * b - c]

    for p in range(3):
        here = plane + (p - 1)
        end = jnp.where((here >= 0) & (here < planes), highest, 0)
        valid = (row >= lowest) & (row < end)
        for k in range(8):
            cols = slice(128 * k, 128 * k + 128)
            value = stencil_sum(weight, source, p, cols)
            middle[1, p, :, cols] = jnp.where(valid, value, 0.0)
    for p in range(3):
        value = middle[1, p]
        left, right = shifted_columns(value)
        middle[0, p], middle[2, p] = left, right
    inside = (row >= lowest) & (row < highest)
    for k in range(8):
        cols = slice(128 * k, 128 * k + 128)
        back_ref[:, cols] = jnp.where(inside, stencil_sum(flipped, middle, 0, cols), 0.0)


def row_of(values):
    lane = lanes((1, 128))
    out = jnp.zeros((1, 128), F32)
    for k, value in values:
        out = jnp.where(lane == k, jnp.sum(value), out)
    return out


def image_kernel(place, weights, table, o, u1, u2, d1, d2, blurred, upstream, image_ref, mapped_ref, out_ref, row_ref, *scratch):
    source, middle, back = scratch
    apply_stencils(place, weights, (o, u1, u2, d1, d2), source, middle, back)
    out_ref[...] = x_forward(back[8:40, :], table).reshape(32, 8, 128)
    mapped_ref[...] = middle[1, 1, 8:40, :]
    image_ref[...] = blurred[...] + back[...]
    b, ab, u = o[8:40, :], image_ref[8:40, :], upstream[...]
    row_ref[...] = row_of(((0, b * b), (1, b * ab), (2, ab * ab), (4, u * b), (5, u * ab)))


def loss_kernel(place, weights, o, u1, u2, d1, d2, back_ref, mapped_ref, source, middle):
    apply_stencils(place, weights, (o, u1, u2, d1, d2), source, middle, back_ref)
    mapped_ref[...] = middle[1, 1, 8:40, :]


def further_kernel(place, weights, o, u1, u2, d1, d2, back_ref, mapped_ref, row_ref, source, middle):
    apply_stencils(place, weights, (o, u1, u2, d1, d2), source, middle, back_ref)
    mapped = middle[1, 1, 8:40, :]
    mapped_ref[...] = mapped
    row_ref[...] = row_of(((3, mapped * mapped),))


def last_kernel(
    place, weights, factor, table, o, u1, u2, d1, d2, image_back, loss_back, upstream, mapped_ref, out_ref, source, middle, back
):
    apply_stencils(place, weights, (o, u1, u2, d1, d2), source, middle, back)
    mapped_ref[...] = middle[1, 1, 8:40, :]
    u, again = upstream[...], image_back[8:40, :]
    first = factor[0] * u + factor[1] * loss_back[8:40, :] + factor[4] * again + factor[5] * back[8:40, :]
    second = factor[1] * u + factor[5] * again
    out_ref[:, 0:8, :] = x_forward(first, table).reshape(32, 8, 128)
    out_ref[:, 8:16, :] = x_forward(second, table).reshape(32, 8, 128)


def correlate_kernel(factor_ref, *refs):
    out_ref, scaled, mapped = refs[-3:]
    right, image, further, upstream = refs[0:3], refs[3:6], refs[6:9], refs[9:12]
    right_map, image_map, further_map, upstream_map = refs[12:16]
    f = [factor_ref[k] for k in range(5)]
    for p in range(3):
        scaled[p] = f[0] * upstream[p][...] + f[1] * right[p][...] + f[2] * image[p][...] + f[3] * further[p][...]
    mapped[0] = (
        f[0] * upstream_map[...] + f[1] * right_map[...] + f[2] * image_map[...] + f[3] * further_map[...]
    )
    mapped[1] = right_map[...]
    mapped[2] = f[4] * image_map[...]
    lane = lanes((1, 128))
    out = jnp.zeros((1, 128), F32)
    column = lanes((ROWS, COLS))
    left_edge, right_edge = column < COLS - 1, column >= 1
    for c in range(3):
        parts = []
        for k in range(3):
            value = mapped[k]
            if c == 0:
                value = jnp.where(left_edge, pltpu.roll(value, COLS - 1, 1), 0.0)
            elif c == 2:
                value = jnp.where(right_edge, pltpu.roll(value, 1, 1), 0.0)
            parts.append(value)
        for a in range(3):
            for b in range(3):
                rows = slice(7 + b, 39 + b)
                total = parts[0] * right[a][rows, :] + parts[1] * scaled[a, rows, :] + parts[2] * image[a][rows, :]
                out = jnp.where(lane == 9 * a + 3 * b + c, jnp.sum(total), out)
    out_ref[...] = out


def shape(*dims):
    return jax.ShapeDtypeStruct(dims, F32)


STENCIL_SCRATCH = (pltpu.VMEM((3, 5, FRAME, COLS), F32), pltpu.VMEM((3, 3, FRAME, COLS), F32))
BACK_SCRATCH = (pltpu.VMEM((FRAME, COLS), F32),)


def call(body, out_shape, scalars, operands, scratch=(), flops=400_000_000):
    smem, vmem = pl.BlockSpec(memory_space=pltpu.SMEM), pl.BlockSpec(memory_space=pltpu.VMEM)
    return pl.pallas_call(
        body,
        out_shape=out_shape,
        in_specs=[smem] * len(scalars) + [vmem] * len(operands),
        out_specs=jax.tree.map(lambda _: vmem, out_shape),
        scratch_shapes=list(scratch),
        compiler_params=pltpu.CompilerParams(vmem_limit_bytes=VMEM),
        cost_estimate=pl.CostEstimate(flops=flops, bytes_accessed=4_000_000, transcendentals=0),
    )(*scalars, *operands)


def exchange(value):
    return lax.all_to_all(value, GY, 0, 0, tiled=True)


def neighbours(value):
    size = lax.axis_size(GZ)

    def moved(by):
        pairs = [(i, i + by) for i in range(size) if 0 <= i + by < size]
        return lax.ppermute(value, GZ, pairs)

    return value, moved(1), moved(2), moved(-1), moved(-2)


def with_rows(value):
    size = lax.axis_size(GY)
    below = lax.ppermute(value[24:32], GY, [(i, i + 1) for i in range(size - 1)])
    above = lax.ppermute(value[0:8], GY, [(i + 1, i) for i in range(size - 1)])
    return jnp.concatenate([below, value, above], 0)


def from_all(row, axis):
    size = lax.axis_size(axis)
    return lax.all_to_all(jnp.broadcast_to(row[None], (size, 1, 128)), axis, 0, 0, tiled=True)


def over_ring(row, axis):
    for bit in (1, 2, 4, 8):
        row = row + lax.ppermute(row, axis, [(i, i ^ bit) for i in range(16)])
    return row


def factors(m0, m1, m2, m3, u0, u1):
    def pair(m0, m1, m2, m3):
        step0 = m0 / m1
        norm1 = m0 - 2.0 * step0 * m1 + step0 * step0 * m2
        ratio = norm1 / m0
        keep = 1.0 + ratio
        curvature = keep * keep * m1 - 2.0 * keep * step0 * m2 + step0 * step0 * m3
        step1 = norm1 / curvature
        return step0 + step1 * keep, -step1 * step0

    (alpha, gamma), back = jax.vjp(pair, m0, m1, m2, m3)
    return (alpha, gamma, *back((u0, u1)))


def factors_kernel(rows, filter_ref, stencil_ref):
    total = jnp.sum(rows[...], 0)
    lane = lanes((1, 128))
    moments = [jnp.sum(jnp.where(lane == k, total, 0.0), axis=1, keepdims=True) for k in range(6)]
    alpha, gamma, g0, g1, g2, g3 = factors(*moments)
    for k, value in enumerate((alpha, gamma, 2.0 * g0, 2.0 * g1, 2.0 * g2, 2.0 * g3)):
        filter_ref[k] = value[0, 0]
    for k, value in enumerate((gamma, g1, 2.0 * g2, 2.0 * g3, 2.0 * g3)):
        stencil_ref[k] = value[0, 0]


def local(measured, point_spread, stencil_weights, upstream):
    cells = measured.size * lax.axis_size(GY) * lax.axis_size(GZ)
    device, plane = lax.axis_index(GY), lax.axis_index(GZ)
    is_first = jnp.where(device == 0, 1.0, 0.0).astype(F32).reshape(1)
    place = jnp.stack([device, plane, jnp.int32(lax.axis_size(GZ))]).astype(jnp.int32)
    weights = stencil_weights.reshape(27)
    table, along_y, turns = jnp.asarray(X_TABLE), jnp.asarray(Y_TABLE), jnp.asarray(Y_TURNS)
    measured, upstream = measured[0], upstream[0]
    tile, tiles, three = shape(32, 8, 128), shape(32, 16, 128), shape(32, 24, 128)
    spectral, frame, rows, row = shape(32 * BLOCKS, 128), shape(FRAME, COLS), shape(ROWS, COLS), shape(1, 128)

    first = exchange(call(spread_kernel, tiles, [], [table, measured, point_spread]))
    first, grown = lax.optimization_barrier((first, with_rows(upstream)))

    right_out, real, imaginary, power, spectrum = call(
        first_filter_kernel, (three,) + (spectral,) * 4, [is_first], [along_y, turns, first]
    )
    right_arrived = exchange(right_out)
    loss_parts = neighbours(grown)
    loss_back, loss_map = call(loss_kernel, (frame, rows), [place, weights], [*loss_parts], STENCIL_SCRATCH)
    right_arrived, loss_back = lax.optimization_barrier((right_arrived, loss_back))
    right, blurred = call(gather_two_kernel, (frame, frame), [], [table, right_arrived])

    right_parts = neighbours(right)
    image, right_map, image_send, row_b = call(
        image_kernel,
        (frame, rows, tile, row),
        [place, weights],
        [table, *right_parts, blurred, upstream],
        STENCIL_SCRATCH + BACK_SCRATCH,
    )
    image_arrived = exchange(image_send)
    image_parts = neighbours(image)
    image_back, image_map, row_ab = call(
        further_kernel, (frame, rows, row), [place, weights], [*image_parts], STENCIL_SCRATCH
    )
    image_arrived, image_back = lax.optimization_barrier((image_arrived, image_back))
    further_out, image_spectrum = call(
        second_filter_kernel,
        (tiles, spectral),
        [is_first],
        [along_y, turns, image_arrived, power, spectrum, row_b, row_ab],
    )
    further, row_sum = call(gather_sum_kernel, (frame, row), [], [table, exchange(further_out), image_back])
    smem = pl.BlockSpec(memory_space=pltpu.SMEM)
    filter_factors, stencil_factors = pl.pallas_call(
        factors_kernel,
        out_shape=(shape(6), shape(5)),
        in_specs=[pl.BlockSpec(memory_space=pltpu.VMEM)],
        out_specs=(smem, smem),
    )(from_all(row_sum, GZ))

    further_parts = neighbours(further)
    further_map, last_send = call(
        last_kernel,
        (rows, tiles),
        [place, weights, filter_factors],
        [table, *further_parts, image_back, loss_back, upstream],
        STENCIL_SCRATCH + BACK_SCRATCH,
    )
    last_arrived = exchange(last_send)

    operands = []
    for parts in (right_parts, image_parts, further_parts, loss_parts):
        operands += [parts[1], parts[0], parts[3]]
    operands += [right_map, image_map, further_map, loss_map]
    scratch = (pltpu.VMEM((3, FRAME, COLS), F32), pltpu.VMEM((3, ROWS, COLS), F32))
    terms = call(correlate_kernel, row, [stencil_factors], operands, scratch)
    terms = lax.psum(lax.psum(lax.psum(terms, "gz_1"), "gz_0"), "gy_1")
    last_arrived, terms = lax.optimization_barrier((last_arrived, terms))
    result_out = call(
        last_filter_kernel,
        tile,
        [is_first, filter_factors],
        [along_y, turns, last_arrived, real, imaginary, power, spectrum, image_spectrum],
    )
    result_out, terms = lax.optimization_barrier((result_out, terms))
    grad_measured = call(final_kernel, rows, [], [table, exchange(result_out)])
    terms = over_ring(terms, "gy_0")
    grad_stencil = terms[0, :27].reshape(3, 3, 3) / math.sqrt(cells)
    return grad_measured[None], grad_stencil


def solution(mesh):
    groups, planes = mesh.devices.shape
    finer = Mesh(mesh.devices.reshape(groups // 2, 2, 4, planes // 4), GY + GZ)
    return jax.shard_map(
        local,
        mesh=finer,
        in_specs=(P(GZ, GY, None), P(GY, None), P(), P(GZ, GY, None)),
        out_specs=(P(GZ, GY, None), P()),
        check_vma=False,
    )
```

```python
import functools
import math

import jax
import jax.numpy as jnp
import ml_dtypes
import numpy as np
from jax import lax
from jax.experimental import pallas as pl
from jax.experimental.pallas import tpu as pltpu
from jax.sharding import Mesh
from jax.sharding import PartitionSpec as P

GY = ("gy_0", "gy_1")
GZ = ("gz_0", "gz_1")
ROWS = 32
COLS = 1024
FRAME = 48
BLOCKS = 9
F32 = jnp.float32
BF16 = jnp.bfloat16
VMEM = 14 * 1024 * 1024


def split_table(table):
    high = table.astype(ml_dtypes.bfloat16)
    low = (table - high.astype(np.float64)).astype(ml_dtypes.bfloat16)
    return high, low


def x_table():
    part, half, device, i = np.meshgrid(
        np.arange(2), np.arange(2), np.arange(32), np.arange(8), indexing="ij"
    )
    kx = 2 * (16 * (device % 16) + 8 * half + i) + device // 16
    part, kx = part.reshape(-1, 1), kx.reshape(-1, 1)
    x = np.arange(COLS // 2)[None, :]
    angle = 2.0 * np.pi * ((kx * x) % COLS) / COLS
    flip = 1.0 - 2.0 * (x % 2)
    wave = np.where(part == 0, np.cos(angle), -np.sin(angle))
    return np.where((kx == 0) & (part == 1), flip, wave)


def y_tables():
    q = np.arange(32)[:, None]
    s = np.arange(32)[None, :]
    angle = 2.0 * np.pi * ((q * s) % 32) / 32
    first = np.concatenate([np.cos(angle), np.sin(angle)], 0)
    lane = np.arange(128)
    part, half, t = lane // 64, lane // 32 % 2, lane % 32
    turn = 2.0 * np.pi * q * t[None, :] / 1024
    sign = np.where(part == 0, 1.0, -1.0)[None, :]
    turn_cos, turn_sin = np.cos(turn), np.sin(turn) * sign
    angle = 2.0 * np.pi * ((t[:, None] * t[None, :]) % 32) / 32
    pi, po = part[:, None], part[None, :]
    block = np.where(pi == po, np.cos(angle), np.where(pi > po, np.sin(angle), -np.sin(angle)))
    second = np.where(half[:, None] == half[None, :], block, 0.0)
    return first, turn_cos, turn_sin, second


def packed_tables():
    first, turn_cos, turn_sin, second = y_tables()
    first = np.pad(first, ((0, 0), (0, 96)))
    tables = [*split_table(second), *split_table(second.T), *split_table(first)]
    return np.concatenate([*tables, turn_cos, turn_sin], 0).astype(np.float32)


X_TABLE = np.concatenate(split_table(x_table()), 0)
Y_TABLE = packed_tables()
SCALE = 2.0 / (COLS * 1024.0)


def halves(value):
    high = value.astype(BF16)
    return high, (value - high.astype(F32)).astype(BF16)


def dot(left, right):
    return lax.dot_general(left, right, (((1,), (0,)), ((), ())), preferred_element_type=F32)


def dot_nt(left, right):
    return lax.dot_general(left, right, (((1,), (1,)), ((), ())), preferred_element_type=F32)


def swap(value):
    return pltpu.roll(value, 64, 1)


def lanes(shape):
    return lax.broadcasted_iota(jnp.int32, shape, 1)


def sublanes(shape):
    return lax.broadcasted_iota(jnp.int32, shape, 0)


def x_forward(value, table_ref):
    left, right = value[:, : COLS // 2], value[:, COLS // 2 :]
    group = lanes((128, 128)) // 32
    outs = []
    for parity, folded in enumerate((left + right, left - right)):
        high, low = halves(folded)
        both = jnp.concatenate([high] * 4 + [low] * 4, 0)
        out = None
        for h in range(4):
            start = 256 * h + 128 * parity
            first = dot_nt(table_ref[start : start + 128, :], both)
            piece = first[:, :128] + first[:, 128:]
            piece = piece + dot_nt(table_ref[1024 + start : 1152 + start, :], both[:128])
            out = piece if out is None else jnp.where(group == h, piece, out)
        outs.append(out)
    return jnp.concatenate(outs, 0)


def x_inverse(spectra, table_ref):
    turned = [value.T for value in spectra]
    sums = []
    for parity in range(2):
        cols = slice(128 * parity, 128 * parity + 128)
        rows = [jnp.concatenate([v[32 * h : 32 * h + 32, cols] for h in range(4)], 1) for v in turned]
        left = rows[0] if len(rows) == 1 else jnp.concatenate(rows, 0)
        count = left.shape[0]
        high, low = halves(left)
        both = jnp.concatenate([high, low], 0)
        total = None
        for h in range(4):
            start = 256 * h + 128 * parity
            k = slice(128 * h, 128 * h + 128)
            first = dot(both[:, k], table_ref[start : start + 128, :])
            piece = first[:count] + first[count:] + dot(high[:, k], table_ref[1024 + start : 1152 + start, :])
            total = piece if total is None else total + piece
        sums.append(total)
    return jnp.concatenate([sums[0] + sums[1], sums[0] - sums[1]], 1)


class Lateral:
    def __init__(self, table, is_first):
        def piece(start, count, width):
            return table[start : start + count, 0:width].astype(BF16)

        self.second = (piece(0, 128, 128), piece(128, 128, 128))
        self.back = (piece(256, 128, 128), piece(384, 128, 128))
        self.first = (piece(512, 64, 32), piece(576, 64, 32))
        self.cos, self.sin = table[640:672, :], table[672:704, :]
        self.is_first = is_first
        self.sign = jnp.where(lanes((32, 128)) < 64, 1.0, -1.0)

    def over_s(self, blocks, direction):
        high, low = halves(jnp.concatenate(blocks, 1))
        both = dot(self.first[0], high) + dot(self.first[0], low) + dot(self.first[1], high)
        out = []
        for i in range(len(blocks)):
            cols = slice(128 * i, 128 * i + 128)
            out.append(both[:32, cols] + direction * self.sign * swap(both[32:, cols]))
        return out

    def over_t(self, value, tables):
        high, low = halves(value)
        return dot(high, tables[0]) + dot(low, tables[0]) + dot(high, tables[1])

    def forward(self, ref, offset):
        blocks = [ref[:, offset + i, :] for i in range(8)]
        lane = lanes((32, 128))
        nyquist = (lane >= 64) & (lane < 96)
        blocks.append(jnp.where(lane < 32, swap(blocks[0]), 0.0) * self.is_first)
        blocks[0] = jnp.where(nyquist, blocks[0] * (1.0 - self.is_first), blocks[0])
        blocks = self.over_s(blocks, 1.0)
        blocks = [z * self.cos + swap(z) * self.sin for z in blocks]
        return self.over_t(jnp.concatenate(blocks, 0), self.second)

    def inverse(self, spectrum):
        all_rows = self.over_t(spectrum, self.back)
        blocks = [all_rows[32 * i : 32 * i + 32] for i in range(BLOCKS)]
        blocks = [z * self.cos - swap(z) * self.sin for z in blocks]
        blocks = self.over_s(blocks, -1.0)
        lane = lanes((32, 128))
        nyquist = (lane >= 64) & (lane < 96)
        own = jnp.where(lane // 32 % 2 == 0, SCALE * (1.0 - 0.5 * self.is_first), SCALE)
        blocks[0] = (blocks[0] + jnp.where(nyquist, swap(blocks[8]), 0.0)) * own
        return [blocks[0]] + [z * SCALE for z in blocks[1:8]]

    def weighted_sum(self, value):
        lane, row = lanes(value.shape), sublanes(value.shape)
        weight = jnp.where((row < 32) & (lane // 32 % 2 == 0), 2.0 - self.is_first, 2.0)
        weight = jnp.where(row >= 256, 1.0, weight)
        return jnp.sum(value * weight) * (1.0 / (COLS * 1024.0))


def halo_rows(block):
    lane, row = lanes((32, 128)) % 32, sublanes((32, 128))
    after = jnp.where((lane < 8) & (row < 31), pltpu.roll(block, 31, 0), 0.0)
    before = jnp.where((lane >= 24) & (row > 0), pltpu.roll(block, 1, 0), 0.0)
    return after, before


def product(real, imaginary, value):
    return real * value + imaginary * swap(value)


def spread_kernel(table_ref, measured, point_spread, out_ref):
    for f, ref in enumerate((measured, point_spread)):
        out_ref[:, 8 * f : 8 * f + 8, :] = x_forward(ref[...], table_ref).reshape(32, 8, 128)


def first_filter_kernel(is_first_ref, table, arrived, out_ref, bank_ref):
    lateral = Lateral(table, is_first_ref[0])
    transfer = lateral.forward(arrived, 8)
    observed = lateral.forward(arrived, 0)
    turned = swap(transfer)
    left = lanes(transfer.shape) < 64
    real = jnp.where(left, transfer, turned)
    imaginary = jnp.where(left, turned, -transfer)
    power = real * real + imaginary * imaginary
    spectrum = product(real, imaginary, observed)
    right = lateral.inverse(spectrum)
    image = lateral.inverse(spectrum * power)
    for i in range(8):
        out_ref[:, i, :] = right[i]
        out_ref[:, 8 + i, :] = image[i]
        after, before = halo_rows(right[i])
        image_after, image_before = halo_rows(image[i])
        image_after, image_before = pltpu.roll(image_after, 8, 1), pltpu.roll(image_before, 120, 1)
        out_ref[:, 16 + i, :] = after + before + image_after + image_before
    for k, value in enumerate((real, imaginary, power, spectrum)):
        bank_ref[k] = value


def second_filter_kernel(is_first_ref, table, arrived, bank_ref, row_b, row_ab, out_ref, image_ref):
    lateral = Lateral(table, is_first_ref[0])
    power = bank_ref[2]
    image = power * bank_ref[3] + lateral.forward(arrived, 0)
    filtered = power * image
    blocks = lateral.inverse(filtered)
    for i in range(8):
        out_ref[:, i, :] = blocks[i]
        after, before = halo_rows(blocks[i])
        out_ref[:, 8 + i, :] = after + before
    image_ref[...] = image
    row = row_b[...] + row_ab[...]
    row = row + jnp.where(lanes((1, 128)) == 3, lateral.weighted_sum(image * filtered), 0.0)
    out_ref[:, 8, :] = out_ref[:, 8, :] + pltpu.roll(jnp.broadcast_to(row, (32, 128)), 8, 1)


def last_filter_kernel(
    is_first_ref, factor_ref, table, arrived, bank_ref, image_ref, terms, out_ref
):
    lateral = Lateral(table, is_first_ref[0])
    power = bank_ref[2]
    image = image_ref[...]
    total = factor_ref[4] * image + factor_ref[5] * (power * image) + lateral.forward(arrived, 8)
    total = power * total + factor_ref[2] * bank_ref[3] + factor_ref[3] * image
    total = total + lateral.forward(arrived, 0)
    blocks = lateral.inverse(product(bank_ref[0], -bank_ref[1], total))
    for i in range(8):
        out_ref[:, i, :] = blocks[i]
        out_ref[:, 8 + i, :] = jnp.broadcast_to(terms[...], (32, 128))


def gather_two_kernel(table_ref, arrived, right_ref, image_ref):
    tiles = [arrived[:, 8 * f : 8 * f + 8, :].reshape(256, 128) for f in range(3)]
    value = x_inverse(tiles, table_ref)
    right_ref[0:8, :] = value[88:96]
    right_ref[8:40, :] = value[0:32]
    right_ref[40:48, :] = value[64:72]
    image_ref[0:8, :] = value[80:88]
    image_ref[8:40, :] = value[32:64]
    image_ref[40:48, :] = value[72:80]


def gather_sum_kernel(table_ref, arrived, base, out_ref, row_ref):
    row = pltpu.roll(jnp.broadcast_to(jnp.sum(arrived[:, 8, :], 0, keepdims=True), (8, 128)), 120, 1)
    row_ref[...] = jnp.where(lanes((1, 128)) < 6, row[0:1], 0.0)
    tiles = [arrived[:, 8 * f : 8 * f + 8, :].reshape(256, 128) for f in range(2)]
    value = x_inverse(tiles, table_ref)
    out_ref[0:8, :] = base[0:8, :] + value[56:64]
    out_ref[8:40, :] = base[8:40, :] + value[0:32]
    out_ref[40:48, :] = base[40:48, :] + value[32:40]


def final_kernel(table_ref, arrived, out_ref, row_ref):
    out_ref[...] = x_inverse([arrived[:, 0:8, :].reshape(256, 128)], table_ref)
    row_ref[...] = jnp.sum(arrived[:, 8, :], 0, keepdims=True)


def shifted_columns(value):
    column = lanes(value.shape)
    left = jnp.where(column >= 1, pltpu.roll(value, 1, 1), 0.0)
    right = jnp.where(column < COLS - 1, pltpu.roll(value, COLS - 1, 1), 0.0)
    return left, right


def stencil_sum(weight, source, start, cols):
    total = None
    for b in range(3):
        part = None
        for a in range(3):
            for c in range(3):
                term = weight(a, b, c) * source[c, start + a, :, cols]
                part = term if part is None else part + term
        if b == 0:
            part = pltpu.roll(part, 1, 0)
        elif b == 2:
            part = pltpu.roll(part, FRAME - 1, 0)
        total = part if total is None else total + part
    return total


def apply_stencils(place_ref, weights_ref, parts, source, middle, back_ref):
    device, plane, planes = place_ref[0], place_ref[1], place_ref[2]
    own, up1, up2, down1, down2 = parts
    for p, ref in enumerate((up2, up1, own, down1, down2)):
        value = ref[...]
        left, right = shifted_columns(value)
        source[0, p], source[1, p], source[2, p] = left, value, right
    row = sublanes((FRAME, 128))
    lowest = jnp.where(device > 0, 0, 8)
    highest = jnp.where(device < 31, FRAME, 40)

    def weight(a, b, c):
        return weights_ref[9 * a + 3 * b + c]

    def flipped(a, b, c):
        return weights_ref[26 - 9 * a - 3 * b - c]

    for p in range(3):
        here = plane + (p - 1)
        end = jnp.where((here >= 0) & (here < planes), highest, 0)
        valid = (row >= lowest) & (row < end)
        for k in range(8):
            cols = slice(128 * k, 128 * k + 128)
            value = stencil_sum(weight, source, p, cols)
            middle[1, p, :, cols] = jnp.where(valid, value, 0.0)
    for p in range(3):
        value = middle[1, p]
        left, right = shifted_columns(value)
        middle[0, p], middle[2, p] = left, right
    inside = (row >= lowest) & (row < highest)
    for k in range(8):
        cols = slice(128 * k, 128 * k + 128)
        back_ref[:, cols] = jnp.where(inside, stencil_sum(flipped, middle, 0, cols), 0.0)


def row_of(values):
    lane = lanes((1, 128))
    out = jnp.zeros((1, 128), F32)
    for k, value in values:
        out = jnp.where(lane == k, jnp.sum(value), out)
    return out


def image_kernel(place, weights, table, o, u1, u2, d1, d2, blurred, upstream, image_ref, mapped_ref, out_ref, row_ref, *scratch):
    source, middle, back = scratch
    apply_stencils(place, weights, (o, u1, u2, d1, d2), source, middle, back)
    out_ref[...] = x_forward(back[8:40, :], table).reshape(32, 8, 128)
    mapped_ref[...] = middle[1, 1, 8:40, :]
    image_ref[...] = blurred[...] + back[...]
    b, ab, u = o[8:40, :], image_ref[8:40, :], upstream[...]
    row_ref[...] = row_of(((0, b * b), (1, b * ab), (2, ab * ab), (4, u * b), (5, u * ab)))


def loss_kernel(place, weights, o, u1, u2, d1, d2, back_ref, mapped_ref, source, middle):
    apply_stencils(place, weights, (o, u1, u2, d1, d2), source, middle, back_ref)
    mapped_ref[...] = middle[1, 1, 8:40, :]


def further_kernel(place, weights, o, u1, u2, d1, d2, back_ref, mapped_ref, row_ref, source, middle):
    apply_stencils(place, weights, (o, u1, u2, d1, d2), source, middle, back_ref)
    mapped = middle[1, 1, 8:40, :]
    mapped_ref[...] = mapped
    row_ref[...] = row_of(((3, mapped * mapped),))


def last_kernel(
    place, weights, factor, table, o, u1, u2, d1, d2, image_back, loss_back, upstream, mapped_ref, out_ref, source, middle, back
):
    apply_stencils(place, weights, (o, u1, u2, d1, d2), source, middle, back)
    mapped_ref[...] = middle[1, 1, 8:40, :]
    u, again = upstream[...], image_back[8:40, :]
    first = factor[0] * u + factor[1] * loss_back[8:40, :] + factor[4] * again + factor[5] * back[8:40, :]
    second = factor[1] * u + factor[5] * again
    out_ref[:, 0:8, :] = x_forward(first, table).reshape(32, 8, 128)
    out_ref[:, 8:16, :] = x_forward(second, table).reshape(32, 8, 128)


def correlate_kernel(factor_ref, *refs):
    out_ref, scaled, mapped = refs[-3:]
    right, image, further, upstream = refs[0:3], refs[3:6], refs[6:9], refs[9:12]
    right_map, image_map, further_map, upstream_map = refs[12:16]
    f = [factor_ref[k] for k in range(5)]
    for p in range(3):
        scaled[p] = f[0] * upstream[p][...] + f[1] * right[p][...] + f[2] * image[p][...] + f[3] * further[p][...]
    mapped[0] = (
        f[0] * upstream_map[...] + f[1] * right_map[...] + f[2] * image_map[...] + f[3] * further_map[...]
    )
    mapped[1] = right_map[...]
    mapped[2] = f[4] * image_map[...]
    lane = lanes((1, 128))
    out = jnp.zeros((1, 128), F32)
    column = lanes((ROWS, COLS))
    left_edge, right_edge = column < COLS - 1, column >= 1
    for c in range(3):
        parts = []
        for k in range(3):
            value = mapped[k]
            if c == 0:
                value = jnp.where(left_edge, pltpu.roll(value, COLS - 1, 1), 0.0)
            elif c == 2:
                value = jnp.where(right_edge, pltpu.roll(value, 1, 1), 0.0)
            parts.append(value)
        for a in range(3):
            for b in range(3):
                rows = slice(7 + b, 39 + b)
                total = parts[0] * right[a][rows, :] + parts[1] * scaled[a, rows, :] + parts[2] * image[a][rows, :]
                out = jnp.where(lane == 9 * a + 3 * b + c, jnp.sum(total), out)
    out_ref[...] = out


def shape(*dims):
    return jax.ShapeDtypeStruct(dims, F32)


STENCIL_SCRATCH = (pltpu.VMEM((3, 5, FRAME, COLS), F32), pltpu.VMEM((3, 3, FRAME, COLS), F32))
BACK_SCRATCH = (pltpu.VMEM((FRAME, COLS), F32),)


def call(body, out_shape, scalars, operands, scratch=(), flops=400_000_000):
    smem, vmem = pl.BlockSpec(memory_space=pltpu.SMEM), pl.BlockSpec(memory_space=pltpu.VMEM)
    return pl.pallas_call(
        body,
        out_shape=out_shape,
        in_specs=[smem] * len(scalars) + [vmem] * len(operands),
        out_specs=jax.tree.map(lambda _: vmem, out_shape),
        scratch_shapes=list(scratch),
        compiler_params=pltpu.CompilerParams(vmem_limit_bytes=VMEM),
        cost_estimate=pl.CostEstimate(flops=flops, bytes_accessed=4_000_000, transcendentals=0),
    )(*scalars, *operands)


def exchange(value):
    return lax.all_to_all(value, GY, 0, 0, tiled=True)


def neighbours(value):
    size = lax.axis_size(GZ)

    def moved(by):
        pairs = [(i, i + by) for i in range(size) if 0 <= i + by < size]
        return lax.ppermute(value, GZ, pairs)

    return value, moved(1), moved(2), moved(-1), moved(-2)


def with_rows(value):
    size = lax.axis_size(GY)
    below = lax.ppermute(value[24:32], GY, [(i, i + 1) for i in range(size - 1)])
    above = lax.ppermute(value[0:8], GY, [(i + 1, i) for i in range(size - 1)])
    return jnp.concatenate([below, value, above], 0)


def from_all(row, axis):
    size = lax.axis_size(axis)
    return lax.all_to_all(jnp.broadcast_to(row[None], (size, 1, 128)), axis, 0, 0, tiled=True)


def factors(m0, m1, m2, m3, u0, u1):
    def pair(m0, m1, m2, m3):
        step0 = m0 / m1
        norm1 = m0 - 2.0 * step0 * m1 + step0 * step0 * m2
        ratio = norm1 / m0
        keep = 1.0 + ratio
        curvature = keep * keep * m1 - 2.0 * keep * step0 * m2 + step0 * step0 * m3
        step1 = norm1 / curvature
        return step0 + step1 * keep, -step1 * step0

    (alpha, gamma), back = jax.vjp(pair, m0, m1, m2, m3)
    return (alpha, gamma, *back((u0, u1)))


def factors_kernel(rows, filter_ref, stencil_ref):
    total = jnp.sum(rows[...], 0)
    lane = lanes((1, 128))
    moments = [jnp.sum(jnp.where(lane == k, total, 0.0), axis=1, keepdims=True) for k in range(6)]
    alpha, gamma, g0, g1, g2, g3 = factors(*moments)
    for k, value in enumerate((alpha, gamma, 2.0 * g0, 2.0 * g1, 2.0 * g2, 2.0 * g3)):
        filter_ref[k] = value[0, 0]
    for k, value in enumerate((gamma, g1, 2.0 * g2, 2.0 * g3, 2.0 * g3)):
        stencil_ref[k] = value[0, 0]


def local(measured, point_spread, stencil_weights, upstream):
    cells = measured.size * lax.axis_size(GY) * lax.axis_size(GZ)
    device, plane = lax.axis_index(GY), lax.axis_index(GZ)
    is_first = jnp.where(device == 0, 1.0, 0.0).astype(F32).reshape(1)
    place = jnp.stack([device, plane, jnp.int32(lax.axis_size(GZ))]).astype(jnp.int32)
    weights = stencil_weights.reshape(27)
    table, along_y = jnp.asarray(X_TABLE), jnp.asarray(Y_TABLE)
    measured, upstream = measured[0], upstream[0]
    tile, tiles, three = shape(32, 8, 128), shape(32, 16, 128), shape(32, 24, 128)
    spectral, frame, rows, row = shape(32 * BLOCKS, 128), shape(FRAME, COLS), shape(ROWS, COLS), shape(1, 128)

    first = exchange(call(spread_kernel, tiles, [], [table, measured, point_spread]))
    first, grown = lax.optimization_barrier((first, with_rows(upstream)))

    right_out, bank = call(
        first_filter_kernel, (three, shape(4, 32 * BLOCKS, 128)), [is_first], [along_y, first]
    )
    right_arrived = exchange(right_out)
    loss_parts = neighbours(grown)
    loss_back, loss_map = call(loss_kernel, (frame, rows), [place, weights], [*loss_parts], STENCIL_SCRATCH)
    right_arrived, loss_back = lax.optimization_barrier((right_arrived, loss_back))
    right, blurred = call(gather_two_kernel, (frame, frame), [], [table, right_arrived])

    right_parts = neighbours(right)
    image, right_map, image_send, row_b = call(
        image_kernel,
        (frame, rows, tile, row),
        [place, weights],
        [table, *right_parts, blurred, upstream],
        STENCIL_SCRATCH + BACK_SCRATCH,
    )
    image_arrived = exchange(image_send)
    image_parts = neighbours(image)
    image_back, image_map, row_ab = call(
        further_kernel, (frame, rows, row), [place, weights], [*image_parts], STENCIL_SCRATCH
    )
    image_arrived, image_back = lax.optimization_barrier((image_arrived, image_back))
    further_out, image_spectrum = call(
        second_filter_kernel,
        (tiles, spectral),
        [is_first],
        [along_y, image_arrived, bank, row_b, row_ab],
    )
    further, row_sum = call(gather_sum_kernel, (frame, row), [], [table, exchange(further_out), image_back])
    moments = from_all(row_sum, GZ)
    further, moments = lax.optimization_barrier((further, moments))
    smem = pl.BlockSpec(memory_space=pltpu.SMEM)
    filter_factors, stencil_factors = pl.pallas_call(
        factors_kernel,
        out_shape=(shape(6), shape(5)),
        in_specs=[pl.BlockSpec(memory_space=pltpu.VMEM)],
        out_specs=(smem, smem),
    )(moments)

    further_parts = neighbours(further)
    further_map, last_send = call(
        last_kernel,
        (rows, tiles),
        [place, weights, filter_factors],
        [table, *further_parts, image_back, loss_back, upstream],
        STENCIL_SCRATCH + BACK_SCRATCH,
    )
    last_arrived = exchange(last_send)

    operands = []
    for parts in (right_parts, image_parts, further_parts, loss_parts):
        operands += [parts[1], parts[0], parts[3]]
    operands += [right_map, image_map, further_map, loss_map]
    scratch = (pltpu.VMEM((3, FRAME, COLS), F32), pltpu.VMEM((3, ROWS, COLS), F32))
    terms = call(correlate_kernel, row, [stencil_factors], operands, scratch)
    terms = lax.psum(lax.psum(terms, "gz_1"), "gz_0")
    result_out = call(
        last_filter_kernel,
        tiles,
        [is_first, filter_factors],
        [along_y, last_arrived, bank, image_spectrum, terms],
    )
    grad_measured, terms = call(final_kernel, (rows, row), [], [table, exchange(result_out)])
    grad_stencil = terms[0, :27].reshape(3, 3, 3) / math.sqrt(cells)
    return grad_measured[None], grad_stencil


def solution(mesh):
    groups, planes = mesh.devices.shape
    finer = Mesh(mesh.devices.reshape(groups // 2, 2, 4, planes // 4), GY + GZ)
    return jax.shard_map(
        local,
        mesh=finer,
        in_specs=(P(GZ, GY, None), P(GY, None), P(), P(GZ, GY, None)),
        out_specs=(P(GZ, GY, None), P()),
        check_vma=False,
    )
```

```python
import functools
import math

import jax
import jax.numpy as jnp
import ml_dtypes
import numpy as np
from jax import lax
from jax.experimental import pallas as pl
from jax.experimental.pallas import tpu as pltpu
from jax.sharding import PartitionSpec as P

GY = "gy"
GZ = "gz"
ROWS = 32
COLS = 1024
FRAME = 48
BLOCKS = 9
F32 = jnp.float32
BF16 = jnp.bfloat16
VMEM = 60 * 1024 * 1024


def split_table(table):
    high = table.astype(ml_dtypes.bfloat16)
    low = (table - high.astype(np.float64)).astype(ml_dtypes.bfloat16)
    return high, low


def x_table():
    part, half, device, i = np.meshgrid(
        np.arange(2), np.arange(2), np.arange(32), np.arange(8), indexing="ij"
    )
    kx = 2 * (16 * (device % 16) + 8 * half + i) + device // 16
    part, kx = part.reshape(-1, 1), kx.reshape(-1, 1)
    x = np.arange(COLS // 2)[None, :]
    angle = 2.0 * np.pi * ((kx * x) % COLS) / COLS
    flip = 1.0 - 2.0 * (x % 2)
    wave = np.where(part == 0, np.cos(angle), -np.sin(angle))
    return np.where((kx == 0) & (part == 1), flip, wave)


def y_tables():
    q = np.arange(32)[:, None]
    s = np.arange(32)[None, :]
    angle = 2.0 * np.pi * ((q * s) % 32) / 32
    first = np.concatenate([np.cos(angle), np.sin(angle)], 0)
    lane = np.arange(128)
    part, half, t = lane // 64, lane // 32 % 2, lane % 32
    turn = 2.0 * np.pi * q * t[None, :] / 1024
    sign = np.where(part == 0, 1.0, -1.0)[None, :]
    turn_cos, turn_sin = np.cos(turn), np.sin(turn) * sign
    angle = 2.0 * np.pi * ((t[:, None] * t[None, :]) % 32) / 32
    pi, po = part[:, None], part[None, :]
    block = np.where(pi == po, np.cos(angle), np.where(pi > po, np.sin(angle), -np.sin(angle)))
    second = np.where(half[:, None] == half[None, :], block, 0.0)
    return first, turn_cos, turn_sin, second


def packed_tables():
    first, turn_cos, turn_sin, second = y_tables()
    first = np.pad(first, ((0, 0), (0, 96)))
    tables = [*split_table(second), *split_table(second.T), *split_table(first)]
    return np.concatenate([*tables, turn_cos, turn_sin], 0).astype(np.float32)


X_TABLE = np.concatenate(split_table(x_table()), 0)
Y_TABLE = packed_tables()
SCALE = 2.0 / (COLS * 1024.0)


def halves(value):
    high = value.astype(BF16)
    return high, (value - high.astype(F32)).astype(BF16)


def dot(left, right):
    return lax.dot_general(left, right, (((1,), (0,)), ((), ())), preferred_element_type=F32)


def dot_nt(left, right):
    return lax.dot_general(left, right, (((1,), (1,)), ((), ())), preferred_element_type=F32)


def swap(value):
    return pltpu.roll(value, 64, 1)


def lanes(shape):
    return lax.broadcasted_iota(jnp.int32, shape, 1)


def sublanes(shape):
    return lax.broadcasted_iota(jnp.int32, shape, 0)


def x_forward(value, table_ref):
    left, right = value[:, : COLS // 2], value[:, COLS // 2 :]
    group = lanes((128, 128)) // 32
    outs = []
    for parity, folded in enumerate((left + right, left - right)):
        high, low = halves(folded)
        both = jnp.concatenate([high] * 4 + [low] * 4, 0)
        out = None
        for h in range(4):
            start = 256 * h + 128 * parity
            first = dot_nt(table_ref[start : start + 128, :], both)
            piece = first[:, :128] + first[:, 128:]
            piece = piece + dot_nt(table_ref[1024 + start : 1152 + start, :], both[:128])
            out = piece if out is None else jnp.where(group == h, piece, out)
        outs.append(out)
    return jnp.concatenate(outs, 0)


def x_inverse(spectra, table_ref):
    turned = [value.T for value in spectra]
    sums = []
    for parity in range(2):
        cols = slice(128 * parity, 128 * parity + 128)
        rows = [jnp.concatenate([v[32 * h : 32 * h + 32, cols] for h in range(4)], 1) for v in turned]
        left = rows[0] if len(rows) == 1 else jnp.concatenate(rows, 0)
        count = left.shape[0]
        high, low = halves(left)
        both = jnp.concatenate([high, low], 0)
        total = None
        for h in range(4):
            start = 256 * h + 128 * parity
            k = slice(128 * h, 128 * h + 128)
            first = dot(both[:, k], table_ref[start : start + 128, :])
            piece = first[:count] + first[count:] + dot(high[:, k], table_ref[1024 + start : 1152 + start, :])
            total = piece if total is None else total + piece
        sums.append(total)
    return jnp.concatenate([sums[0] + sums[1], sums[0] - sums[1]], 1)


class Lateral:
    def __init__(self, table, is_first):
        def piece(start, count, width):
            return table[start : start + count, 0:width].astype(BF16)

        self.second = (piece(0, 128, 128), piece(128, 128, 128))
        self.back = (piece(256, 128, 128), piece(384, 128, 128))
        self.first = (piece(512, 64, 32), piece(576, 64, 32))
        self.cos, self.sin = table[640:672, :], table[672:704, :]
        self.is_first = is_first
        self.sign = jnp.where(lanes((32, 128)) < 64, 1.0, -1.0)

    def over_s(self, blocks, direction):
        high, low = halves(jnp.concatenate(blocks, 1))
        both = dot(self.first[0], high) + dot(self.first[0], low) + dot(self.first[1], high)
        out = []
        for i in range(len(blocks)):
            cols = slice(128 * i, 128 * i + 128)
            out.append(both[:32, cols] + direction * self.sign * swap(both[32:, cols]))
        return out

    def over_t(self, value, tables):
        high, low = halves(value)
        return dot(high, tables[0]) + dot(low, tables[0]) + dot(high, tables[1])

    def forward(self, ref, offset):
        blocks = [ref[:, offset + i, :] for i in range(8)]
        lane = lanes((32, 128))
        nyquist = (lane >= 64) & (lane < 96)
        blocks.append(jnp.where(lane < 32, swap(blocks[0]), 0.0) * self.is_first)
        blocks[0] = jnp.where(nyquist, blocks[0] * (1.0 - self.is_first), blocks[0])
        blocks = self.over_s(blocks, 1.0)
        blocks = [z * self.cos + swap(z) * self.sin for z in blocks]
        return self.over_t(jnp.concatenate(blocks, 0), self.second)

    def inverse(self, spectrum):
        all_rows = self.over_t(spectrum, self.back)
        blocks = [all_rows[32 * i : 32 * i + 32] for i in range(BLOCKS)]
        blocks = [z * self.cos - swap(z) * self.sin for z in blocks]
        blocks = self.over_s(blocks, -1.0)
        lane = lanes((32, 128))
        nyquist = (lane >= 64) & (lane < 96)
        own = jnp.where(lane // 32 % 2 == 0, SCALE * (1.0 - 0.5 * self.is_first), SCALE)
        blocks[0] = (blocks[0] + jnp.where(nyquist, swap(blocks[8]), 0.0)) * own
        return [blocks[0]] + [z * SCALE for z in blocks[1:8]]

    def weighted_sum(self, value):
        lane, row = lanes(value.shape), sublanes(value.shape)
        weight = jnp.where((row < 32) & (lane // 32 % 2 == 0), 2.0 - self.is_first, 2.0)
        weight = jnp.where(row >= 256, 1.0, weight)
        return jnp.sum(value * weight) * (1.0 / (COLS * 1024.0))


def halo_rows(block):
    lane, row = lanes((32, 128)) % 32, sublanes((32, 128))
    after = jnp.where((lane < 8) & (row < 31), pltpu.roll(block, 31, 0), 0.0)
    before = jnp.where((lane >= 24) & (row > 0), pltpu.roll(block, 1, 0), 0.0)
    return after, before


def product(real, imaginary, value):
    return real * value + imaginary * swap(value)


def spread_kernel(table_ref, measured, point_spread, out_ref):
    for f, ref in enumerate((measured, point_spread)):
        out_ref[:, 8 * f : 8 * f + 8, :] = x_forward(ref[...], table_ref).reshape(32, 8, 128)


def first_filter_kernel(is_first_ref, table, arrived, out_ref, bank_ref):
    lateral = Lateral(table, is_first_ref[0])
    transfer = lateral.forward(arrived, 8)
    observed = lateral.forward(arrived, 0)
    turned = swap(transfer)
    left = lanes(transfer.shape) < 64
    real = jnp.where(left, transfer, turned)
    imaginary = jnp.where(left, turned, -transfer)
    power = real * real + imaginary * imaginary
    spectrum = product(real, imaginary, observed)
    right = lateral.inverse(spectrum)
    image = lateral.inverse(spectrum * power)
    for i in range(8):
        out_ref[:, i, :] = right[i]
        out_ref[:, 8 + i, :] = image[i]
        after, before = halo_rows(right[i])
        image_after, image_before = halo_rows(image[i])
        image_after, image_before = pltpu.roll(image_after, 8, 1), pltpu.roll(image_before, 120, 1)
        out_ref[:, 16 + i, :] = after + before + image_after + image_before
    for k, value in enumerate((real, imaginary, power, spectrum)):
        bank_ref[k] = value


def second_filter_kernel(is_first_ref, table, arrived, bank_ref, row_b, row_ab, out_ref, image_ref):
    lateral = Lateral(table, is_first_ref[0])
    power = bank_ref[2]
    image = power * bank_ref[3] + lateral.forward(arrived, 0)
    filtered = power * image
    blocks = lateral.inverse(filtered)
    for i in range(8):
        out_ref[:, i, :] = blocks[i]
        after, before = halo_rows(blocks[i])
        out_ref[:, 8 + i, :] = after + before
    image_ref[...] = image
    row = row_b[...] + row_ab[...]
    row = row + jnp.where(lanes((1, 128)) == 3, lateral.weighted_sum(image * filtered), 0.0)
    out_ref[:, 8, :] = out_ref[:, 8, :] + pltpu.roll(jnp.broadcast_to(row, (32, 128)), 8, 1)


def last_filter_kernel(
    is_first_ref, factor_ref, table, arrived, bank_ref, image_ref, terms, out_ref
):
    lateral = Lateral(table, is_first_ref[0])
    power = bank_ref[2]
    image = image_ref[...]
    total = factor_ref[4] * image + factor_ref[5] * (power * image) + lateral.forward(arrived, 8)
    total = power * total + factor_ref[2] * bank_ref[3] + factor_ref[3] * image
    total = total + lateral.forward(arrived, 0)
    blocks = lateral.inverse(product(bank_ref[0], -bank_ref[1], total))
    for i in range(8):
        out_ref[:, i, :] = blocks[i]
        out_ref[:, 8 + i, :] = jnp.broadcast_to(terms[...], (32, 128))


def gather_two_kernel(table_ref, arrived, right_ref, image_ref):
    tiles = [arrived[:, 8 * f : 8 * f + 8, :].reshape(256, 128) for f in range(3)]
    value = x_inverse(tiles, table_ref)
    right_ref[0:8, :] = value[88:96]
    right_ref[8:40, :] = value[0:32]
    right_ref[40:48, :] = value[64:72]
    image_ref[0:8, :] = value[80:88]
    image_ref[8:40, :] = value[32:64]
    image_ref[40:48, :] = value[72:80]


def gather_sum_kernel(table_ref, arrived, base, out_ref, row_ref):
    row = pltpu.roll(jnp.broadcast_to(jnp.sum(arrived[:, 8, :], 0, keepdims=True), (8, 128)), 120, 1)
    row_ref[...] = jnp.where(lanes((1, 128)) < 6, row[0:1], 0.0)
    tiles = [arrived[:, 8 * f : 8 * f + 8, :].reshape(256, 128) for f in range(2)]
    value = x_inverse(tiles, table_ref)
    out_ref[0:8, :] = base[0:8, :] + value[56:64]
    out_ref[8:40, :] = base[8:40, :] + value[0:32]
    out_ref[40:48, :] = base[40:48, :] + value[32:40]


def final_kernel(table_ref, arrived, out_ref, row_ref):
    out_ref[...] = x_inverse([arrived[:, 0:8, :].reshape(256, 128)], table_ref)
    row_ref[...] = jnp.sum(arrived[:, 8, :], 0, keepdims=True)


def shifted_columns(value):
    column = lanes(value.shape)
    left = jnp.where(column >= 1, pltpu.roll(value, 1, 1), 0.0)
    right = jnp.where(column < COLS - 1, pltpu.roll(value, COLS - 1, 1), 0.0)
    return left, right


def stencil_sum(weight, source, start, cols):
    total = None
    for b in range(3):
        part = None
        for a in range(3):
            for c in range(3):
                term = weight(a, b, c) * source[c, start + a, :, cols]
                part = term if part is None else part + term
        if b == 0:
            part = pltpu.roll(part, 1, 0)
        elif b == 2:
            part = pltpu.roll(part, FRAME - 1, 0)
        total = part if total is None else total + part
    return total


def load_planes(parts, source, sems):
    copies = [pltpu.make_async_copy(ref, source.at[1, p], sems.at[p]) for p, ref in enumerate(parts)]
    for copy in copies:
        copy.start()
    for copy in copies:
        copy.wait()
    for p in range(len(parts)):
        source[0, p], source[2, p] = shifted_columns(source[1, p])


def row_bounds(place_ref):
    device, plane, planes = place_ref[0], place_ref[1], place_ref[2]
    lowest = jnp.where(device > 0, 0, 8)
    highest = jnp.where(device < 31, FRAME, 40)

    def highest_at(here):
        return jnp.where((here >= 0) & (here < planes), highest, 0)

    return sublanes((FRAME, 128)), lowest, highest, lambda p: highest_at(plane + p)


def weight_of(weights_ref):
    return lambda a, b, c: weights_ref[9 * a + 3 * b + c]


def flipped_of(weights_ref):
    return lambda a, b, c: weights_ref[26 - 9 * a - 3 * b - c]


def apply_stencils(place_ref, weights_ref, source, middle, back_ref):
    row, lowest, highest, highest_at = row_bounds(place_ref)
    for p in range(3):
        valid = (row >= lowest) & (row < highest_at(p - 1))
        for k in range(8):
            cols = slice(128 * k, 128 * k + 128)
            value = stencil_sum(weight_of(weights_ref), source, p, cols)
            middle[1, p, :, cols] = jnp.where(valid, value, 0.0)
    for p in range(3):
        middle[0, p], middle[2, p] = shifted_columns(middle[1, p])
    inside = (row >= lowest) & (row < highest)
    for k in range(8):
        cols = slice(128 * k, 128 * k + 128)
        back_ref[:, cols] = jnp.where(inside, stencil_sum(flipped_of(weights_ref), middle, 0, cols), 0.0)


def row_of(values):
    lane = lanes((1, 128))
    out = jnp.zeros((1, 128), F32)
    for k, value in values:
        out = jnp.where(lane == k, jnp.sum(value), out)
    return out


def image_kernel(place, weights, table, blurred, upstream, u2, u1, o, d1, d2, image_ref, mapped_ref, out_ref, row_ref, *scratch):
    source, middle, sems, back = scratch
    load_planes((u2, u1, o, d1, d2), source, sems)
    apply_stencils(place, weights, source, middle, back)
    out_ref[...] = x_forward(back[8:40, :], table).reshape(32, 8, 128)
    mapped_ref[...] = middle[1, 1, 8:40, :]
    image_ref[...] = blurred[...] + back[...]
    b, ab, u = source[1, 2, 8:40, :], image_ref[8:40, :], upstream[...]
    row_ref[...] = row_of(((0, b * b), (1, b * ab), (2, ab * ab), (4, u * b), (5, u * ab)))


def loss_kernel(place, weights, u2, u1, o, d1, d2, back_ref, mapped_ref, source, middle, sems):
    load_planes((u2, u1, o, d1, d2), source, sems)
    apply_stencils(place, weights, source, middle, back_ref)
    mapped_ref[...] = middle[1, 1, 8:40, :]


def map_kernel(weights, u1, o, d1, mapped_ref, row_ref, source, whole, sems):
    load_planes((u1, o, d1), source, sems)
    for k in range(8):
        cols = slice(128 * k, 128 * k + 128)
        whole[:, cols] = stencil_sum(weight_of(weights), source, 0, cols)
    mapped = whole[8:40, :]
    mapped_ref[...] = mapped
    row_ref[...] = row_of(((3, mapped * mapped),))


def further_kernel(place, weights, u2, u1, o, d1, d2, back_ref, source, middle, sems):
    load_planes((u2, u1, o, d1, d2), source, sems)
    apply_stencils(place, weights, source, middle, back_ref)


def last_kernel(
    place, weights, factor, table, image_back, loss_back, upstream, u2, u1, o, d1, d2, mapped_ref, out_ref, source, middle, sems, back
):
    load_planes((u2, u1, o, d1, d2), source, sems)
    apply_stencils(place, weights, source, middle, back)
    mapped_ref[...] = middle[1, 1, 8:40, :]
    u, again = upstream[...], image_back[8:40, :]
    first = factor[0] * u + factor[1] * loss_back[8:40, :] + factor[4] * again + factor[5] * back[8:40, :]
    second = factor[1] * u + factor[5] * again
    out_ref[:, 0:8, :] = x_forward(first, table).reshape(32, 8, 128)
    out_ref[:, 8:16, :] = x_forward(second, table).reshape(32, 8, 128)


def correlate_kernel(factor_ref, *refs):
    out_ref, scaled, mapped = refs[-3:]
    right, image, further, upstream = refs[0:3], refs[3:6], refs[6:9], refs[9:12]
    right_map, image_map, further_map, upstream_map = refs[12:16]
    f = [factor_ref[k] for k in range(5)]
    for p in range(3):
        scaled[p] = f[0] * upstream[p][...] + f[1] * right[p][...] + f[2] * image[p][...] + f[3] * further[p][...]
    mapped[0] = (
        f[0] * upstream_map[...] + f[1] * right_map[...] + f[2] * image_map[...] + f[3] * further_map[...]
    )
    mapped[1] = right_map[...]
    mapped[2] = f[4] * image_map[...]
    lane = lanes((1, 128))
    out = jnp.zeros((1, 128), F32)
    column = lanes((ROWS, COLS))
    left_edge, right_edge = column < COLS - 1, column >= 1
    for c in range(3):
        parts = []
        for k in range(3):
            value = mapped[k]
            if c == 0:
                value = jnp.where(left_edge, pltpu.roll(value, COLS - 1, 1), 0.0)
            elif c == 2:
                value = jnp.where(right_edge, pltpu.roll(value, 1, 1), 0.0)
            parts.append(value)
        for a in range(3):
            for b in range(3):
                rows = slice(7 + b, 39 + b)
                total = parts[0] * right[a][rows, :] + parts[1] * scaled[a, rows, :] + parts[2] * image[a][rows, :]
                out = jnp.where(lane == 9 * a + 3 * b + c, jnp.sum(total), out)
    out_ref[...] = out


def shape(*dims):
    return jax.ShapeDtypeStruct(dims, F32)


STENCIL_SCRATCH = (
    pltpu.VMEM((3, 5, FRAME, COLS), F32),
    pltpu.VMEM((3, 3, FRAME, COLS), F32),
    pltpu.SemaphoreType.DMA((5,)),
)
BACK_SCRATCH = (pltpu.VMEM((FRAME, COLS), F32),)


def call(body, out_shape, scalars, operands, scratch=(), far=(), far_out=(), planes=(), flops=400_000_000):
    smem, vmem, hbm = (pl.BlockSpec(memory_space=m) for m in (pltpu.SMEM, pltpu.VMEM, pltpu.HBM))
    outs = out_shape if isinstance(out_shape, tuple) else (out_shape,)
    first, count = len(scalars), len(scalars) + len(operands) + len(planes)
    buffers = [pltpu.VMEM(operands[i].shape, operands[i].dtype) for i in far]
    buffers += [pltpu.VMEM(outs[i].shape, outs[i].dtype) for i in far_out]
    extra = [*buffers, pltpu.SemaphoreType.DMA((len(buffers),))] if buffers else []

    def whole(*refs):
        ins, results = list(refs[:count]), list(refs[count : count + len(outs)])
        own = refs[count + len(outs) :]
        held, sems, own = own[: len(buffers)], own[len(buffers)] if buffers else None, own[len(extra) :]
        copies = []
        for k, i in enumerate(far):
            copies.append(pltpu.make_async_copy(ins[first + i], held[k], sems.at[k]))
            ins[first + i] = held[k]
        for copy in copies:
            copy.start()
        for copy in copies:
            copy.wait()
        copies = []
        for k, i in enumerate(far_out, len(far)):
            copies.append(pltpu.make_async_copy(held[k], results[i], sems.at[k]))
            results[i] = held[k]
        body(*ins, *results, *own)
        for copy in copies:
            copy.start()
        for copy in copies:
            copy.wait()

    spec_in = [smem] * len(scalars) + [hbm if i in far else vmem for i in range(len(operands))] + [hbm] * len(planes)
    spec_out = tuple(hbm if i in far_out else vmem for i in range(len(outs)))
    return pl.pallas_call(
        whole,
        out_shape=out_shape,
        in_specs=spec_in,
        out_specs=spec_out if isinstance(out_shape, tuple) else spec_out[0],
        scratch_shapes=[*extra, *scratch],
        compiler_params=pltpu.CompilerParams(vmem_limit_bytes=VMEM),
        cost_estimate=pl.CostEstimate(flops=flops, bytes_accessed=4_000_000, transcendentals=0),
    )(*scalars, *operands, *planes)


def exchange(value):
    return lax.all_to_all(value, GY, 0, 0, tiled=True)


def moved(value, by):
    size = lax.axis_size(GZ)
    return lax.ppermute(value, GZ, [(i, i + by) for i in range(size) if 0 <= i + by < size])


def neighbours(value):
    return moved(value, 2), moved(value, 1), value, moved(value, -1), moved(value, -2)


def with_rows(value):
    size = lax.axis_size(GY)
    below = lax.ppermute(value[24:32], GY, [(i, i + 1) for i in range(size - 1)])
    above = lax.ppermute(value[0:8], GY, [(i + 1, i) for i in range(size - 1)])
    return jnp.concatenate([below, value, above], 0)


def from_all(row):
    size = lax.axis_size(GZ)
    return lax.all_to_all(jnp.broadcast_to(row[None], (size, 8, 128)), GZ, 0, 0, tiled=True)


def over_planes(row):
    size = lax.axis_size(GZ)
    bit = 1
    while bit < size:
        row = row + lax.ppermute(row, GZ, [(i, i ^ bit) for i in range(size)])
        bit *= 2
    return row


def factors(m0, m1, m2, m3, u0, u1):
    def pair(m0, m1, m2, m3):
        step0 = m0 / m1
        norm1 = m0 - 2.0 * step0 * m1 + step0 * step0 * m2
        ratio = norm1 / m0
        keep = 1.0 + ratio
        curvature = keep * keep * m1 - 2.0 * keep * step0 * m2 + step0 * step0 * m3
        step1 = norm1 / curvature
        return step0 + step1 * keep, -step1 * step0

    (alpha, gamma), back = jax.vjp(pair, m0, m1, m2, m3)
    return (alpha, gamma, *back((u0, u1)))


def factors_kernel(rows, filter_ref, stencil_ref):
    total = jnp.sum(rows[:, 0, :], 0, keepdims=True)
    lane = lanes((1, 128))
    moments = [jnp.sum(jnp.where(lane == k, total, 0.0), axis=1, keepdims=True) for k in range(6)]
    alpha, gamma, g0, g1, g2, g3 = factors(*moments)
    for k, value in enumerate((alpha, gamma, 2.0 * g0, 2.0 * g1, 2.0 * g2, 2.0 * g3)):
        filter_ref[k] = value[0, 0]
    for k, value in enumerate((gamma, g1, 2.0 * g2, 2.0 * g3, 2.0 * g3)):
        stencil_ref[k] = value[0, 0]


def local(measured, point_spread, stencil_weights, upstream):
    cells = measured.size * lax.axis_size(GY) * lax.axis_size(GZ)
    device, plane = lax.axis_index(GY), lax.axis_index(GZ)
    is_first = jnp.where(device == 0, 1.0, 0.0).astype(F32).reshape(1)
    place = jnp.stack([device, plane, jnp.int32(lax.axis_size(GZ))]).astype(jnp.int32)
    weights = stencil_weights.reshape(27)
    table, along_y = jnp.asarray(X_TABLE), jnp.asarray(Y_TABLE)
    measured, upstream = measured[0], upstream[0]
    tile, tiles, three = shape(32, 8, 128), shape(32, 16, 128), shape(32, 24, 128)
    spectral, frame, rows, row = shape(32 * BLOCKS, 128), shape(FRAME, COLS), shape(ROWS, COLS), shape(1, 128)

    first = exchange(call(spread_kernel, tiles, [], [table, measured, point_spread], far=(1, 2), far_out=(0,)))
    first, grown = lax.optimization_barrier((first, with_rows(upstream)))

    right_out, bank = call(
        first_filter_kernel, (three, shape(4, 32 * BLOCKS, 128)), [is_first], [along_y, first], far_out=(0, 1)
    )
    right_arrived = exchange(right_out)
    loss_parts = neighbours(grown)
    loss_back, loss_map = call(
        loss_kernel, (frame, rows), [place, weights], [], STENCIL_SCRATCH, far_out=(0, 1), planes=loss_parts
    )
    right_arrived, loss_back = lax.optimization_barrier((right_arrived, loss_back))
    right, blurred = call(gather_two_kernel, (frame, frame), [], [table, right_arrived], far_out=(0, 1))

    right_parts = neighbours(right)
    image, right_map, image_send, row_b = call(
        image_kernel,
        (frame, rows, tile, row),
        [place, weights],
        [table, blurred, upstream],
        STENCIL_SCRATCH + BACK_SCRATCH,
        far=(1, 2),
        far_out=(0, 1, 2, 3),
        planes=right_parts,
    )
    image_arrived = exchange(image_send)
    image_near = (moved(image, 1), image, moved(image, -1))
    map_scratch = (pltpu.VMEM((3, 3, FRAME, COLS), F32), pltpu.VMEM((FRAME, COLS), F32), pltpu.SemaphoreType.DMA((3,)))
    image_map, row_ab = call(map_kernel, (rows, row), [weights], [], map_scratch, far_out=(0, 1), planes=image_near)
    further_out, image_spectrum = call(
        second_filter_kernel,
        (tiles, spectral),
        [is_first],
        [along_y, image_arrived, bank, row_b, row_ab],
        far=(2, 3, 4),
        far_out=(0, 1),
    )
    further_out, image_again = lax.optimization_barrier((further_out, image))
    further_arrived = exchange(further_out)
    image_parts = (moved(image_again, 2), *image_near, moved(image_again, -2))
    image_back = call(further_kernel, frame, [place, weights], [], STENCIL_SCRATCH, far_out=(0,), planes=image_parts)
    further_arrived, image_back = lax.optimization_barrier((further_arrived, image_back))

    further, row_sum = call(
        gather_sum_kernel, (frame, row), [], [table, further_arrived, image_back], far=(2,), far_out=(0,)
    )
    smem = pl.BlockSpec(memory_space=pltpu.SMEM)
    filter_factors, stencil_factors = pl.pallas_call(
        factors_kernel,
        out_shape=(shape(6), shape(5)),
        in_specs=[pl.BlockSpec(memory_space=pltpu.VMEM)],
        out_specs=(smem, smem),
    )(from_all(row_sum))

    further_parts = neighbours(further)
    further_map, last_send = call(
        last_kernel,
        (rows, tiles),
        [place, weights, filter_factors],
        [table, image_back, loss_back, upstream],
        STENCIL_SCRATCH + BACK_SCRATCH,
        far=(1, 2, 3),
        far_out=(0, 1),
        planes=further_parts,
    )
    last_arrived = exchange(last_send)

    operands = []
    for parts in (right_parts, image_parts, further_parts, loss_parts):
        operands += parts[1:4]
    operands += [right_map, image_map, further_map, loss_map]
    scratch = (pltpu.VMEM((3, FRAME, COLS), F32), pltpu.VMEM((3, ROWS, COLS), F32))
    terms = call(correlate_kernel, row, [stencil_factors], operands, scratch, far=tuple(range(16)), far_out=(0,))
    terms = over_planes(terms)
    result_out = call(
        last_filter_kernel,
        tiles,
        [is_first, filter_factors],
        [along_y, last_arrived, bank, image_spectrum, terms],
        far=(2, 3, 4),
        far_out=(0,),
    )
    grad_measured, terms = call(final_kernel, (rows, row), [], [table, exchange(result_out)])
    grad_stencil = terms[0, :27].reshape(3, 3, 3) / math.sqrt(cells)
    return grad_measured[None], grad_stencil


def solution(mesh):
    return jax.shard_map(
        local,
        mesh=mesh,
        in_specs=(P(GZ, GY, None), P(GY, None), P(), P(GZ, GY, None)),
        out_specs=(P(GZ, GY, None), P()),
        check_vma=False,
    )
```

```python
import functools
import math

import jax
import jax.numpy as jnp
import ml_dtypes
import numpy as np
from jax import lax
from jax.experimental import pallas as pl
from jax.experimental.pallas import tpu as pltpu
from jax.sharding import PartitionSpec as P

GY = "gy"
GZ = "gz"
ROWS = 32
COLS = 1024
FRAME = 48
BLOCKS = 9
F32 = jnp.float32
BF16 = jnp.bfloat16
VMEM = 14 * 1024 * 1024


def split_table(table):
    high = table.astype(ml_dtypes.bfloat16)
    low = (table - high.astype(np.float64)).astype(ml_dtypes.bfloat16)
    return high, low


def x_table():
    part, half, device, i = np.meshgrid(
        np.arange(2), np.arange(2), np.arange(32), np.arange(8), indexing="ij"
    )
    kx = 2 * (16 * (device % 16) + 8 * half + i) + device // 16
    part, kx = part.reshape(-1, 1), kx.reshape(-1, 1)
    x = np.arange(COLS // 2)[None, :]
    angle = 2.0 * np.pi * ((kx * x) % COLS) / COLS
    flip = 1.0 - 2.0 * (x % 2)
    wave = np.where(part == 0, np.cos(angle), -np.sin(angle))
    return np.where((kx == 0) & (part == 1), flip, wave)


def y_tables():
    q = np.arange(32)[:, None]
    s = np.arange(32)[None, :]
    angle = 2.0 * np.pi * ((q * s) % 32) / 32
    first = np.concatenate([np.cos(angle), np.sin(angle)], 0)
    lane = np.arange(128)
    part, half, t = lane // 64, lane // 32 % 2, lane % 32
    turn = 2.0 * np.pi * q * t[None, :] / 1024
    sign = np.where(part == 0, 1.0, -1.0)[None, :]
    turn_cos, turn_sin = np.cos(turn), np.sin(turn) * sign
    angle = 2.0 * np.pi * ((t[:, None] * t[None, :]) % 32) / 32
    pi, po = part[:, None], part[None, :]
    block = np.where(pi == po, np.cos(angle), np.where(pi > po, np.sin(angle), -np.sin(angle)))
    second = np.where(half[:, None] == half[None, :], block, 0.0)
    return first, turn_cos, turn_sin, second


def packed_tables():
    first, turn_cos, turn_sin, second = y_tables()
    first = np.pad(first, ((0, 0), (0, 96)))
    tables = [*split_table(second), *split_table(second.T), *split_table(first)]
    return np.concatenate([*tables, turn_cos, turn_sin], 0).astype(np.float32)


X_TABLE = np.concatenate(split_table(x_table()), 0)
Y_TABLE = packed_tables()
SCALE = 2.0 / (COLS * 1024.0)


def halves(value):
    high = value.astype(BF16)
    return high, (value - high.astype(F32)).astype(BF16)


def dot(left, right):
    return lax.dot_general(left, right, (((1,), (0,)), ((), ())), preferred_element_type=F32)


def dot_nt(left, right):
    return lax.dot_general(left, right, (((1,), (1,)), ((), ())), preferred_element_type=F32)


def swap(value):
    return pltpu.roll(value, 64, 1)


def lanes(shape):
    return lax.broadcasted_iota(jnp.int32, shape, 1)


def sublanes(shape):
    return lax.broadcasted_iota(jnp.int32, shape, 0)


def x_forward(value, table_ref):
    left, right = value[:, : COLS // 2], value[:, COLS // 2 :]
    group = lanes((128, 128)) // 32
    outs = []
    for parity, folded in enumerate((left + right, left - right)):
        high, low = halves(folded)
        both = jnp.concatenate([high] * 4 + [low] * 4, 0)
        out = None
        for h in range(4):
            start = 256 * h + 128 * parity
            first = dot_nt(table_ref[start : start + 128, :], both)
            piece = first[:, :128] + first[:, 128:]
            piece = piece + dot_nt(table_ref[1024 + start : 1152 + start, :], both[:128])
            out = piece if out is None else jnp.where(group == h, piece, out)
        outs.append(out)
    return jnp.concatenate(outs, 0)


def x_inverse(spectra, table_ref):
    turned = [value.T for value in spectra]
    sums = []
    for parity in range(2):
        cols = slice(128 * parity, 128 * parity + 128)
        rows = [jnp.concatenate([v[32 * h : 32 * h + 32, cols] for h in range(4)], 1) for v in turned]
        left = rows[0] if len(rows) == 1 else jnp.concatenate(rows, 0)
        count = left.shape[0]
        high, low = halves(left)
        both = jnp.concatenate([high, low], 0)
        total = None
        for h in range(4):
            start = 256 * h + 128 * parity
            k = slice(128 * h, 128 * h + 128)
            first = dot(both[:, k], table_ref[start : start + 128, :])
            piece = first[:count] + first[count:] + dot(high[:, k], table_ref[1024 + start : 1152 + start, :])
            total = piece if total is None else total + piece
        sums.append(total)
    return jnp.concatenate([sums[0] + sums[1], sums[0] - sums[1]], 1)


class Lateral:
    def __init__(self, table):
        def piece(start, count, width):
            return table[start : start + count, 0:width].astype(BF16)

        self.second = (piece(0, 128, 128), piece(128, 128, 128))
        self.back = (piece(256, 128, 128), piece(384, 128, 128))
        self.first = (piece(512, 64, 32), piece(576, 64, 32))
        self.cos, self.sin = table[640:672, :], table[672:704, :]
        self.is_first = jnp.where(lax.axis_index(GY) == 0, 1.0, 0.0).astype(F32)
        self.sign = jnp.where(lanes((32, 128)) < 64, 1.0, -1.0)

    def over_s(self, blocks, direction):
        high, low = halves(jnp.concatenate(blocks, 1))
        both = dot(self.first[0], high) + dot(self.first[0], low) + dot(self.first[1], high)
        out = []
        for i in range(len(blocks)):
            cols = slice(128 * i, 128 * i + 128)
            out.append(both[:32, cols] + direction * self.sign * swap(both[32:, cols]))
        return out

    def over_t(self, value, tables):
        high, low = halves(value)
        return dot(high, tables[0]) + dot(low, tables[0]) + dot(high, tables[1])

    def forward(self, ref, offset):
        blocks = [ref[:, offset + i, :] for i in range(8)]
        lane = lanes((32, 128))
        nyquist = (lane >= 64) & (lane < 96)
        blocks.append(jnp.where(lane < 32, swap(blocks[0]), 0.0) * self.is_first)
        blocks[0] = jnp.where(nyquist, blocks[0] * (1.0 - self.is_first), blocks[0])
        blocks = self.over_s(blocks, 1.0)
        blocks = [z * self.cos + swap(z) * self.sin for z in blocks]
        return self.over_t(jnp.concatenate(blocks, 0), self.second)

    def inverse(self, spectrum):
        all_rows = self.over_t(spectrum, self.back)
        blocks = [all_rows[32 * i : 32 * i + 32] for i in range(BLOCKS)]
        blocks = [z * self.cos - swap(z) * self.sin for z in blocks]
        blocks = self.over_s(blocks, -1.0)
        lane = lanes((32, 128))
        nyquist = (lane >= 64) & (lane < 96)
        own = jnp.where(lane // 32 % 2 == 0, SCALE * (1.0 - 0.5 * self.is_first), SCALE)
        blocks[0] = (blocks[0] + jnp.where(nyquist, swap(blocks[8]), 0.0)) * own
        return [blocks[0]] + [z * SCALE for z in blocks[1:8]]

    def weighted_sum(self, value):
        lane, row = lanes(value.shape), sublanes(value.shape)
        weight = jnp.where((row < 32) & (lane // 32 % 2 == 0), 2.0 - self.is_first, 2.0)
        weight = jnp.where(row >= 256, 1.0, weight)
        return jnp.sum(value * weight) * (1.0 / (COLS * 1024.0))


def halo_rows(block):
    lane, row = lanes((32, 128)) % 32, sublanes((32, 128))
    after = jnp.where((lane < 8) & (row < 31), pltpu.roll(block, 31, 0), 0.0)
    before = jnp.where((lane >= 24) & (row > 0), pltpu.roll(block, 1, 0), 0.0)
    return after, before


def product(real, imaginary, value):
    return real * value + imaginary * swap(value)


def conjugate_factors(transfer):
    turned, left = swap(transfer), lanes(transfer.shape) < 64
    return jnp.where(left, transfer, turned), jnp.where(left, turned, -transfer)


def spread_kernel(table_ref, measured, point_spread, out_ref):
    for f, ref in enumerate((measured, point_spread)):
        out_ref[:, 8 * f : 8 * f + 8, :] = x_forward(ref[...], table_ref).reshape(32, 8, 128)


def first_filter_kernel(table, arrived, out_ref, bank_ref):
    lateral = Lateral(table)
    transfer = lateral.forward(arrived, 8)
    observed = lateral.forward(arrived, 0)
    real, imaginary = conjugate_factors(transfer)
    power = real * real + imaginary * imaginary
    spectrum = product(real, imaginary, observed)
    right = lateral.inverse(spectrum)
    image = lateral.inverse(spectrum * power)
    for i in range(8):
        out_ref[:, i, :] = right[i]
        out_ref[:, 8 + i, :] = image[i]
        after, before = halo_rows(right[i])
        image_after, image_before = halo_rows(image[i])
        image_after, image_before = pltpu.roll(image_after, 8, 1), pltpu.roll(image_before, 120, 1)
        out_ref[:, 16 + i, :] = after + before + image_after + image_before
    bank_ref[0] = transfer
    bank_ref[1] = spectrum


def second_filter_kernel(table, arrived, bank_ref, sums, out_ref, image_ref):
    lateral = Lateral(table)
    real, imaginary = conjugate_factors(bank_ref[0])
    power = real * real + imaginary * imaginary
    image = power * bank_ref[1] + lateral.forward(arrived, 0)
    filtered = power * image
    blocks = lateral.inverse(filtered)
    for i in range(8):
        out_ref[:, i, :] = blocks[i]
        after, before = halo_rows(blocks[i])
        out_ref[:, 8 + i, :] = after + before
    image_ref[...] = image
    row = sums[...] + jnp.where(lanes((1, 128)) == 3, lateral.weighted_sum(image * filtered), 0.0)
    out_ref[:, 8, :] = out_ref[:, 8, :] + pltpu.roll(jnp.broadcast_to(row, (32, 128)), 8, 1)


def last_filter_kernel(
    factors_ref, table, arrived, bank_ref, image_ref, terms, out_ref
):
    lateral = Lateral(table)
    factor_ref = [factors_ref[27 + k] for k in range(6)]
    real, imaginary = conjugate_factors(bank_ref[0])
    power = real * real + imaginary * imaginary
    image = image_ref[...]
    total = factor_ref[4] * image + factor_ref[5] * (power * image) + lateral.forward(arrived, 8)
    total = power * total + factor_ref[2] * bank_ref[1] + factor_ref[3] * image
    total = total + lateral.forward(arrived, 0)
    blocks = lateral.inverse(product(real, -imaginary, total))
    for i in range(8):
        out_ref[:, i, :] = blocks[i]
        out_ref[:, 8 + i, :] = jnp.broadcast_to(terms[...], (32, 128))


def gather_two_kernel(table_ref, arrived, right_ref, image_ref):
    tiles = [arrived[:, 8 * f : 8 * f + 8, :].reshape(256, 128) for f in range(3)]
    value = x_inverse(tiles, table_ref)
    right_ref[0:8, :] = value[88:96]
    right_ref[8:40, :] = value[0:32]
    right_ref[40:48, :] = value[64:72]
    image_ref[0:8, :] = value[80:88]
    image_ref[8:40, :] = value[32:64]
    image_ref[40:48, :] = value[72:80]


def gather_sum_kernel(table_ref, arrived, base, out_ref, row_ref):
    row = pltpu.roll(jnp.broadcast_to(jnp.sum(arrived[:, 8, :], 0, keepdims=True), (8, 128)), 120, 1)
    row_ref[...] = jnp.where(lanes((1, 128)) < 6, row[0:1], 0.0)
    tiles = [arrived[:, 8 * f : 8 * f + 8, :].reshape(256, 128) for f in range(2)]
    value = x_inverse(tiles, table_ref)
    out_ref[0:8, :] = base[0:8, :] + value[56:64]
    out_ref[8:40, :] = base[8:40, :] + value[0:32]
    out_ref[40:48, :] = base[40:48, :] + value[32:40]


def final_kernel(table_ref, arrived, out_ref, row_ref):
    out_ref[...] = x_inverse([arrived[:, 0:8, :].reshape(256, 128)], table_ref)
    row_ref[...] = jnp.sum(arrived[:, 8, :], 0, keepdims=True)


def shifted_columns(value):
    column = lanes(value.shape)
    left = jnp.where(column >= 1, pltpu.roll(value, 1, 1), 0.0)
    right = jnp.where(column < COLS - 1, pltpu.roll(value, COLS - 1, 1), 0.0)
    return left, right


def stencil_sum(weight, source, start, cols):
    total = None
    for b in range(3):
        part = None
        for a in range(3):
            for c in range(3):
                term = weight(a, b, c) * source[c, start + a, :, cols]
                part = term if part is None else part + term
        if b == 0:
            part = pltpu.roll(part, 1, 0)
        elif b == 2:
            part = pltpu.roll(part, FRAME - 1, 0)
        total = part if total is None else total + part
    return total


def load_planes(parts, source):
    for p, ref in enumerate(parts):
        value = ref[...]
        source[1, p] = value
        source[0, p], source[2, p] = shifted_columns(value)


def row_bounds():
    device, plane, planes = lax.axis_index(GY), lax.axis_index(GZ), lax.axis_size(GZ)
    lowest = jnp.where(device > 0, 0, 8)
    highest = jnp.where(device < 31, FRAME, 40)

    def highest_at(here):
        return jnp.where((here >= 0) & (here < planes), highest, 0)

    return sublanes((FRAME, 128)), lowest, highest, lambda p: highest_at(plane + p)


def weight_of(weights_ref):
    return lambda a, b, c: weights_ref[9 * a + 3 * b + c]


def flipped_of(weights_ref):
    return lambda a, b, c: weights_ref[26 - 9 * a - 3 * b - c]


def apply_stencils(weights_ref, source, middle, back_ref):
    row, lowest, highest, highest_at = row_bounds()
    for p in range(3):
        valid = (row >= lowest) & (row < highest_at(p - 1))
        for k in range(8):
            cols = slice(128 * k, 128 * k + 128)
            value = stencil_sum(weight_of(weights_ref), source, p, cols)
            middle[1, p, :, cols] = jnp.where(valid, value, 0.0)
    for p in range(3):
        middle[0, p], middle[2, p] = shifted_columns(middle[1, p])
    inside = (row >= lowest) & (row < highest)
    for k in range(8):
        cols = slice(128 * k, 128 * k + 128)
        back_ref[:, cols] = jnp.where(inside, stencil_sum(flipped_of(weights_ref), middle, 0, cols), 0.0)


def row_of(values):
    lane = lanes((1, 128))
    out = jnp.zeros((1, 128), F32)
    for k, value in values:
        out = jnp.where(lane == k, jnp.sum(value), out)
    return out


def image_kernel(weights, table, blurred, upstream, u2, u1, o, d1, d2, image_ref, mapped_ref, out_ref, row_ref, *scratch):
    source, middle, back = scratch
    load_planes((u2, u1, o, d1, d2), source)
    apply_stencils(weights, source, middle, back)
    out_ref[...] = x_forward(back[8:40, :], table).reshape(32, 8, 128)
    mapped_ref[...] = middle[1, 1, 8:40, :]
    image_ref[...] = blurred[...] + back[...]
    b, ab, u = source[1, 2, 8:40, :], image_ref[8:40, :], upstream[...]
    row_ref[...] = row_of(((0, b * b), (1, b * ab), (2, ab * ab), (4, u * b), (5, u * ab)))


def loss_kernel(weights, u2, u1, o, d1, d2, back_ref, mapped_ref, source, middle):
    load_planes((u2, u1, o, d1, d2), source)
    apply_stencils(weights, source, middle, back_ref)
    mapped_ref[...] = middle[1, 1, 8:40, :]


def map_kernel(weights, row_b, u1, o, d1, mapped_ref, row_ref, source, whole):
    load_planes((u1, o, d1), source)
    for k in range(8):
        cols = slice(128 * k, 128 * k + 128)
        whole[:, cols] = stencil_sum(weight_of(weights), source, 0, cols)
    mapped = whole[8:40, :]
    mapped_ref[...] = mapped
    row_ref[...] = row_b[...] + row_of(((3, mapped * mapped),))


def further_kernel(weights, u2, u1, o, d1, d2, back_ref, source, middle):
    load_planes((u2, u1, o, d1, d2), source)
    apply_stencils(weights, source, middle, back_ref)


def last_kernel(
    weights, table, image_back, loss_back, upstream, u2, u1, o, d1, d2, mapped_ref, out_ref, source, middle, back
):
    load_planes((u2, u1, o, d1, d2), source)
    apply_stencils(weights, source, middle, back)
    mapped_ref[...] = middle[1, 1, 8:40, :]
    factor = [weights[27 + k] for k in range(6)]
    u, again = upstream[...], image_back[8:40, :]
    first = factor[0] * u + factor[1] * loss_back[8:40, :] + factor[4] * again + factor[5] * back[8:40, :]
    second = factor[1] * u + factor[5] * again
    out_ref[:, 0:8, :] = x_forward(first, table).reshape(32, 8, 128)
    out_ref[:, 8:16, :] = x_forward(second, table).reshape(32, 8, 128)


def correlate_kernel(factor_ref, *refs):
    out_ref, scaled, mapped = refs[-3:]
    right, image, further, upstream = refs[0:3], refs[3:6], refs[6:9], refs[9:12]
    right_map, image_map, further_map, upstream_map = refs[12:16]
    f = [factor_ref[33 + k] for k in range(5)]
    for p in range(3):
        scaled[p] = f[0] * upstream[p][...] + f[1] * right[p][...] + f[2] * image[p][...] + f[3] * further[p][...]
    mapped[0] = (
        f[0] * upstream_map[...] + f[1] * right_map[...] + f[2] * image_map[...] + f[3] * further_map[...]
    )
    mapped[1] = right_map[...]
    mapped[2] = f[4] * image_map[...]
    lane = lanes((1, 128))
    out = jnp.zeros((1, 128), F32)
    column = lanes((ROWS, COLS))
    left_edge, right_edge = column < COLS - 1, column >= 1
    for c in range(3):
        parts = []
        for k in range(3):
            value = mapped[k]
            if c == 0:
                value = jnp.where(left_edge, pltpu.roll(value, COLS - 1, 1), 0.0)
            elif c == 2:
                value = jnp.where(right_edge, pltpu.roll(value, 1, 1), 0.0)
            parts.append(value)
        for a in range(3):
            for b in range(3):
                rows = slice(7 + b, 39 + b)
                total = parts[0] * right[a][rows, :] + parts[1] * scaled[a, rows, :] + parts[2] * image[a][rows, :]
                out = jnp.where(lane == 9 * a + 3 * b + c, jnp.sum(total), out)
    out_ref[...] = out


def shape(*dims):
    return jax.ShapeDtypeStruct(dims, F32)


STENCIL_SCRATCH = (
    pltpu.VMEM((3, 5, FRAME, COLS), F32),
    pltpu.VMEM((3, 3, FRAME, COLS), F32),
)
BACK_SCRATCH = (pltpu.VMEM((FRAME, COLS), F32),)


def call(body, out_shape, scalars, operands, scratch=(), far=(), planes=(), flops=400_000_000):
    operands = [*operands, *planes]
    smem, vmem, hbm = (pl.BlockSpec(memory_space=m) for m in (pltpu.SMEM, pltpu.VMEM, pltpu.HBM))
    outs = out_shape if isinstance(out_shape, tuple) else (out_shape,)
    first, count = len(scalars), len(scalars) + len(operands)
    buffers = [pltpu.VMEM(operands[i].shape, operands[i].dtype) for i in far]
    extra = [*buffers, pltpu.SemaphoreType.DMA((len(buffers),))] if buffers else []

    def whole(*refs):
        ins, results = list(refs[:count]), list(refs[count : count + len(outs)])
        own = refs[count + len(outs) :]
        held, sems, own = own[: len(buffers)], own[len(buffers)] if buffers else None, own[len(extra) :]
        copies = []
        for k, i in enumerate(far):
            copies.append(pltpu.make_async_copy(ins[first + i], held[k], sems.at[k]))
            ins[first + i] = held[k]
        for copy in copies:
            copy.start()
        for copy in copies:
            copy.wait()
        body(*ins, *results, *own)

    spec_in = [smem] * len(scalars) + [hbm if i in far else vmem for i in range(len(operands))]
    spec_out = (vmem,) * len(outs)
    return pl.pallas_call(
        whole,
        out_shape=out_shape,
        in_specs=spec_in,
        out_specs=spec_out if isinstance(out_shape, tuple) else spec_out[0],
        scratch_shapes=[*extra, *scratch],
        compiler_params=pltpu.CompilerParams(vmem_limit_bytes=VMEM),
        cost_estimate=pl.CostEstimate(flops=flops, bytes_accessed=4_000_000, transcendentals=0),
    )(*scalars, *operands)


def exchange(value):
    return lax.all_to_all(value, GY, 0, 0, tiled=True)


def moved(value, by):
    size = lax.axis_size(GZ)
    return lax.ppermute(value, GZ, [(i, i + by) for i in range(size) if 0 <= i + by < size])


def neighbours(value):
    return moved(value, 2), moved(value, 1), value, moved(value, -1), moved(value, -2)


def with_rows(value):
    size = lax.axis_size(GY)
    below = lax.ppermute(value[24:32], GY, [(i, i + 1) for i in range(size - 1)])
    above = lax.ppermute(value[0:8], GY, [(i + 1, i) for i in range(size - 1)])
    return jnp.concatenate([below, value, above], 0)


def from_all(row):
    size = lax.axis_size(GZ)
    return lax.all_to_all(jnp.broadcast_to(row[None], (size, 8, 128)), GZ, 0, 0, tiled=True)


def factors_of(m0, m1, m2, m3, u0, u1):
    def pair(m0, m1, m2, m3):
        step0 = m0 / m1
        norm1 = m0 - 2.0 * step0 * m1 + step0 * step0 * m2
        ratio = norm1 / m0
        keep = 1.0 + ratio
        curvature = keep * keep * m1 - 2.0 * keep * step0 * m2 + step0 * step0 * m3
        step1 = norm1 / curvature
        return step0 + step1 * keep, -step1 * step0

    (alpha, gamma), back = jax.vjp(pair, m0, m1, m2, m3)
    return (alpha, gamma, *back((u0, u1)))


def factors_kernel(weights_ref, rows, out_ref):
    total = jnp.sum(rows[:, 0, :], 0, keepdims=True)
    lane = lanes((1, 128))
    moments = [jnp.sum(jnp.where(lane == k, total, 0.0), axis=1, keepdims=True) for k in range(6)]
    alpha, gamma, g0, g1, g2, g3 = factors_of(*moments)
    for k in range(27):
        out_ref[k] = weights_ref[k]
    values = (alpha, gamma, 2.0 * g0, 2.0 * g1, 2.0 * g2, 2.0 * g3, gamma, g1, 2.0 * g2, 2.0 * g3, 2.0 * g3)
    for k, value in enumerate(values):
        out_ref[27 + k] = value[0, 0]


def local(measured, point_spread, stencil_weights, upstream):
    cells = measured.size * lax.axis_size(GY) * lax.axis_size(GZ)
    weights = stencil_weights.reshape(27)
    table, along_y = jnp.asarray(X_TABLE), jnp.asarray(Y_TABLE)
    measured, upstream = measured[0], upstream[0]
    tile, tiles, three = shape(32, 8, 128), shape(32, 16, 128), shape(32, 24, 128)
    spectral, frame, rows, row = shape(32 * BLOCKS, 128), shape(FRAME, COLS), shape(ROWS, COLS), shape(1, 128)

    first = exchange(call(spread_kernel, tiles, [], [table, measured, point_spread], far=(0, 1, 2)))
    first, grown = lax.optimization_barrier((first, with_rows(upstream)))

    right_out, bank = call(first_filter_kernel, (three, shape(2, 32 * BLOCKS, 128)), [], [along_y, first])
    right_arrived = exchange(right_out)
    loss_parts = neighbours(grown)
    right_arrived, loss_parts = lax.optimization_barrier((right_arrived, loss_parts))
    right, blurred = call(gather_two_kernel, (frame, frame), [], [table, right_arrived])

    right_parts = neighbours(right)
    image, right_map, image_send, row_b = call(
        image_kernel,
        (frame, rows, tile, row),
        [weights],
        [table, blurred, upstream],
        STENCIL_SCRATCH + BACK_SCRATCH,
        planes=right_parts,
    )
    image_arrived = exchange(image_send)
    image_near = (moved(image, 1), image, moved(image, -1))
    map_scratch = (pltpu.VMEM((3, 3, FRAME, COLS), F32), pltpu.VMEM((FRAME, COLS), F32))
    image_map, sums = call(map_kernel, (rows, row), [weights], [row_b], map_scratch, planes=image_near)
    further_out, image_spectrum = call(
        second_filter_kernel, (tiles, spectral), [], [along_y, image_arrived, bank, sums]
    )
    further_out, image_again, loss_parts = lax.optimization_barrier((further_out, image, loss_parts))
    further_arrived = exchange(further_out)
    image_parts = (moved(image_again, 2), *image_near, moved(image_again, -2))
    loss_back, loss_map = call(loss_kernel, (frame, rows), [weights], [], STENCIL_SCRATCH, planes=loss_parts)
    image_back = call(further_kernel, frame, [weights], [], STENCIL_SCRATCH, planes=image_parts)
    further_arrived, image_back, loss_back = lax.optimization_barrier((further_arrived, image_back, loss_back))

    further, row_sum = call(gather_sum_kernel, (frame, row), [], [table, further_arrived, image_back])
    moments = from_all(row_sum)
    further, moments = lax.optimization_barrier((further, moments))
    factors = pl.pallas_call(
        factors_kernel,
        out_shape=shape(38),
        in_specs=[pl.BlockSpec(memory_space=pltpu.SMEM), pl.BlockSpec(memory_space=pltpu.VMEM)],
        out_specs=pl.BlockSpec(memory_space=pltpu.SMEM),
    )(weights, moments)

    further_parts = neighbours(further)
    further_map, last_send = call(
        last_kernel,
        (rows, tiles),
        [factors],
        [table, image_back, loss_back, upstream],
        STENCIL_SCRATCH + BACK_SCRATCH,
        planes=further_parts,
    )
    last_arrived = exchange(last_send)

    operands = []
    for parts in (right_parts, image_parts, further_parts, loss_parts):
        operands += parts[1:4]
    operands += [right_map, image_map, further_map, loss_map]
    scratch = (pltpu.VMEM((3, FRAME, COLS), F32), pltpu.VMEM((3, ROWS, COLS), F32))
    terms = call(correlate_kernel, row, [factors], operands, scratch)
    result_out = call(last_filter_kernel, tiles, [factors], [along_y, last_arrived, bank, image_spectrum, terms])
    grad_measured, terms = call(final_kernel, (rows, row), [], [table, exchange(result_out)])
    terms = jnp.sum(from_all(terms)[:, 0, :], 0)
    grad_stencil = terms[:27].reshape(3, 3, 3) / math.sqrt(cells)
    return grad_measured[None], grad_stencil


def solution(mesh):
    return jax.shard_map(
        local,
        mesh=mesh,
        in_specs=(P(GZ, GY, None), P(GY, None), P(), P(GZ, GY, None)),
        out_specs=(P(GZ, GY, None), P()),
        check_vma=False,
    )
```

```python
import functools
import math

import jax
import jax.numpy as jnp
import ml_dtypes
import numpy as np
from jax import lax
from jax.experimental import pallas as pl
from jax.experimental.pallas import tpu as pltpu
from jax.sharding import Mesh
from jax.sharding import PartitionSpec as P

GY = "gy"
GZ = ("gz_0", "gz_1")
ROWS = 32
COLS = 1024
FRAME = 48
BLOCKS = 9
F32 = jnp.float32
BF16 = jnp.bfloat16
VMEM = 14 * 1024 * 1024
ALL_VMEM = 60 * 1024 * 1024


def split_table(table):
    high = table.astype(ml_dtypes.bfloat16)
    low = (table - high.astype(np.float64)).astype(ml_dtypes.bfloat16)
    return high, low


def x_table():
    part, half, device, i = np.meshgrid(
        np.arange(2), np.arange(2), np.arange(32), np.arange(8), indexing="ij"
    )
    kx = 2 * (16 * (device % 16) + 8 * half + i) + device // 16
    part, kx = part.reshape(-1, 1), kx.reshape(-1, 1)
    x = np.arange(COLS // 2)[None, :]
    angle = 2.0 * np.pi * ((kx * x) % COLS) / COLS
    flip = 1.0 - 2.0 * (x % 2)
    wave = np.where(part == 0, np.cos(angle), -np.sin(angle))
    return np.where((kx == 0) & (part == 1), flip, wave)


def y_tables():
    q = np.arange(32)[:, None]
    s = np.arange(32)[None, :]
    angle = 2.0 * np.pi * ((q * s) % 32) / 32
    first = np.concatenate([np.cos(angle), np.sin(angle)], 0)
    lane = np.arange(128)
    part, half, t = lane // 64, lane // 32 % 2, lane % 32
    turn = 2.0 * np.pi * q * t[None, :] / 1024
    sign = np.where(part == 0, 1.0, -1.0)[None, :]
    turn_cos, turn_sin = np.cos(turn), np.sin(turn) * sign
    angle = 2.0 * np.pi * ((t[:, None] * t[None, :]) % 32) / 32
    pi, po = part[:, None], part[None, :]
    block = np.where(pi == po, np.cos(angle), np.where(pi > po, np.sin(angle), -np.sin(angle)))
    second = np.where(half[:, None] == half[None, :], block, 0.0)
    return first, turn_cos, turn_sin, second


def packed_tables():
    first, turn_cos, turn_sin, second = y_tables()
    first = np.pad(first, ((0, 0), (0, 96)))
    tables = [*split_table(second), *split_table(second.T), *split_table(first)]
    return np.concatenate([*tables, turn_cos, turn_sin], 0).astype(np.float32)


X_TABLE = np.concatenate(split_table(x_table()), 0)
Y_TABLE = packed_tables()
SCALE = 2.0 / (COLS * 1024.0)


def halves(value):
    high = value.astype(BF16)
    return high, (value - high.astype(F32)).astype(BF16)


def dot(left, right):
    return lax.dot_general(left, right, (((1,), (0,)), ((), ())), preferred_element_type=F32)


def dot_nt(left, right):
    return lax.dot_general(left, right, (((1,), (1,)), ((), ())), preferred_element_type=F32)


def swap(value):
    return pltpu.roll(value, 64, 1)


def lanes(shape):
    return lax.broadcasted_iota(jnp.int32, shape, 1)


def sublanes(shape):
    return lax.broadcasted_iota(jnp.int32, shape, 0)


def x_forward(value, table_ref):
    left, right = value[:, : COLS // 2], value[:, COLS // 2 :]
    group = lanes((128, 128)) // 32
    outs = []
    for parity, folded in enumerate((left + right, left - right)):
        high, low = halves(folded)
        both = jnp.concatenate([high] * 4 + [low] * 4, 0)
        out = None
        for h in range(4):
            start = 256 * h + 128 * parity
            first = dot_nt(table_ref[start : start + 128, :], both)
            piece = first[:, :128] + first[:, 128:]
            piece = piece + dot_nt(table_ref[1024 + start : 1152 + start, :], both[:128])
            out = piece if out is None else jnp.where(group == h, piece, out)
        outs.append(out)
    return jnp.concatenate(outs, 0)


def x_inverse(spectra, table_ref):
    turned = [value.T for value in spectra]
    sums = []
    for parity in range(2):
        cols = slice(128 * parity, 128 * parity + 128)
        rows = [jnp.concatenate([v[32 * h : 32 * h + 32, cols] for h in range(4)], 1) for v in turned]
        left = rows[0] if len(rows) == 1 else jnp.concatenate(rows, 0)
        count = left.shape[0]
        high, low = halves(left)
        both = jnp.concatenate([high, low], 0)
        total = None
        for h in range(4):
            start = 256 * h + 128 * parity
            k = slice(128 * h, 128 * h + 128)
            first = dot(both[:, k], table_ref[start : start + 128, :])
            piece = first[:count] + first[count:] + dot(high[:, k], table_ref[1024 + start : 1152 + start, :])
            total = piece if total is None else total + piece
        sums.append(total)
    return jnp.concatenate([sums[0] + sums[1], sums[0] - sums[1]], 1)


class Lateral:
    def __init__(self, table):
        def piece(start, count, width):
            return table[start : start + count, 0:width].astype(BF16)

        self.second = (piece(0, 128, 128), piece(128, 128, 128))
        self.back = (piece(256, 128, 128), piece(384, 128, 128))
        self.first = (piece(512, 64, 32), piece(576, 64, 32))
        self.cos, self.sin = table[640:672, :], table[672:704, :]
        self.is_first = jnp.where(lax.axis_index(GY) == 0, 1.0, 0.0).astype(F32)
        self.sign = jnp.where(lanes((32, 128)) < 64, 1.0, -1.0)

    def over_s(self, blocks, direction):
        high, low = halves(jnp.concatenate(blocks, 1))
        both = dot(self.first[0], high) + dot(self.first[0], low) + dot(self.first[1], high)
        out = []
        for i in range(len(blocks)):
            cols = slice(128 * i, 128 * i + 128)
            out.append(both[:32, cols] + direction * self.sign * swap(both[32:, cols]))
        return out

    def over_t(self, value, tables):
        high, low = halves(value)
        return dot(high, tables[0]) + dot(low, tables[0]) + dot(high, tables[1])

    def forward(self, ref, offset):
        blocks = [ref[:, offset + i, :] for i in range(8)]
        lane = lanes((32, 128))
        nyquist = (lane >= 64) & (lane < 96)
        blocks.append(jnp.where(lane < 32, swap(blocks[0]), 0.0) * self.is_first)
        blocks[0] = jnp.where(nyquist, blocks[0] * (1.0 - self.is_first), blocks[0])
        blocks = self.over_s(blocks, 1.0)
        blocks = [z * self.cos + swap(z) * self.sin for z in blocks]
        return self.over_t(jnp.concatenate(blocks, 0), self.second)

    def inverse(self, spectrum):
        all_rows = self.over_t(spectrum, self.back)
        blocks = [all_rows[32 * i : 32 * i + 32] for i in range(BLOCKS)]
        blocks = [z * self.cos - swap(z) * self.sin for z in blocks]
        blocks = self.over_s(blocks, -1.0)
        lane = lanes((32, 128))
        nyquist = (lane >= 64) & (lane < 96)
        own = jnp.where(lane // 32 % 2 == 0, SCALE * (1.0 - 0.5 * self.is_first), SCALE)
        blocks[0] = (blocks[0] + jnp.where(nyquist, swap(blocks[8]), 0.0)) * own
        return [blocks[0]] + [z * SCALE for z in blocks[1:8]]

    def weighted_sum(self, value):
        lane, row = lanes(value.shape), sublanes(value.shape)
        weight = jnp.where((row < 32) & (lane // 32 % 2 == 0), 2.0 - self.is_first, 2.0)
        weight = jnp.where(row >= 256, 1.0, weight)
        return jnp.sum(value * weight) * (1.0 / (COLS * 1024.0))


def halo_rows(block):
    lane, row = lanes((32, 128)) % 32, sublanes((32, 128))
    after = jnp.where((lane < 8) & (row < 31), pltpu.roll(block, 31, 0), 0.0)
    before = jnp.where((lane >= 24) & (row > 0), pltpu.roll(block, 1, 0), 0.0)
    return after, before


def product(real, imaginary, value):
    return real * value + imaginary * swap(value)


def conjugate_factors(transfer):
    turned, left = swap(transfer), lanes(transfer.shape) < 64
    return jnp.where(left, transfer, turned), jnp.where(left, turned, -transfer)


def spread_kernel(table_ref, measured, point_spread, out_ref):
    for f, ref in enumerate((measured, point_spread)):
        out_ref[:, 8 * f : 8 * f + 8, :] = x_forward(ref[...], table_ref).reshape(32, 8, 128)


def first_filter_kernel(table, arrived, out_ref, bank_ref):
    lateral = Lateral(table)
    transfer = lateral.forward(arrived, 8)
    observed = lateral.forward(arrived, 0)
    real, imaginary = conjugate_factors(transfer)
    power = real * real + imaginary * imaginary
    spectrum = product(real, imaginary, observed)
    right = lateral.inverse(spectrum)
    image = lateral.inverse(spectrum * power)
    for i in range(8):
        out_ref[:, i, :] = right[i]
        out_ref[:, 8 + i, :] = image[i]
        after, before = halo_rows(right[i])
        image_after, image_before = halo_rows(image[i])
        image_after, image_before = pltpu.roll(image_after, 8, 1), pltpu.roll(image_before, 120, 1)
        out_ref[:, 16 + i, :] = after + before + image_after + image_before
    bank_ref[0] = transfer
    bank_ref[1] = spectrum


def second_filter_kernel(table, arrived, bank_ref, sums, out_ref, image_ref):
    lateral = Lateral(table)
    real, imaginary = conjugate_factors(bank_ref[0])
    power = real * real + imaginary * imaginary
    image = power * bank_ref[1] + lateral.forward(arrived, 0)
    filtered = power * image
    blocks = lateral.inverse(filtered)
    for i in range(8):
        out_ref[:, i, :] = blocks[i]
        after, before = halo_rows(blocks[i])
        out_ref[:, 8 + i, :] = after + before
    image_ref[...] = image
    row = sums[...] + jnp.where(lanes((1, 128)) == 3, lateral.weighted_sum(image * filtered), 0.0)
    out_ref[:, 8, :] = out_ref[:, 8, :] + pltpu.roll(jnp.broadcast_to(row, (32, 128)), 8, 1)


def last_filter_kernel(
    factors_ref, table, arrived, bank_ref, image_ref, terms, out_ref
):
    lateral = Lateral(table)
    factor_ref = [factors_ref[27 + k] for k in range(6)]
    real, imaginary = conjugate_factors(bank_ref[0])
    power = real * real + imaginary * imaginary
    image = image_ref[...]
    total = factor_ref[4] * image + factor_ref[5] * (power * image) + lateral.forward(arrived, 8)
    total = power * total + factor_ref[2] * bank_ref[1] + factor_ref[3] * image
    total = total + lateral.forward(arrived, 0)
    blocks = lateral.inverse(product(real, -imaginary, total))
    for i in range(8):
        out_ref[:, i, :] = blocks[i]
        out_ref[:, 8 + i, :] = jnp.broadcast_to(terms[...], (32, 128))


def gather_two_kernel(table_ref, arrived, right_ref, image_ref):
    tiles = [arrived[:, 8 * f : 8 * f + 8, :].reshape(256, 128) for f in range(3)]
    value = x_inverse(tiles, table_ref)
    right_ref[0:8, :] = value[88:96]
    right_ref[8:40, :] = value[0:32]
    right_ref[40:48, :] = value[64:72]
    image_ref[0:8, :] = value[80:88]
    image_ref[8:40, :] = value[32:64]
    image_ref[40:48, :] = value[72:80]


def gather_sum_kernel(table_ref, arrived, base, out_ref, row_ref):
    row = pltpu.roll(jnp.broadcast_to(jnp.sum(arrived[:, 8, :], 0, keepdims=True), (8, 128)), 120, 1)
    row_ref[...] = jnp.where(lanes((1, 128)) < 6, row[0:1], 0.0)
    tiles = [arrived[:, 8 * f : 8 * f + 8, :].reshape(256, 128) for f in range(2)]
    value = x_inverse(tiles, table_ref)
    out_ref[0:8, :] = base[0:8, :] + value[56:64]
    out_ref[8:40, :] = base[8:40, :] + value[0:32]
    out_ref[40:48, :] = base[40:48, :] + value[32:40]


def final_kernel(table_ref, arrived, out_ref, row_ref):
    out_ref[...] = x_inverse([arrived[:, 0:8, :].reshape(256, 128)], table_ref)
    row_ref[...] = jnp.sum(arrived[:, 8, :], 0, keepdims=True)


def shifted_columns(value):
    column = lanes(value.shape)
    left = jnp.where(column >= 1, pltpu.roll(value, 1, 1), 0.0)
    right = jnp.where(column < COLS - 1, pltpu.roll(value, COLS - 1, 1), 0.0)
    return left, right


def stencil_sum(weight, source, start, cols):
    total = None
    for b in range(3):
        part = None
        for a in range(3):
            for c in range(3):
                term = weight(a, b, c) * source[c, start + a, :, cols]
                part = term if part is None else part + term
        if b == 0:
            part = pltpu.roll(part, 1, 0)
        elif b == 2:
            part = pltpu.roll(part, FRAME - 1, 0)
        total = part if total is None else total + part
    return total


def load_planes(parts, source):
    for p, ref in enumerate(parts):
        value = ref[...]
        source[1, p] = value
        source[0, p], source[2, p] = shifted_columns(value)


def row_bounds():
    device, plane, planes = lax.axis_index(GY), lax.axis_index(GZ), lax.axis_size(GZ)
    lowest = jnp.where(device > 0, 0, 8)
    highest = jnp.where(device < 31, FRAME, 40)

    def highest_at(here):
        return jnp.where((here >= 0) & (here < planes), highest, 0)

    return sublanes((FRAME, 128)), lowest, highest, lambda p: highest_at(plane + p)


def weight_of(weights_ref):
    return lambda a, b, c: weights_ref[9 * a + 3 * b + c]


def flipped_of(weights_ref):
    return lambda a, b, c: weights_ref[26 - 9 * a - 3 * b - c]


def apply_stencils(weights_ref, source, middle, back_ref):
    row, lowest, highest, highest_at = row_bounds()
    for p in range(3):
        valid = (row >= lowest) & (row < highest_at(p - 1))
        for k in range(8):
            cols = slice(128 * k, 128 * k + 128)
            value = stencil_sum(weight_of(weights_ref), source, p, cols)
            middle[1, p, :, cols] = jnp.where(valid, value, 0.0)
    for p in range(3):
        middle[0, p], middle[2, p] = shifted_columns(middle[1, p])
    inside = (row >= lowest) & (row < highest)
    for k in range(8):
        cols = slice(128 * k, 128 * k + 128)
        back_ref[:, cols] = jnp.where(inside, stencil_sum(flipped_of(weights_ref), middle, 0, cols), 0.0)


def row_of(values):
    lane = lanes((1, 128))
    out = jnp.zeros((1, 128), F32)
    for k, value in values:
        out = jnp.where(lane == k, jnp.sum(value), out)
    return out


def image_kernel(weights, table, blurred, upstream, u2, u1, o, d1, d2, image_ref, mapped_ref, out_ref, row_ref, *scratch):
    source, middle, back = scratch
    load_planes((u2, u1, o, d1, d2), source)
    apply_stencils(weights, source, middle, back)
    out_ref[...] = x_forward(back[8:40, :], table).reshape(32, 8, 128)
    mapped_ref[...] = middle[1, 1, 8:40, :]
    image_ref[...] = blurred[...] + back[...]
    b, ab, u = source[1, 2, 8:40, :], image_ref[8:40, :], upstream[...]
    row_ref[...] = row_of(((0, b * b), (1, b * ab), (2, ab * ab), (4, u * b), (5, u * ab)))


def map_kernel(weights, row_b, u1, o, d1, mapped_ref, row_ref, source, whole):
    load_planes((u1, o, d1), source)
    for k in range(8):
        cols = slice(128 * k, 128 * k + 128)
        whole[:, cols] = stencil_sum(weight_of(weights), source, 0, cols)
    mapped = whole[8:40, :]
    mapped_ref[...] = mapped
    row_ref[...] = row_b[...] + row_of(((3, mapped * mapped),))


def further_kernel(weights, u2, u1, o, d1, d2, back_ref, source, middle):
    load_planes((u2, u1, o, d1, d2), source)
    apply_stencils(weights, source, middle, back_ref)


def last_kernel(
    weights, table, image_back, upstream, u2, u1, o, d1, d2, mapped_ref, out_ref, source, middle, back
):
    load_planes((u2, u1, o, d1, d2), source)
    apply_stencils(weights, source, middle, back)
    mapped_ref[...] = middle[1, 1, 8:40, :]
    alpha, gamma, twice_g2, twice_g3 = weights[27], weights[28], weights[31], weights[32]
    u, again = upstream[...], image_back[8:40, :]
    first = alpha * u + twice_g2 * again + back[8:40, :]
    second = gamma * u + twice_g3 * again
    out_ref[:, 0:8, :] = x_forward(first, table).reshape(32, 8, 128)
    out_ref[:, 8:16, :] = x_forward(second, table).reshape(32, 8, 128)


def correlate_kernel(factor_ref, *refs):
    out_ref, scaled, mapped = refs[-3:]
    right, image, mixed = refs[0:3], refs[3:6], refs[6:9]
    right_map, image_map, mixed_map = refs[9:12]
    g1, twice_g2, twice_g3 = (factor_ref[k] for k in (33, 31, 32))
    for p in range(3):
        scaled[p] = mixed[p][...] + g1 * right[p][...] + twice_g2 * image[p][...]
    mapped[0] = mixed_map[...] + g1 * right_map[...] + twice_g2 * image_map[...]
    mapped[1] = right_map[...]
    mapped[2] = twice_g3 * image_map[...]
    lane = lanes((1, 128))
    out = jnp.zeros((1, 128), F32)
    column = lanes((ROWS, COLS))
    left_edge, right_edge = column < COLS - 1, column >= 1
    for c in range(3):
        parts = []
        for k in range(3):
            value = mapped[k]
            if c == 0:
                value = jnp.where(left_edge, pltpu.roll(value, COLS - 1, 1), 0.0)
            elif c == 2:
                value = jnp.where(right_edge, pltpu.roll(value, 1, 1), 0.0)
            parts.append(value)
        for a in range(3):
            for b in range(3):
                rows = slice(7 + b, 39 + b)
                total = parts[0] * right[a][rows, :] + parts[1] * scaled[a, rows, :] + parts[2] * image[a][rows, :]
                out = jnp.where(lane == 9 * a + 3 * b + c, jnp.sum(total), out)
    out_ref[...] = out


def shape(*dims):
    return jax.ShapeDtypeStruct(dims, F32)


STENCIL_SCRATCH = (
    pltpu.VMEM((3, 5, FRAME, COLS), F32),
    pltpu.VMEM((3, 3, FRAME, COLS), F32),
)
BACK_SCRATCH = (pltpu.VMEM((FRAME, COLS), F32),)


def call(body, out_shape, scalars, operands, scratch=(), far=(), planes=(), limit=VMEM, flops=400_000_000):
    operands = [*operands, *planes]
    smem, vmem, hbm = (pl.BlockSpec(memory_space=m) for m in (pltpu.SMEM, pltpu.VMEM, pltpu.HBM))
    outs = out_shape if isinstance(out_shape, tuple) else (out_shape,)
    first, count = len(scalars), len(scalars) + len(operands)
    buffers = [pltpu.VMEM(operands[i].shape, operands[i].dtype) for i in far]
    extra = [*buffers, pltpu.SemaphoreType.DMA((len(buffers),))] if buffers else []

    def whole(*refs):
        ins, results = list(refs[:count]), list(refs[count : count + len(outs)])
        own = refs[count + len(outs) :]
        held, sems, own = own[: len(buffers)], own[len(buffers)] if buffers else None, own[len(extra) :]
        copies = []
        for k, i in enumerate(far):
            copies.append(pltpu.make_async_copy(ins[first + i], held[k], sems.at[k]))
            ins[first + i] = held[k]
        for copy in copies:
            copy.start()
        for copy in copies:
            copy.wait()
        body(*ins, *results, *own)

    spec_in = [smem] * len(scalars) + [hbm if i in far else vmem for i in range(len(operands))]
    spec_out = (vmem,) * len(outs)
    return pl.pallas_call(
        whole,
        out_shape=out_shape,
        in_specs=spec_in,
        out_specs=spec_out if isinstance(out_shape, tuple) else spec_out[0],
        scratch_shapes=[*extra, *scratch],
        compiler_params=pltpu.CompilerParams(vmem_limit_bytes=limit),
        cost_estimate=pl.CostEstimate(flops=flops, bytes_accessed=4_000_000, transcendentals=0),
    )(*scalars, *operands)


def exchange(value):
    return lax.all_to_all(value, GY, 0, 0, tiled=True)


def moved(value, by):
    size = lax.axis_size(GZ)
    return lax.ppermute(value, GZ, [(i, i + by) for i in range(size) if 0 <= i + by < size])


def neighbours(value):
    return moved(value, 2), moved(value, 1), value, moved(value, -1), moved(value, -2)


def with_rows(value):
    size = lax.axis_size(GY)
    below = lax.ppermute(value[24:32], GY, [(i, i + 1) for i in range(size - 1)])
    above = lax.ppermute(value[0:8], GY, [(i + 1, i) for i in range(size - 1)])
    return jnp.concatenate([below, value, above], 0)


def from_all(row):
    size = lax.axis_size(GZ)
    return lax.all_to_all(jnp.broadcast_to(row[None], (size, 8, 128)), GZ, 0, 0, tiled=True)


def factors_of(m0, m1, m2, m3, u0, u1):
    def pair(m0, m1, m2, m3):
        step0 = m0 / m1
        norm1 = m0 - 2.0 * step0 * m1 + step0 * step0 * m2
        ratio = norm1 / m0
        keep = 1.0 + ratio
        curvature = keep * keep * m1 - 2.0 * keep * step0 * m2 + step0 * step0 * m3
        step1 = norm1 / curvature
        return step0 + step1 * keep, -step1 * step0

    (alpha, gamma), back = jax.vjp(pair, m0, m1, m2, m3)
    return (alpha, gamma, *back((u0, u1)))


def factors_kernel(weights_ref, rows, further, grown, out_ref, mixed_ref):
    total = jnp.sum(rows[:, 0, :], 0, keepdims=True)
    lane = lanes((1, 128))
    moments = [jnp.sum(jnp.where(lane == k, total, 0.0), axis=1, keepdims=True) for k in range(6)]
    alpha, gamma, g0, g1, g2, g3 = factors_of(*moments)
    for k in range(27):
        out_ref[k] = weights_ref[k]
    for k, value in enumerate((alpha, gamma, 2.0 * g0, 2.0 * g1, 2.0 * g2, 2.0 * g3, g1)):
        out_ref[27 + k] = value[0, 0]
    mixed_ref[...] = gamma * grown[...] + (2.0 * g3) * further[...]


def local(measured, point_spread, stencil_weights, upstream):
    cells = measured.size * lax.axis_size(GY) * lax.axis_size(GZ)
    weights = stencil_weights.reshape(27)
    table, along_y = jnp.asarray(X_TABLE), jnp.asarray(Y_TABLE)
    measured, upstream = measured[0], upstream[0]
    tile, tiles, three = shape(32, 8, 128), shape(32, 16, 128), shape(32, 24, 128)
    spectral, frame, rows, row = shape(32 * BLOCKS, 128), shape(FRAME, COLS), shape(ROWS, COLS), shape(1, 128)

    first = exchange(
        call(spread_kernel, tiles, [], [table, measured, point_spread], far=(0, 1, 2), limit=ALL_VMEM)
    )
    first, grown = lax.optimization_barrier((first, with_rows(upstream)))

    right_out, bank = call(first_filter_kernel, (three, shape(2, 32 * BLOCKS, 128)), [], [along_y, first])
    right, blurred = call(gather_two_kernel, (frame, frame), [], [table, exchange(right_out)])

    right_parts = neighbours(right)
    image, right_map, image_send, row_b = call(
        image_kernel,
        (frame, rows, tile, row),
        [weights],
        [table, blurred, upstream],
        STENCIL_SCRATCH + BACK_SCRATCH,
        planes=right_parts,
    )
    image_arrived = exchange(image_send)
    image_near = (moved(image, 1), image, moved(image, -1))
    map_scratch = (pltpu.VMEM((3, 3, FRAME, COLS), F32), pltpu.VMEM((FRAME, COLS), F32))
    image_map, sums = call(map_kernel, (rows, row), [weights], [row_b], map_scratch, planes=image_near)
    further_out, image_spectrum = call(
        second_filter_kernel, (tiles, spectral), [], [along_y, image_arrived, bank, sums]
    )
    further_out, image_again = lax.optimization_barrier((further_out, image))
    further_arrived = exchange(further_out)
    image_parts = (moved(image_again, 2), *image_near, moved(image_again, -2))
    image_back = call(further_kernel, frame, [weights], [], STENCIL_SCRATCH, planes=image_parts)
    further_arrived, image_back = lax.optimization_barrier((further_arrived, image_back))

    further, row_sum = call(gather_sum_kernel, (frame, row), [], [table, further_arrived, image_back])
    smem, vmem = (pl.BlockSpec(memory_space=m) for m in (pltpu.SMEM, pltpu.VMEM))
    factors, mixed = pl.pallas_call(
        factors_kernel,
        out_shape=(shape(34), frame),
        in_specs=[smem, vmem, vmem, vmem],
        out_specs=(smem, vmem),
        compiler_params=pltpu.CompilerParams(vmem_limit_bytes=VMEM),
    )(weights, from_all(row_sum), further, grown)

    mixed_parts = neighbours(mixed)
    mixed_map, last_send = call(
        last_kernel,
        (rows, tiles),
        [factors],
        [table, image_back, upstream],
        STENCIL_SCRATCH + BACK_SCRATCH,
        planes=mixed_parts,
    )
    operands = []
    for parts in (right_parts, image_parts, mixed_parts):
        operands += parts[1:4]
    operands += [right_map, image_map, mixed_map]
    scratch = (pltpu.VMEM((3, FRAME, COLS), F32), pltpu.VMEM((3, ROWS, COLS), F32))
    terms = call(correlate_kernel, row, [factors], operands, scratch, far=tuple(range(12)), limit=ALL_VMEM)
    terms = lax.psum(terms, "gz_1")
    last_arrived = exchange(last_send)
    result_out = call(last_filter_kernel, tiles, [factors], [along_y, last_arrived, bank, image_spectrum, terms])
    grad_measured, terms = call(final_kernel, (rows, row), [], [table, exchange(result_out)])
    grad_stencil = lax.psum(terms, "gz_0")[0, :27].reshape(3, 3, 3) / math.sqrt(cells)
    return grad_measured[None], grad_stencil


def solution(mesh):
    groups, planes = mesh.devices.shape
    finer = Mesh(mesh.devices.reshape(groups, 4, planes // 4), (GY, *GZ))
    return jax.shard_map(
        local,
        mesh=finer,
        in_specs=(P(GZ, GY, None), P(GY, None), P(), P(GZ, GY, None)),
        out_specs=(P(GZ, GY, None), P()),
        check_vma=False,
    )
```

```python
import functools
import math

import jax
import jax.numpy as jnp
import ml_dtypes
import numpy as np
from jax import lax
from jax.experimental import pallas as pl
from jax.experimental.pallas import tpu as pltpu
from jax.sharding import Mesh
from jax.sharding import PartitionSpec as P

GY = "gy"
GZ = ("gz_0", "gz_1")
ROWS = 32
COLS = 1024
FRAME = 48
BLOCKS = 9
F32 = jnp.float32
BF16 = jnp.bfloat16
VMEM = 14 * 1024 * 1024
ALL_VMEM = 60 * 1024 * 1024


def split_table(table):
    high = table.astype(ml_dtypes.bfloat16)
    low = (table - high.astype(np.float64)).astype(ml_dtypes.bfloat16)
    return high, low


def x_table():
    part, half, device, i = np.meshgrid(
        np.arange(2), np.arange(2), np.arange(32), np.arange(8), indexing="ij"
    )
    kx = 2 * (16 * (device % 16) + 8 * half + i) + device // 16
    part, kx = part.reshape(-1, 1), kx.reshape(-1, 1)
    x = np.arange(COLS // 2)[None, :]
    angle = 2.0 * np.pi * ((kx * x) % COLS) / COLS
    flip = 1.0 - 2.0 * (x % 2)
    wave = np.where(part == 0, np.cos(angle), -np.sin(angle))
    return np.where((kx == 0) & (part == 1), flip, wave)


def y_tables():
    q = np.arange(32)[:, None]
    s = np.arange(32)[None, :]
    angle = 2.0 * np.pi * ((q * s) % 32) / 32
    first = np.concatenate([np.cos(angle), np.sin(angle)], 0)
    lane = np.arange(128)
    part, half, t = lane // 64, lane // 32 % 2, lane % 32
    turn = 2.0 * np.pi * q * t[None, :] / 1024
    sign = np.where(part == 0, 1.0, -1.0)[None, :]
    turn_cos, turn_sin = np.cos(turn), np.sin(turn) * sign
    angle = 2.0 * np.pi * ((t[:, None] * t[None, :]) % 32) / 32
    pi, po = part[:, None], part[None, :]
    block = np.where(pi == po, np.cos(angle), np.where(pi > po, np.sin(angle), -np.sin(angle)))
    second = np.where(half[:, None] == half[None, :], block, 0.0)
    return first, turn_cos, turn_sin, second


def packed_tables():
    first, turn_cos, turn_sin, second = y_tables()
    first = np.pad(first, ((0, 0), (0, 96)))
    return np.concatenate([second, first, turn_cos, turn_sin], 0).astype(np.float32)


X_TABLE = np.concatenate(split_table(x_table()), 0)
Y_TABLE = packed_tables()
SCALE = 2.0 / (COLS * 1024.0)


def halves(value):
    high = value.astype(BF16)
    return high, (value - high.astype(F32)).astype(BF16)


def dot(left, right):
    return lax.dot_general(left, right, (((1,), (0,)), ((), ())), preferred_element_type=F32)


def dot_nt(left, right):
    return lax.dot_general(left, right, (((1,), (1,)), ((), ())), preferred_element_type=F32)


def swap(value):
    return pltpu.roll(value, 64, 1)


def lanes(shape):
    return lax.broadcasted_iota(jnp.int32, shape, 1)


def sublanes(shape):
    return lax.broadcasted_iota(jnp.int32, shape, 0)


def x_forward(value, table_ref):
    left, right = value[:, : COLS // 2], value[:, COLS // 2 :]
    group = lanes((128, 128)) // 32
    outs = []
    for parity, folded in enumerate((left + right, left - right)):
        high, low = halves(folded)
        both = jnp.concatenate([high] * 4 + [low] * 4, 0)
        out = None
        for h in range(4):
            start = 256 * h + 128 * parity
            first = dot_nt(table_ref[start : start + 128, :], both)
            piece = first[:, :128] + first[:, 128:]
            piece = piece + dot_nt(table_ref[1024 + start : 1152 + start, :], both[:128])
            out = piece if out is None else jnp.where(group == h, piece, out)
        outs.append(out)
    return jnp.concatenate(outs, 0)


def x_inverse(spectra, table_ref):
    turned = [value.T for value in spectra]
    sums = []
    for parity in range(2):
        cols = slice(128 * parity, 128 * parity + 128)
        rows = [jnp.concatenate([v[32 * h : 32 * h + 32, cols] for h in range(4)], 1) for v in turned]
        left = rows[0] if len(rows) == 1 else jnp.concatenate(rows, 0)
        count = left.shape[0]
        high, low = halves(left)
        both = jnp.concatenate([high, low], 0)
        total = None
        for h in range(4):
            start = 256 * h + 128 * parity
            k = slice(128 * h, 128 * h + 128)
            first = dot(both[:, k], table_ref[start : start + 128, :])
            piece = first[:count] + first[count:] + dot(high[:, k], table_ref[1024 + start : 1152 + start, :])
            total = piece if total is None else total + piece
        sums.append(total)
    return jnp.concatenate([sums[0] + sums[1], sums[0] - sums[1]], 1)


class Lateral:
    def __init__(self, table):
        second = table[0:128, :]
        self.second = halves(second)
        self.back = halves(second.T)
        self.first = halves(table[128:192, :][:, 0:32])
        self.cos, self.sin = table[192:224, :], table[224:256, :]
        self.is_first = jnp.where(lax.axis_index(GY) == 0, 1.0, 0.0).astype(F32)
        self.sign = jnp.where(lanes((32, 128)) < 64, 1.0, -1.0)

    def over_s(self, blocks, direction):
        high, low = halves(jnp.concatenate(blocks, 1))
        both = dot(self.first[0], high) + dot(self.first[0], low) + dot(self.first[1], high)
        out = []
        for i in range(len(blocks)):
            cols = slice(128 * i, 128 * i + 128)
            out.append(both[:32, cols] + direction * self.sign * swap(both[32:, cols]))
        return out

    def over_t(self, value, tables):
        high, low = halves(value)
        return dot(high, tables[0]) + dot(low, tables[0]) + dot(high, tables[1])

    def forward(self, ref, offset):
        blocks = [ref[:, offset + i, :] for i in range(8)]
        lane = lanes((32, 128))
        nyquist = (lane >= 64) & (lane < 96)
        blocks.append(jnp.where(lane < 32, swap(blocks[0]), 0.0) * self.is_first)
        blocks[0] = jnp.where(nyquist, blocks[0] * (1.0 - self.is_first), blocks[0])
        blocks = self.over_s(blocks, 1.0)
        blocks = [z * self.cos + swap(z) * self.sin for z in blocks]
        return self.over_t(jnp.concatenate(blocks, 0), self.second)

    def inverse(self, spectrum):
        all_rows = self.over_t(spectrum, self.back)
        blocks = [all_rows[32 * i : 32 * i + 32] for i in range(BLOCKS)]
        blocks = [z * self.cos - swap(z) * self.sin for z in blocks]
        blocks = self.over_s(blocks, -1.0)
        lane = lanes((32, 128))
        nyquist = (lane >= 64) & (lane < 96)
        own = jnp.where(lane // 32 % 2 == 0, SCALE * (1.0 - 0.5 * self.is_first), SCALE)
        blocks[0] = (blocks[0] + jnp.where(nyquist, swap(blocks[8]), 0.0)) * own
        return [blocks[0]] + [z * SCALE for z in blocks[1:8]]

    def weighted_sum(self, value):
        lane, row = lanes(value.shape), sublanes(value.shape)
        weight = jnp.where((row < 32) & (lane // 32 % 2 == 0), 2.0 - self.is_first, 2.0)
        weight = jnp.where(row >= 256, 1.0, weight)
        return jnp.sum(value * weight) * (1.0 / (COLS * 1024.0))


def halo_rows(block):
    lane, row = lanes((32, 128)) % 32, sublanes((32, 128))
    after = jnp.where((lane < 8) & (row < 31), pltpu.roll(block, 31, 0), 0.0)
    before = jnp.where((lane >= 24) & (row > 0), pltpu.roll(block, 1, 0), 0.0)
    return after, before


def product(real, imaginary, value):
    return real * value + imaginary * swap(value)


def conjugate_factors(transfer):
    turned, left = swap(transfer), lanes(transfer.shape) < 64
    return jnp.where(left, transfer, turned), jnp.where(left, turned, -transfer)


def spread_kernel(table_ref, measured, point_spread, out_ref):
    for f, ref in enumerate((measured, point_spread)):
        out_ref[:, 8 * f : 8 * f + 8, :] = x_forward(ref[...], table_ref).reshape(32, 8, 128)


def first_filter_kernel(table, arrived, out_ref, bank_ref):
    lateral = Lateral(table)
    transfer = lateral.forward(arrived, 8)
    observed = lateral.forward(arrived, 0)
    real, imaginary = conjugate_factors(transfer)
    power = real * real + imaginary * imaginary
    spectrum = product(real, imaginary, observed)
    right = lateral.inverse(spectrum)
    image = lateral.inverse(spectrum * power)
    for i in range(8):
        out_ref[:, i, :] = right[i]
        out_ref[:, 8 + i, :] = image[i]
        after, before = halo_rows(right[i])
        image_after, image_before = halo_rows(image[i])
        image_after, image_before = pltpu.roll(image_after, 8, 1), pltpu.roll(image_before, 120, 1)
        out_ref[:, 16 + i, :] = after + before + image_after + image_before
    bank_ref[0] = transfer
    bank_ref[1] = spectrum


def second_filter_kernel(table, arrived, bank_ref, sums, out_ref, image_ref):
    lateral = Lateral(table)
    real, imaginary = conjugate_factors(bank_ref[0])
    power = real * real + imaginary * imaginary
    image = power * bank_ref[1] + lateral.forward(arrived, 0)
    filtered = power * image
    blocks = lateral.inverse(filtered)
    for i in range(8):
        out_ref[:, i, :] = blocks[i]
        after, before = halo_rows(blocks[i])
        out_ref[:, 8 + i, :] = after + before
    image_ref[...] = image
    row = sums[...] + jnp.where(lanes((1, 128)) == 3, lateral.weighted_sum(image * filtered), 0.0)
    out_ref[:, 8, :] = out_ref[:, 8, :] + pltpu.roll(jnp.broadcast_to(row, (32, 128)), 8, 1)


def last_filter_kernel(
    factors_ref, table, arrived, bank_ref, image_ref, terms, out_ref
):
    lateral = Lateral(table)
    factor_ref = [factors_ref[27 + k] for k in range(6)]
    real, imaginary = conjugate_factors(bank_ref[0])
    power = real * real + imaginary * imaginary
    image = image_ref[...]
    total = factor_ref[4] * image + factor_ref[5] * (power * image) + lateral.forward(arrived, 8)
    total = power * total + factor_ref[2] * bank_ref[1] + factor_ref[3] * image
    total = total + lateral.forward(arrived, 0)
    blocks = lateral.inverse(product(real, -imaginary, total))
    for i in range(8):
        out_ref[:, i, :] = blocks[i]
        out_ref[:, 8 + i, :] = jnp.broadcast_to(terms[...], (32, 128))


def gather_two_kernel(table_ref, arrived, right_ref, image_ref):
    tiles = [arrived[:, 8 * f : 8 * f + 8, :].reshape(256, 128) for f in range(3)]
    value = x_inverse(tiles, table_ref)
    right_ref[0:8, :] = value[88:96]
    right_ref[8:40, :] = value[0:32]
    right_ref[40:48, :] = value[64:72]
    image_ref[0:8, :] = value[80:88]
    image_ref[8:40, :] = value[32:64]
    image_ref[40:48, :] = value[72:80]


def gather_sum_kernel(table_ref, arrived, base, out_ref, row_ref):
    row = pltpu.roll(jnp.broadcast_to(jnp.sum(arrived[:, 8, :], 0, keepdims=True), (8, 128)), 120, 1)
    row_ref[...] = jnp.where(lanes((1, 128)) < 6, row[0:1], 0.0)
    tiles = [arrived[:, 8 * f : 8 * f + 8, :].reshape(256, 128) for f in range(2)]
    value = x_inverse(tiles, table_ref)
    out_ref[0:8, :] = base[0:8, :] + value[56:64]
    out_ref[8:40, :] = base[8:40, :] + value[0:32]
    out_ref[40:48, :] = base[40:48, :] + value[32:40]


def final_kernel(table_ref, arrived, out_ref, row_ref):
    out_ref[...] = x_inverse([arrived[:, 0:8, :].reshape(256, 128)], table_ref)
    row_ref[...] = jnp.sum(arrived[:, 8, :], 0, keepdims=True)


def shifted_columns(value):
    column = lanes(value.shape)
    left = jnp.where(column >= 1, pltpu.roll(value, 1, 1), 0.0)
    right = jnp.where(column < COLS - 1, pltpu.roll(value, COLS - 1, 1), 0.0)
    return left, right


def stencil_sum(weight, source, start, cols):
    total = None
    for b in range(3):
        part = None
        for a in range(3):
            for c in range(3):
                term = weight(a, b, c) * source[c, start + a, :, cols]
                part = term if part is None else part + term
        if b == 0:
            part = pltpu.roll(part, 1, 0)
        elif b == 2:
            part = pltpu.roll(part, FRAME - 1, 0)
        total = part if total is None else total + part
    return total


def load_planes(parts, source):
    for p, ref in enumerate(parts):
        value = ref[...]
        source[1, p] = value
        source[0, p], source[2, p] = shifted_columns(value)


def row_bounds():
    device, plane, planes = lax.axis_index(GY), lax.axis_index(GZ), lax.axis_size(GZ)
    lowest = jnp.where(device > 0, 0, 8)
    highest = jnp.where(device < 31, FRAME, 40)

    def highest_at(here):
        return jnp.where((here >= 0) & (here < planes), highest, 0)

    return sublanes((FRAME, 128)), lowest, highest, lambda p: highest_at(plane + p)


def weight_of(weights_ref):
    return lambda a, b, c: weights_ref[9 * a + 3 * b + c]


def flipped_of(weights_ref):
    return lambda a, b, c: weights_ref[26 - 9 * a - 3 * b - c]


def apply_stencils(weights_ref, source, middle, back_ref):
    row, lowest, highest, highest_at = row_bounds()
    for p in range(3):
        valid = (row >= lowest) & (row < highest_at(p - 1))
        for k in range(8):
            cols = slice(128 * k, 128 * k + 128)
            value = stencil_sum(weight_of(weights_ref), source, p, cols)
            middle[1, p, :, cols] = jnp.where(valid, value, 0.0)
    for p in range(3):
        middle[0, p], middle[2, p] = shifted_columns(middle[1, p])
    inside = (row >= lowest) & (row < highest)
    for k in range(8):
        cols = slice(128 * k, 128 * k + 128)
        back_ref[:, cols] = jnp.where(inside, stencil_sum(flipped_of(weights_ref), middle, 0, cols), 0.0)


def row_of(values):
    lane = lanes((1, 128))
    out = jnp.zeros((1, 128), F32)
    for k, value in values:
        out = jnp.where(lane == k, jnp.sum(value), out)
    return out


def image_kernel(weights, table, blurred, upstream, u2, u1, o, d1, d2, image_ref, mapped_ref, out_ref, row_ref, *scratch):
    source, middle, back = scratch
    load_planes((u2, u1, o, d1, d2), source)
    apply_stencils(weights, source, middle, back)
    out_ref[...] = x_forward(back[8:40, :], table).reshape(32, 8, 128)
    mapped_ref[...] = middle[1, 1, 8:40, :]
    image_ref[...] = blurred[...] + back[...]
    b, ab, u = source[1, 2, 8:40, :], image_ref[8:40, :], upstream[...]
    row_ref[...] = row_of(((0, b * b), (1, b * ab), (2, ab * ab), (4, u * b), (5, u * ab)))


def map_kernel(weights, row_b, u1, o, d1, mapped_ref, row_ref, source):
    load_planes((u1, o, d1), source)
    row, lowest, highest, _ = row_bounds()
    inside = (row >= lowest) & (row < highest)
    for k in range(8):
        cols = slice(128 * k, 128 * k + 128)
        mapped_ref[:, cols] = jnp.where(inside, stencil_sum(weight_of(weights), source, 0, cols), 0.0)
    mapped = mapped_ref[8:40, :]
    row_ref[...] = row_b[...] + row_of(((3, mapped * mapped),))


def further_kernel(weights, u1, o, d1, back_ref, middle):
    load_planes((u1, o, d1), middle)
    row, lowest, highest, _ = row_bounds()
    inside = (row >= lowest) & (row < highest)
    for k in range(8):
        cols = slice(128 * k, 128 * k + 128)
        back_ref[:, cols] = jnp.where(inside, stencil_sum(flipped_of(weights), middle, 0, cols), 0.0)


def last_kernel(
    weights, table, image_back, upstream, u2, u1, o, d1, d2, mapped_ref, out_ref, source, middle, back
):
    load_planes((u2, u1, o, d1, d2), source)
    apply_stencils(weights, source, middle, back)
    mapped_ref[...] = middle[1, 1, 8:40, :]
    alpha, gamma, twice_g2, twice_g3 = weights[27], weights[28], weights[31], weights[32]
    u, again = upstream[...], image_back[8:40, :]
    first = alpha * u + twice_g2 * again + back[8:40, :]
    second = gamma * u + twice_g3 * again
    out_ref[:, 0:8, :] = x_forward(first, table).reshape(32, 8, 128)
    out_ref[:, 8:16, :] = x_forward(second, table).reshape(32, 8, 128)


def correlate_kernel(factor_ref, *refs):
    out_ref, scaled, mapped = refs[-3:]
    right, image, mixed = refs[0:3], refs[3:6], refs[6:9]
    right_map, image_map, mixed_map = refs[9:12]
    g1, twice_g2, twice_g3 = (factor_ref[k] for k in (33, 31, 32))
    for p in range(3):
        scaled[p] = mixed[p][...] + g1 * right[p][...] + twice_g2 * image[p][...]
    mapped[0] = mixed_map[...] + g1 * right_map[...] + twice_g2 * image_map[8:40, :]
    mapped[1] = right_map[...]
    mapped[2] = twice_g3 * image_map[8:40, :]
    lane = lanes((1, 128))
    out = jnp.zeros((1, 128), F32)
    column = lanes((ROWS, COLS))
    left_edge, right_edge = column < COLS - 1, column >= 1
    for c in range(3):
        parts = []
        for k in range(3):
            value = mapped[k]
            if c == 0:
                value = jnp.where(left_edge, pltpu.roll(value, COLS - 1, 1), 0.0)
            elif c == 2:
                value = jnp.where(right_edge, pltpu.roll(value, 1, 1), 0.0)
            parts.append(value)
        for a in range(3):
            for b in range(3):
                rows = slice(7 + b, 39 + b)
                total = parts[0] * right[a][rows, :] + parts[1] * scaled[a, rows, :] + parts[2] * image[a][rows, :]
                out = jnp.where(lane == 9 * a + 3 * b + c, jnp.sum(total), out)
    out_ref[...] = out


def shape(*dims):
    return jax.ShapeDtypeStruct(dims, F32)


STENCIL_SCRATCH = (
    pltpu.VMEM((3, 5, FRAME, COLS), F32),
    pltpu.VMEM((3, 3, FRAME, COLS), F32),
)
BACK_SCRATCH = (pltpu.VMEM((FRAME, COLS), F32),)


def call(body, out_shape, scalars, operands, scratch=(), far=(), planes=(), limit=VMEM, flops=400_000_000):
    operands = [*operands, *planes]
    smem, vmem, hbm = (pl.BlockSpec(memory_space=m) for m in (pltpu.SMEM, pltpu.VMEM, pltpu.HBM))
    outs = out_shape if isinstance(out_shape, tuple) else (out_shape,)
    first, count = len(scalars), len(scalars) + len(operands)
    buffers = [pltpu.VMEM(operands[i].shape, operands[i].dtype) for i in far]
    extra = [*buffers, pltpu.SemaphoreType.DMA((len(buffers),))] if buffers else []

    def whole(*refs):
        ins, results = list(refs[:count]), list(refs[count : count + len(outs)])
        own = refs[count + len(outs) :]
        held, sems, own = own[: len(buffers)], own[len(buffers)] if buffers else None, own[len(extra) :]
        copies = []
        for k, i in enumerate(far):
            copies.append(pltpu.make_async_copy(ins[first + i], held[k], sems.at[k]))
            ins[first + i] = held[k]
        for copy in copies:
            copy.start()
        for copy in copies:
            copy.wait()
        body(*ins, *results, *own)

    spec_in = [smem] * len(scalars) + [hbm if i in far else vmem for i in range(len(operands))]
    spec_out = (vmem,) * len(outs)
    return pl.pallas_call(
        whole,
        out_shape=out_shape,
        in_specs=spec_in,
        out_specs=spec_out if isinstance(out_shape, tuple) else spec_out[0],
        scratch_shapes=[*extra, *scratch],
        compiler_params=pltpu.CompilerParams(vmem_limit_bytes=limit),
        cost_estimate=pl.CostEstimate(flops=flops, bytes_accessed=4_000_000, transcendentals=0),
    )(*scalars, *operands)


def exchange(value):
    return lax.all_to_all(value, GY, 0, 0, tiled=True)


def moved(value, by):
    size = lax.axis_size(GZ)
    return lax.ppermute(value, GZ, [(i, i + by) for i in range(size) if 0 <= i + by < size])


def neighbours(value):
    return moved(value, 2), moved(value, 1), value, moved(value, -1), moved(value, -2)


def with_rows(value):
    size = lax.axis_size(GY)
    below = lax.ppermute(value[24:32], GY, [(i, i + 1) for i in range(size - 1)])
    above = lax.ppermute(value[0:8], GY, [(i + 1, i) for i in range(size - 1)])
    return jnp.concatenate([below, value, above], 0)


def from_all(row):
    size = lax.axis_size(GZ)
    return lax.all_to_all(jnp.broadcast_to(row[None], (size, 1, 128)), GZ, 0, 0, tiled=True)


def factors_of(m0, m1, m2, m3, u0, u1):
    def pair(m0, m1, m2, m3):
        step0 = m0 / m1
        norm1 = m0 - 2.0 * step0 * m1 + step0 * step0 * m2
        ratio = norm1 / m0
        keep = 1.0 + ratio
        curvature = keep * keep * m1 - 2.0 * keep * step0 * m2 + step0 * step0 * m3
        step1 = norm1 / curvature
        return step0 + step1 * keep, -step1 * step0

    (alpha, gamma), back = jax.vjp(pair, m0, m1, m2, m3)
    return (alpha, gamma, *back((u0, u1)))


def factors_kernel(weights_ref, rows, further, grown, out_ref, mixed_ref):
    total = jnp.sum(rows[...], 0)
    lane = lanes((1, 128))
    moments = [jnp.sum(jnp.where(lane == k, total, 0.0), axis=1, keepdims=True) for k in range(6)]
    alpha, gamma, g0, g1, g2, g3 = factors_of(*moments)
    for k in range(27):
        out_ref[k] = weights_ref[k]
    for k, value in enumerate((alpha, gamma, 2.0 * g0, 2.0 * g1, 2.0 * g2, 2.0 * g3, g1)):
        out_ref[27 + k] = value[0, 0]
    mixed_ref[...] = gamma * grown[...] + (2.0 * g3) * further[...]


def local(measured, point_spread, stencil_weights, upstream):
    cells = measured.size * lax.axis_size(GY) * lax.axis_size(GZ)
    weights = stencil_weights.reshape(27)
    table, along_y = jnp.asarray(X_TABLE), jnp.asarray(Y_TABLE)
    measured, upstream = measured[0], upstream[0]
    tile, tiles, three = shape(32, 8, 128), shape(32, 16, 128), shape(32, 24, 128)
    spectral, frame, rows, row = shape(32 * BLOCKS, 128), shape(FRAME, COLS), shape(ROWS, COLS), shape(1, 128)

    first = exchange(
        call(spread_kernel, tiles, [], [table, measured, point_spread], far=(0, 1, 2), limit=ALL_VMEM)
    )
    first, grown = lax.optimization_barrier((first, with_rows(upstream)))

    right_out, bank = call(first_filter_kernel, (three, shape(2, 32 * BLOCKS, 128)), [], [along_y, first])
    right, blurred = call(gather_two_kernel, (frame, frame), [], [table, exchange(right_out)])

    right_parts = neighbours(right)
    image, right_map, image_send, row_b = call(
        image_kernel,
        (frame, rows, tile, row),
        [weights],
        [table, blurred, upstream],
        STENCIL_SCRATCH + BACK_SCRATCH,
        planes=right_parts,
    )
    image_arrived = exchange(image_send)
    image_parts = (moved(image, 1), image, moved(image, -1))
    plane_scratch = (pltpu.VMEM((3, 3, FRAME, COLS), F32),)
    image_map, sums = call(map_kernel, (frame, row), [weights], [row_b], plane_scratch, planes=image_parts)
    further_out, image_spectrum = call(
        second_filter_kernel, (tiles, spectral), [], [along_y, image_arrived, bank, sums]
    )
    further_out, image_map = lax.optimization_barrier((further_out, image_map))
    further_arrived = exchange(further_out)
    map_parts = (moved(image_map, 1), image_map, moved(image_map, -1))
    image_back = call(further_kernel, frame, [weights], [], plane_scratch, planes=map_parts)
    further_arrived, image_back = lax.optimization_barrier((further_arrived, image_back))

    further, row_sum = call(gather_sum_kernel, (frame, row), [], [table, further_arrived, image_back])
    smem, vmem = (pl.BlockSpec(memory_space=m) for m in (pltpu.SMEM, pltpu.VMEM))
    factors, mixed = pl.pallas_call(
        factors_kernel,
        out_shape=(shape(34), frame),
        in_specs=[smem, vmem, vmem, vmem],
        out_specs=(smem, vmem),
        compiler_params=pltpu.CompilerParams(vmem_limit_bytes=VMEM),
    )(weights, from_all(row_sum), further, grown)

    mixed_parts = neighbours(mixed)
    mixed_map, last_send = call(
        last_kernel,
        (rows, tiles),
        [factors],
        [table, image_back, upstream],
        STENCIL_SCRATCH + BACK_SCRATCH,
        planes=mixed_parts,
    )
    operands = [*right_parts[1:4], *image_parts, *mixed_parts[1:4], right_map, image_map, mixed_map]
    scratch = (pltpu.VMEM((3, FRAME, COLS), F32), pltpu.VMEM((3, ROWS, COLS), F32))
    terms = call(correlate_kernel, row, [factors], operands, scratch, far=tuple(range(12)), limit=ALL_VMEM)
    terms = lax.psum(terms, "gz_1")
    last_arrived = exchange(last_send)
    result_out = call(last_filter_kernel, tiles, [factors], [along_y, last_arrived, bank, image_spectrum, terms])
    grad_measured, terms = call(final_kernel, (rows, row), [], [table, exchange(result_out)])
    grad_stencil = lax.psum(terms, "gz_0")[0, :27].reshape(3, 3, 3) / math.sqrt(cells)
    return grad_measured[None], grad_stencil


def solution(mesh):
    groups, planes = mesh.devices.shape
    finer = Mesh(mesh.devices.reshape(groups, 4, planes // 4), (GY, *GZ))
    return jax.shard_map(
        local,
        mesh=finer,
        in_specs=(P(GZ, GY, None), P(GY, None), P(), P(GZ, GY, None)),
        out_specs=(P(GZ, GY, None), P()),
        check_vma=False,
    )
```

```python
import functools
import math

import jax
import jax.numpy as jnp
import ml_dtypes
import numpy as np
from jax import lax
from jax.experimental import pallas as pl
from jax.experimental.pallas import tpu as pltpu
from jax.sharding import Mesh
from jax.sharding import PartitionSpec as P

GY = "gy"
GZ = ("gz_0", "gz_1")
ROWS = 32
COLS = 1024
FRAME = 48
BLOCKS = 9
F32 = jnp.float32
BF16 = jnp.bfloat16
VMEM = 14 * 1024 * 1024
ALL_VMEM = 60 * 1024 * 1024


def split_table(table):
    high = table.astype(ml_dtypes.bfloat16)
    low = (table - high.astype(np.float64)).astype(ml_dtypes.bfloat16)
    return high, low


def x_table():
    part, half, device, i = np.meshgrid(
        np.arange(2), np.arange(2), np.arange(32), np.arange(8), indexing="ij"
    )
    kx = 2 * (16 * (device % 16) + 8 * half + i) + device // 16
    part, kx = part.reshape(-1, 1), kx.reshape(-1, 1)
    x = np.arange(COLS // 2)[None, :]
    angle = 2.0 * np.pi * ((kx * x) % COLS) / COLS
    flip = 1.0 - 2.0 * (x % 2)
    wave = np.where(part == 0, np.cos(angle), -np.sin(angle))
    return np.where((kx == 0) & (part == 1), flip, wave)


def y_tables():
    q = np.arange(32)[:, None]
    s = np.arange(32)[None, :]
    angle = 2.0 * np.pi * ((q * s) % 32) / 32
    first = np.concatenate([np.cos(angle), np.sin(angle)], 0)
    lane = np.arange(128)
    part, half, t = lane // 64, lane // 32 % 2, lane % 32
    turn = 2.0 * np.pi * q * t[None, :] / 1024
    sign = np.where(part == 0, 1.0, -1.0)[None, :]
    turn_cos, turn_sin = np.cos(turn), np.sin(turn) * sign
    angle = 2.0 * np.pi * ((t[:, None] * t[None, :]) % 32) / 32
    pi, po = part[:, None], part[None, :]
    block = np.where(pi == po, np.cos(angle), np.where(pi > po, np.sin(angle), -np.sin(angle)))
    second = np.where(half[:, None] == half[None, :], block, 0.0)
    return first, turn_cos, turn_sin, second


def packed_tables():
    first, turn_cos, turn_sin, second = y_tables()
    first = np.pad(first, ((0, 0), (0, 96)))
    return np.concatenate([second, first, turn_cos, turn_sin], 0).astype(np.float32)


X_TABLE = np.concatenate(split_table(x_table()), 0)
Y_TABLE = packed_tables()
SCALE = 2.0 / (COLS * 1024.0)


def halves(value):
    high = value.astype(BF16)
    return high, (value - high.astype(F32)).astype(BF16)


def dot(left, right):
    return lax.dot_general(left, right, (((1,), (0,)), ((), ())), preferred_element_type=F32)


def dot_nt(left, right):
    return lax.dot_general(left, right, (((1,), (1,)), ((), ())), preferred_element_type=F32)


def swap(value):
    return pltpu.roll(value, 64, 1)


def lanes(shape):
    return lax.broadcasted_iota(jnp.int32, shape, 1)


def sublanes(shape):
    return lax.broadcasted_iota(jnp.int32, shape, 0)


def x_forward(value, table_ref, ready=None):
    left, right = value[:, : COLS // 2], value[:, COLS // 2 :]
    group = lanes((128, 128)) // 32
    outs = []
    for parity, folded in enumerate((left + right, left - right)):
        high, low = halves(folded)
        both = jnp.concatenate([high] * 4 + [low] * 4, 0)
        out = None
        for h in range(4):
            start = 256 * h + 128 * parity
            if ready:
                ready(start)
            first = dot_nt(table_ref[start : start + 128, :], both)
            piece = first[:, :128] + first[:, 128:]
            piece = piece + dot_nt(table_ref[1024 + start : 1152 + start, :], both[:128])
            out = piece if out is None else jnp.where(group == h, piece, out)
        outs.append(out)
    return jnp.concatenate(outs, 0)


def x_inverse(spectra, table_ref):
    turned = [value.T for value in spectra]
    sums = []
    for parity in range(2):
        cols = slice(128 * parity, 128 * parity + 128)
        rows = [jnp.concatenate([v[32 * h : 32 * h + 32, cols] for h in range(4)], 1) for v in turned]
        left = rows[0] if len(rows) == 1 else jnp.concatenate(rows, 0)
        count = left.shape[0]
        high, low = halves(left)
        both = jnp.concatenate([high, low], 0)
        total = None
        for h in range(4):
            start = 256 * h + 128 * parity
            k = slice(128 * h, 128 * h + 128)
            first = dot(both[:, k], table_ref[start : start + 128, :])
            piece = first[:count] + first[count:] + dot(high[:, k], table_ref[1024 + start : 1152 + start, :])
            total = piece if total is None else total + piece
        sums.append(total)
    return jnp.concatenate([sums[0] + sums[1], sums[0] - sums[1]], 1)


class Lateral:
    def __init__(self, table):
        second = table[0:128, :]
        self.second = halves(second)
        self.back = halves(second.T)
        self.first = halves(table[128:192, :][:, 0:32])
        self.cos, self.sin = table[192:224, :], table[224:256, :]
        self.is_first = jnp.where(lax.axis_index(GY) == 0, 1.0, 0.0).astype(F32)
        self.sign = jnp.where(lanes((32, 128)) < 64, 1.0, -1.0)

    def over_s(self, blocks, direction):
        high, low = halves(jnp.concatenate(blocks, 1))
        both = dot(self.first[0], high) + dot(self.first[0], low) + dot(self.first[1], high)
        out = []
        for i in range(len(blocks)):
            cols = slice(128 * i, 128 * i + 128)
            out.append(both[:32, cols] + direction * self.sign * swap(both[32:, cols]))
        return out

    def over_t(self, value, tables):
        high, low = halves(value)
        return dot(high, tables[0]) + dot(low, tables[0]) + dot(high, tables[1])

    def forward(self, ref, offset):
        blocks = [ref[:, offset + i, :] for i in range(8)]
        lane = lanes((32, 128))
        nyquist = (lane >= 64) & (lane < 96)
        blocks.append(jnp.where(lane < 32, swap(blocks[0]), 0.0) * self.is_first)
        blocks[0] = jnp.where(nyquist, blocks[0] * (1.0 - self.is_first), blocks[0])
        blocks = self.over_s(blocks, 1.0)
        blocks = [z * self.cos + swap(z) * self.sin for z in blocks]
        return self.over_t(jnp.concatenate(blocks, 0), self.second)

    def inverse(self, spectrum):
        all_rows = self.over_t(spectrum, self.back)
        blocks = [all_rows[32 * i : 32 * i + 32] for i in range(BLOCKS)]
        blocks = [z * self.cos - swap(z) * self.sin for z in blocks]
        blocks = self.over_s(blocks, -1.0)
        lane = lanes((32, 128))
        nyquist = (lane >= 64) & (lane < 96)
        own = jnp.where(lane // 32 % 2 == 0, SCALE * (1.0 - 0.5 * self.is_first), SCALE)
        blocks[0] = (blocks[0] + jnp.where(nyquist, swap(blocks[8]), 0.0)) * own
        return [blocks[0]] + [z * SCALE for z in blocks[1:8]]

    def weighted_sum(self, value):
        lane, row = lanes(value.shape), sublanes(value.shape)
        weight = jnp.where((row < 32) & (lane // 32 % 2 == 0), 2.0 - self.is_first, 2.0)
        weight = jnp.where(row >= 256, 1.0, weight)
        return jnp.sum(value * weight) * (1.0 / (COLS * 1024.0))


def halo_rows(block):
    lane, row = lanes((32, 128)) % 32, sublanes((32, 128))
    after = jnp.where((lane < 8) & (row < 31), pltpu.roll(block, 31, 0), 0.0)
    before = jnp.where((lane >= 24) & (row > 0), pltpu.roll(block, 1, 0), 0.0)
    return after, before


def product(real, imaginary, value):
    return real * value + imaginary * swap(value)


def conjugate_factors(transfer):
    turned, left = swap(transfer), lanes(transfer.shape) < 64
    return jnp.where(left, transfer, turned), jnp.where(left, turned, -transfer)


def spread_kernel(table_far, measured_far, spread_far, out_ref, table_ref, rows_ref, sems):
    copies = [pltpu.make_async_copy(ref, rows_ref.at[f], sems.at[16 + f]) for f, ref in enumerate((measured_far, spread_far))]
    pieces = {}
    for parity in range(2):
        for h in range(4):
            start = 256 * h + 128 * parity
            pieces[start] = []
            for low in range(2):
                part = pl.ds(1024 * low + start, 128)
                sem = sems.at[8 * low + 4 * parity + h]
                pieces[start].append(pltpu.make_async_copy(table_far.at[part, :], table_ref.at[part, :], sem))
    for copy in copies:
        copy.start()
    for pair in pieces.values():
        for copy in pair:
            copy.start()

    def ready(start):
        for copy in pieces[start]:
            copy.wait()

    copies[0].wait()
    out_ref[:, 0:8, :] = x_forward(rows_ref[0], table_ref, ready).reshape(32, 8, 128)
    copies[1].wait()
    out_ref[:, 8:16, :] = x_forward(rows_ref[1], table_ref).reshape(32, 8, 128)


def first_filter_kernel(table, arrived, out_ref, bank_ref):
    lateral = Lateral(table)
    transfer = lateral.forward(arrived, 8)
    observed = lateral.forward(arrived, 0)
    real, imaginary = conjugate_factors(transfer)
    power = real * real + imaginary * imaginary
    spectrum = product(real, imaginary, observed)
    right = lateral.inverse(spectrum)
    image = lateral.inverse(spectrum * power)
    for i in range(8):
        out_ref[:, i, :] = right[i]
        out_ref[:, 8 + i, :] = image[i]
        after, before = halo_rows(right[i])
        image_after, image_before = halo_rows(image[i])
        image_after, image_before = pltpu.roll(image_after, 8, 1), pltpu.roll(image_before, 120, 1)
        out_ref[:, 16 + i, :] = after + before + image_after + image_before
    bank_ref[0] = transfer
    bank_ref[1] = spectrum


def second_filter_kernel(table, arrived, bank_ref, out_ref, image_ref, row_ref):
    lateral = Lateral(table)
    real, imaginary = conjugate_factors(bank_ref[0])
    power = real * real + imaginary * imaginary
    image = power * bank_ref[1] + lateral.forward(arrived, 0)
    filtered = power * image
    blocks = lateral.inverse(filtered)
    for i in range(8):
        out_ref[:, i, :] = blocks[i]
        after, before = halo_rows(blocks[i])
        out_ref[:, 8 + i, :] = after + before
    image_ref[...] = image
    row_ref[...] = jnp.where(lanes((1, 128)) == 3, lateral.weighted_sum(image * filtered), 0.0)


def last_filter_kernel(
    factors_ref, table, arrived, bank_ref, image_ref, terms, out_ref
):
    lateral = Lateral(table)
    factor_ref = [factors_ref[27 + k] for k in range(6)]
    real, imaginary = conjugate_factors(bank_ref[0])
    power = real * real + imaginary * imaginary
    image = image_ref[...]
    total = factor_ref[4] * image + factor_ref[5] * (power * image) + lateral.forward(arrived, 8)
    total = power * total + factor_ref[2] * bank_ref[1] + factor_ref[3] * image
    total = total + lateral.forward(arrived, 0)
    blocks = lateral.inverse(product(real, -imaginary, total))
    for i in range(8):
        out_ref[:, i, :] = blocks[i]
        out_ref[:, 8 + i, :] = jnp.broadcast_to(terms[...], (32, 128))


def gather_two_kernel(table_ref, arrived, right_ref, image_ref):
    tiles = [arrived[:, 8 * f : 8 * f + 8, :].reshape(256, 128) for f in range(3)]
    value = x_inverse(tiles, table_ref)
    right_ref[0:8, :] = value[88:96]
    right_ref[8:40, :] = value[0:32]
    right_ref[40:48, :] = value[64:72]
    image_ref[0:8, :] = value[80:88]
    image_ref[8:40, :] = value[32:64]
    image_ref[40:48, :] = value[72:80]


def gather_sum_kernel(table_ref, arrived, base, out_ref, row_ref):
    row = pltpu.roll(jnp.broadcast_to(jnp.sum(arrived[:, 8, :], 0, keepdims=True), (8, 128)), 120, 1)
    row_ref[...] = jnp.where(lanes((1, 128)) < 6, row[0:1], 0.0)
    tiles = [arrived[:, 8 * f : 8 * f + 8, :].reshape(256, 128) for f in range(2)]
    value = x_inverse(tiles, table_ref)
    out_ref[0:8, :] = base[0:8, :] + value[56:64]
    out_ref[8:40, :] = base[8:40, :] + value[0:32]
    out_ref[40:48, :] = base[40:48, :] + value[32:40]


def final_kernel(table_ref, arrived, out_ref, row_ref):
    out_ref[...] = x_inverse([arrived[:, 0:8, :].reshape(256, 128)], table_ref)
    row_ref[...] = jnp.sum(arrived[:, 8, :], 0, keepdims=True)


def shifted_columns(value):
    column = lanes(value.shape)
    left = jnp.where(column >= 1, pltpu.roll(value, 1, 1), 0.0)
    right = jnp.where(column < COLS - 1, pltpu.roll(value, COLS - 1, 1), 0.0)
    return left, right


def stencil_sum(weight, source, start, cols):
    total = None
    for b in range(3):
        part = None
        for a in range(3):
            for c in range(3):
                term = weight(a, b, c) * source[c, start + a, :, cols]
                part = term if part is None else part + term
        if b == 0:
            part = pltpu.roll(part, 1, 0)
        elif b == 2:
            part = pltpu.roll(part, FRAME - 1, 0)
        total = part if total is None else total + part
    return total


def load_planes(parts, source):
    for p, ref in enumerate(parts):
        value = ref[...]
        source[1, p] = value
        source[0, p], source[2, p] = shifted_columns(value)


def row_bounds():
    device, plane, planes = lax.axis_index(GY), lax.axis_index(GZ), lax.axis_size(GZ)
    lowest = jnp.where(device > 0, 0, 8)
    highest = jnp.where(device < 31, FRAME, 40)

    def highest_at(here):
        return jnp.where((here >= 0) & (here < planes), highest, 0)

    return sublanes((FRAME, 128)), lowest, highest, lambda p: highest_at(plane + p)


def weight_of(weights_ref):
    return lambda a, b, c: weights_ref[9 * a + 3 * b + c]


def flipped_of(weights_ref):
    return lambda a, b, c: weights_ref[26 - 9 * a - 3 * b - c]


def apply_stencils(weights_ref, source, middle, back_ref):
    row, lowest, highest, highest_at = row_bounds()
    for p in range(3):
        valid = (row >= lowest) & (row < highest_at(p - 1))
        for k in range(8):
            cols = slice(128 * k, 128 * k + 128)
            value = stencil_sum(weight_of(weights_ref), source, p, cols)
            middle[1, p, :, cols] = jnp.where(valid, value, 0.0)
    for p in range(3):
        middle[0, p], middle[2, p] = shifted_columns(middle[1, p])
    inside = (row >= lowest) & (row < highest)
    for k in range(8):
        cols = slice(128 * k, 128 * k + 128)
        back_ref[:, cols] = jnp.where(inside, stencil_sum(flipped_of(weights_ref), middle, 0, cols), 0.0)


def row_of(values):
    lane = lanes((1, 128))
    out = jnp.zeros((1, 128), F32)
    for k, value in values:
        out = jnp.where(lane == k, jnp.sum(value), out)
    return out


def image_kernel(weights, table, blurred, upstream, u2, u1, o, d1, d2, image_ref, mapped_ref, out_ref, row_ref, *scratch):
    source, middle, back = scratch
    load_planes((u2, u1, o, d1, d2), source)
    apply_stencils(weights, source, middle, back)
    out_ref[...] = x_forward(back[8:40, :], table).reshape(32, 8, 128)
    mapped_ref[...] = middle[1, 1, 8:40, :]
    image_ref[...] = blurred[...] + back[...]
    b, ab, u = source[1, 2, 8:40, :], image_ref[8:40, :], upstream[...]
    row_ref[...] = row_of(((0, b * b), (1, b * ab), (2, ab * ab), (4, u * b), (5, u * ab)))


def map_kernel(weights, row_b, row_f, further, u1, o, d1, mapped_ref, out_ref, source):
    load_planes((u1, o, d1), source)
    row, lowest, highest, _ = row_bounds()
    inside = (row >= lowest) & (row < highest)
    for k in range(8):
        cols = slice(128 * k, 128 * k + 128)
        mapped_ref[:, cols] = jnp.where(inside, stencil_sum(weight_of(weights), source, 0, cols), 0.0)
    mapped = mapped_ref[8:40, :]
    sums = row_b[...] + row_f[...] + row_of(((3, mapped * mapped),))
    out_ref[...] = further[...]
    out_ref[:, 8, :] = further[:, 8, :] + pltpu.roll(jnp.broadcast_to(sums, (32, 128)), 8, 1)


def further_kernel(weights, u1, o, d1, back_ref, middle):
    load_planes((u1, o, d1), middle)
    row, lowest, highest, _ = row_bounds()
    inside = (row >= lowest) & (row < highest)
    for k in range(8):
        cols = slice(128 * k, 128 * k + 128)
        back_ref[:, cols] = jnp.where(inside, stencil_sum(flipped_of(weights), middle, 0, cols), 0.0)


def last_kernel(
    weights, table, image_back, upstream, u2, u1, o, d1, d2, mapped_ref, out_ref, source, middle, back
):
    load_planes((u2, u1, o, d1, d2), source)
    apply_stencils(weights, source, middle, back)
    mapped_ref[...] = middle[1, 1, 8:40, :]
    alpha, gamma, twice_g2, twice_g3 = weights[27], weights[28], weights[31], weights[32]
    u, again = upstream[...], image_back[8:40, :]
    first = alpha * u + twice_g2 * again + back[8:40, :]
    second = gamma * u + twice_g3 * again
    out_ref[:, 0:8, :] = x_forward(first, table).reshape(32, 8, 128)
    out_ref[:, 8:16, :] = x_forward(second, table).reshape(32, 8, 128)


def correlate_kernel(factor_ref, *refs):
    out_ref, scaled, mapped = refs[-3:]
    right, image, mixed = refs[0:3], refs[3:6], refs[6:9]
    right_map, image_map, mixed_map = refs[9:12]
    g1, twice_g2, twice_g3 = (factor_ref[k] for k in (33, 31, 32))
    for p in range(3):
        scaled[p] = mixed[p][...] + g1 * right[p][...] + twice_g2 * image[p][...]
    mapped[0] = mixed_map[...] + g1 * right_map[...] + twice_g2 * image_map[8:40, :]
    mapped[1] = right_map[...]
    mapped[2] = twice_g3 * image_map[8:40, :]
    lane = lanes((1, 128))
    out = jnp.zeros((1, 128), F32)
    column = lanes((ROWS, COLS))
    left_edge, right_edge = column < COLS - 1, column >= 1
    for c in range(3):
        parts = []
        for k in range(3):
            value = mapped[k]
            if c == 0:
                value = jnp.where(left_edge, pltpu.roll(value, COLS - 1, 1), 0.0)
            elif c == 2:
                value = jnp.where(right_edge, pltpu.roll(value, 1, 1), 0.0)
            parts.append(value)
        for a in range(3):
            for b in range(3):
                rows = slice(7 + b, 39 + b)
                total = parts[0] * right[a][rows, :] + parts[1] * scaled[a, rows, :] + parts[2] * image[a][rows, :]
                out = jnp.where(lane == 9 * a + 3 * b + c, jnp.sum(total), out)
    out_ref[...] = out


def shape(*dims):
    return jax.ShapeDtypeStruct(dims, F32)


STENCIL_SCRATCH = (
    pltpu.VMEM((3, 5, FRAME, COLS), F32),
    pltpu.VMEM((3, 3, FRAME, COLS), F32),
)
BACK_SCRATCH = (pltpu.VMEM((FRAME, COLS), F32),)


def call(body, out_shape, scalars, operands, scratch=(), far=(), planes=(), limit=VMEM, flops=400_000_000):
    operands = [*operands, *planes]
    smem, vmem, hbm = (pl.BlockSpec(memory_space=m) for m in (pltpu.SMEM, pltpu.VMEM, pltpu.HBM))
    outs = out_shape if isinstance(out_shape, tuple) else (out_shape,)
    first, count = len(scalars), len(scalars) + len(operands)
    buffers = [pltpu.VMEM(operands[i].shape, operands[i].dtype) for i in far]
    extra = [*buffers, pltpu.SemaphoreType.DMA((len(buffers),))] if buffers else []

    def whole(*refs):
        ins, results = list(refs[:count]), list(refs[count : count + len(outs)])
        own = refs[count + len(outs) :]
        held, sems, own = own[: len(buffers)], own[len(buffers)] if buffers else None, own[len(extra) :]
        copies = []
        for k, i in enumerate(far):
            copies.append(pltpu.make_async_copy(ins[first + i], held[k], sems.at[k]))
            ins[first + i] = held[k]
        for copy in copies:
            copy.start()
        for copy in copies:
            copy.wait()
        body(*ins, *results, *own)

    spec_in = [smem] * len(scalars) + [hbm if i in far else vmem for i in range(len(operands))]
    spec_out = (vmem,) * len(outs)
    return pl.pallas_call(
        whole,
        out_shape=out_shape,
        in_specs=spec_in,
        out_specs=spec_out if isinstance(out_shape, tuple) else spec_out[0],
        scratch_shapes=[*extra, *scratch],
        compiler_params=pltpu.CompilerParams(vmem_limit_bytes=limit),
        cost_estimate=pl.CostEstimate(flops=flops, bytes_accessed=4_000_000, transcendentals=0),
    )(*scalars, *operands)


def exchange(value):
    return lax.all_to_all(value, GY, 0, 0, tiled=True)


def moved(value, by):
    size = lax.axis_size(GZ)
    return lax.ppermute(value, GZ, [(i, i + by) for i in range(size) if 0 <= i + by < size])


def neighbours(value):
    return moved(value, 2), moved(value, 1), value, moved(value, -1), moved(value, -2)


def with_rows(value):
    size = lax.axis_size(GY)
    below = lax.ppermute(value[24:32], GY, [(i, i + 1) for i in range(size - 1)])
    above = lax.ppermute(value[0:8], GY, [(i + 1, i) for i in range(size - 1)])
    return jnp.concatenate([below, value, above], 0)


def from_all(row):
    size = lax.axis_size(GZ)
    return lax.all_to_all(jnp.broadcast_to(row[None], (size, 1, 128)), GZ, 0, 0, tiled=True)


def factors_of(m0, m1, m2, m3, u0, u1):
    def pair(m0, m1, m2, m3):
        step0 = m0 / m1
        norm1 = m0 - 2.0 * step0 * m1 + step0 * step0 * m2
        ratio = norm1 / m0
        keep = 1.0 + ratio
        curvature = keep * keep * m1 - 2.0 * keep * step0 * m2 + step0 * step0 * m3
        step1 = norm1 / curvature
        return step0 + step1 * keep, -step1 * step0

    (alpha, gamma), back = jax.vjp(pair, m0, m1, m2, m3)
    return (alpha, gamma, *back((u0, u1)))


def factors_kernel(weights_ref, rows, further, grown, out_ref, mixed_ref):
    total = jnp.sum(rows[...], 0)
    lane = lanes((1, 128))
    moments = [jnp.sum(jnp.where(lane == k, total, 0.0), axis=1, keepdims=True) for k in range(6)]
    alpha, gamma, g0, g1, g2, g3 = factors_of(*moments)
    for k in range(27):
        out_ref[k] = weights_ref[k]
    for k, value in enumerate((alpha, gamma, 2.0 * g0, 2.0 * g1, 2.0 * g2, 2.0 * g3, g1)):
        out_ref[27 + k] = value[0, 0]
    mixed_ref[...] = gamma * grown[...] + (2.0 * g3) * further[...]


def local(measured, point_spread, stencil_weights, upstream):
    cells = measured.size * lax.axis_size(GY) * lax.axis_size(GZ)
    weights = stencil_weights.reshape(27)
    table, along_y = jnp.asarray(X_TABLE), jnp.asarray(Y_TABLE)
    measured, upstream = measured[0], upstream[0]
    tile, tiles, three = shape(32, 8, 128), shape(32, 16, 128), shape(32, 24, 128)
    spectral, frame, rows, row = shape(32 * BLOCKS, 128), shape(FRAME, COLS), shape(ROWS, COLS), shape(1, 128)

    smem, vmem, hbm = (pl.BlockSpec(memory_space=m) for m in (pltpu.SMEM, pltpu.VMEM, pltpu.HBM))
    sent = pl.pallas_call(
        spread_kernel,
        out_shape=tiles,
        in_specs=[hbm] * 3,
        out_specs=vmem,
        scratch_shapes=[
            pltpu.VMEM(table.shape, BF16),
            pltpu.VMEM((2, ROWS, COLS), F32),
            pltpu.SemaphoreType.DMA((18,)),
        ],
        compiler_params=pltpu.CompilerParams(vmem_limit_bytes=ALL_VMEM),
    )(table, measured, point_spread)
    first = exchange(sent)
    first, grown = lax.optimization_barrier((first, with_rows(upstream)))

    right_out, bank = call(first_filter_kernel, (three, shape(2, 32 * BLOCKS, 128)), [], [along_y, first])
    right, blurred = call(gather_two_kernel, (frame, frame), [], [table, exchange(right_out)])

    right_parts = neighbours(right)
    image, right_map, image_send, row_b = call(
        image_kernel,
        (frame, rows, tile, row),
        [weights],
        [table, blurred, upstream],
        STENCIL_SCRATCH + BACK_SCRATCH,
        planes=right_parts,
    )
    image_arrived = exchange(image_send)
    image_parts = (moved(image, 1), image, moved(image, -1))
    plane_scratch = (pltpu.VMEM((3, 3, FRAME, COLS), F32),)
    further_out, image_spectrum, row_f = call(
        second_filter_kernel, (tiles, spectral, row), [], [along_y, image_arrived, bank]
    )
    image_map, further_out = call(
        map_kernel, (frame, tiles), [weights], [row_b, row_f, further_out], plane_scratch, planes=image_parts
    )
    further_arrived = exchange(further_out)
    map_parts = (moved(image_map, 1), image_map, moved(image_map, -1))
    image_back = call(further_kernel, frame, [weights], [], plane_scratch, planes=map_parts)
    further_arrived, image_back = lax.optimization_barrier((further_arrived, image_back))

    further, row_sum = call(gather_sum_kernel, (frame, row), [], [table, further_arrived, image_back])
    factors, mixed = pl.pallas_call(
        factors_kernel,
        out_shape=(shape(34), frame),
        in_specs=[smem, vmem, vmem, vmem],
        out_specs=(smem, vmem),
        compiler_params=pltpu.CompilerParams(vmem_limit_bytes=VMEM),
    )(weights, from_all(row_sum), further, grown)

    mixed_parts = neighbours(mixed)
    mixed_map, last_send = call(
        last_kernel,
        (rows, tiles),
        [factors],
        [table, image_back, upstream],
        STENCIL_SCRATCH + BACK_SCRATCH,
        planes=mixed_parts,
    )
    operands = [*right_parts[1:4], *image_parts, *mixed_parts[1:4], right_map, image_map, mixed_map]
    scratch = (pltpu.VMEM((3, FRAME, COLS), F32), pltpu.VMEM((3, ROWS, COLS), F32))
    terms = call(correlate_kernel, row, [factors], operands, scratch, far=tuple(range(12)), limit=ALL_VMEM)
    terms = lax.psum(terms, "gz_1")
    last_arrived = exchange(last_send)
    result_out = call(last_filter_kernel, tiles, [factors], [along_y, last_arrived, bank, image_spectrum, terms])
    grad_measured, terms = call(final_kernel, (rows, row), [], [table, exchange(result_out)])
    grad_stencil = lax.psum(terms, "gz_0")[0, :27].reshape(3, 3, 3) / math.sqrt(cells)
    return grad_measured[None], grad_stencil


def solution(mesh):
    groups, planes = mesh.devices.shape
    finer = Mesh(mesh.devices.reshape(groups, 4, planes // 4), (GY, *GZ))
    return jax.shard_map(
        local,
        mesh=finer,
        in_specs=(P(GZ, GY, None), P(GY, None), P(), P(GZ, GY, None)),
        out_specs=(P(GZ, GY, None), P()),
        check_vma=False,
    )
```

```python
import functools
import math

import jax
import jax.numpy as jnp
import ml_dtypes
import numpy as np
from jax import lax
from jax.experimental import pallas as pl
from jax.experimental.pallas import tpu as pltpu
from jax.sharding import Mesh
from jax.sharding import PartitionSpec as P

GY = "gy"
GZ = ("gz_0", "gz_1")
ROWS = 32
COLS = 1024
FRAME = 48
BLOCKS = 9
F32 = jnp.float32
BF16 = jnp.bfloat16
VMEM = 14 * 1024 * 1024
ALL_VMEM = 60 * 1024 * 1024


def split_table(table):
    high = table.astype(ml_dtypes.bfloat16)
    low = (table - high.astype(np.float64)).astype(ml_dtypes.bfloat16)
    return high, low


def x_table():
    part, half, device, i = np.meshgrid(
        np.arange(2), np.arange(2), np.arange(32), np.arange(8), indexing="ij"
    )
    kx = 2 * (16 * (device % 16) + 8 * half + i) + device // 16
    part, kx = part.reshape(-1, 1), kx.reshape(-1, 1)
    x = np.arange(COLS // 2)[None, :]
    angle = 2.0 * np.pi * ((kx * x) % COLS) / COLS
    flip = 1.0 - 2.0 * (x % 2)
    wave = np.where(part == 0, np.cos(angle), -np.sin(angle))
    return np.where((kx == 0) & (part == 1), flip, wave)


def y_tables():
    q = np.arange(32)[:, None]
    s = np.arange(32)[None, :]
    angle = 2.0 * np.pi * ((q * s) % 32) / 32
    first = np.concatenate([np.cos(angle), np.sin(angle)], 0)
    lane = np.arange(128)
    part, half, t = lane // 64, lane // 32 % 2, lane % 32
    turn = 2.0 * np.pi * q * t[None, :] / 1024
    sign = np.where(part == 0, 1.0, -1.0)[None, :]
    turn_cos, turn_sin = np.cos(turn), np.sin(turn) * sign
    angle = 2.0 * np.pi * ((t[:, None] * t[None, :]) % 32) / 32
    pi, po = part[:, None], part[None, :]
    block = np.where(pi == po, np.cos(angle), np.where(pi > po, np.sin(angle), -np.sin(angle)))
    second = np.where(half[:, None] == half[None, :], block, 0.0)
    return first, turn_cos, turn_sin, second


def packed_tables():
    first, turn_cos, turn_sin, second = y_tables()
    first = np.pad(first, ((0, 0), (0, 96)))
    return np.concatenate([second, first, turn_cos, turn_sin], 0).astype(np.float32)


X_TABLE = np.concatenate(split_table(x_table()), 0)
Y_TABLE = packed_tables()
SCALE = 2.0 / (COLS * 1024.0)


def halves(value):
    high = value.astype(BF16)
    return high, (value - high.astype(F32)).astype(BF16)


def dot(left, right):
    return lax.dot_general(left, right, (((1,), (0,)), ((), ())), preferred_element_type=F32)


def dot_nt(left, right):
    return lax.dot_general(left, right, (((1,), (1,)), ((), ())), preferred_element_type=F32)


def swap(value):
    return pltpu.roll(value, 64, 1)


def lanes(shape):
    return lax.broadcasted_iota(jnp.int32, shape, 1)


def sublanes(shape):
    return lax.broadcasted_iota(jnp.int32, shape, 0)


def x_forward(value, table_ref):
    left, right = value[:, : COLS // 2], value[:, COLS // 2 :]
    group = lanes((128, 128)) // 32
    outs = []
    for parity, folded in enumerate((left + right, left - right)):
        high, low = halves(folded)
        both = jnp.concatenate([high] * 4 + [low] * 4, 0)
        out = None
        for h in range(4):
            start = 256 * h + 128 * parity
            first = dot_nt(table_ref[start : start + 128, :], both)
            piece = first[:, :128] + first[:, 128:]
            piece = piece + dot_nt(table_ref[1024 + start : 1152 + start, :], both[:128])
            out = piece if out is None else jnp.where(group == h, piece, out)
        outs.append(out)
    return jnp.concatenate(outs, 0)


def x_inverse(spectra, table_ref):
    turned = [value.T for value in spectra]
    sums = []
    for parity in range(2):
        cols = slice(128 * parity, 128 * parity + 128)
        rows = [jnp.concatenate([v[32 * h : 32 * h + 32, cols] for h in range(4)], 1) for v in turned]
        left = rows[0] if len(rows) == 1 else jnp.concatenate(rows, 0)
        count = left.shape[0]
        high, low = halves(left)
        both = jnp.concatenate([high, low], 0)
        total = None
        for h in range(4):
            start = 256 * h + 128 * parity
            k = slice(128 * h, 128 * h + 128)
            first = dot(both[:, k], table_ref[start : start + 128, :])
            piece = first[:count] + first[count:] + dot(high[:, k], table_ref[1024 + start : 1152 + start, :])
            total = piece if total is None else total + piece
        sums.append(total)
    return jnp.concatenate([sums[0] + sums[1], sums[0] - sums[1]], 1)


class Lateral:
    def __init__(self, table):
        second = table[0:128, :]
        self.second = halves(second)
        self.back = halves(second.T)
        self.first = halves(table[128:192, :][:, 0:32])
        self.cos, self.sin = table[192:224, :], table[224:256, :]
        self.is_first = jnp.where(lax.axis_index(GY) == 0, 1.0, 0.0).astype(F32)
        self.sign = jnp.where(lanes((32, 128)) < 64, 1.0, -1.0)

    def over_s(self, blocks, direction):
        high, low = halves(jnp.concatenate(blocks, 1))
        both = dot(self.first[0], high) + dot(self.first[0], low) + dot(self.first[1], high)
        out = []
        for i in range(len(blocks)):
            cols = slice(128 * i, 128 * i + 128)
            out.append(both[:32, cols] + direction * self.sign * swap(both[32:, cols]))
        return out

    def over_t(self, value, tables):
        high, low = halves(value)
        return dot(high, tables[0]) + dot(low, tables[0]) + dot(high, tables[1])

    def forward(self, ref, offset):
        blocks = [ref[:, offset + i, :] for i in range(8)]
        lane = lanes((32, 128))
        nyquist = (lane >= 64) & (lane < 96)
        blocks.append(jnp.where(lane < 32, swap(blocks[0]), 0.0) * self.is_first)
        blocks[0] = jnp.where(nyquist, blocks[0] * (1.0 - self.is_first), blocks[0])
        blocks = self.over_s(blocks, 1.0)
        blocks = [z * self.cos + swap(z) * self.sin for z in blocks]
        return self.over_t(jnp.concatenate(blocks, 0), self.second)

    def inverse(self, spectrum):
        all_rows = self.over_t(spectrum, self.back)
        blocks = [all_rows[32 * i : 32 * i + 32] for i in range(BLOCKS)]
        blocks = [z * self.cos - swap(z) * self.sin for z in blocks]
        blocks = self.over_s(blocks, -1.0)
        lane = lanes((32, 128))
        nyquist = (lane >= 64) & (lane < 96)
        own = jnp.where(lane // 32 % 2 == 0, SCALE * (1.0 - 0.5 * self.is_first), SCALE)
        blocks[0] = (blocks[0] + jnp.where(nyquist, swap(blocks[8]), 0.0)) * own
        return [blocks[0]] + [z * SCALE for z in blocks[1:8]]

    def weighted_sum(self, value):
        lane, row = lanes(value.shape), sublanes(value.shape)
        weight = jnp.where((row < 32) & (lane // 32 % 2 == 0), 2.0 - self.is_first, 2.0)
        weight = jnp.where(row >= 256, 1.0, weight)
        return jnp.sum(value * weight) * (1.0 / (COLS * 1024.0))


def halo_rows(block):
    lane, row = lanes((32, 128)) % 32, sublanes((32, 128))
    after = jnp.where((lane < 8) & (row < 31), pltpu.roll(block, 31, 0), 0.0)
    before = jnp.where((lane >= 24) & (row > 0), pltpu.roll(block, 1, 0), 0.0)
    return after, before


def product(real, imaginary, value):
    return real * value + imaginary * swap(value)


def conjugate_factors(transfer):
    turned, left = swap(transfer), lanes(transfer.shape) < 64
    return jnp.where(left, transfer, turned), jnp.where(left, turned, -transfer)


def spread_kernel(table_ref, measured, point_spread, out_ref):
    for f, ref in enumerate((measured, point_spread)):
        out_ref[:, 8 * f : 8 * f + 8, :] = x_forward(ref[...], table_ref).reshape(32, 8, 128)


def first_filter_kernel(table, arrived, out_ref, bank_ref):
    lateral = Lateral(table)
    transfer = lateral.forward(arrived, 8)
    observed = lateral.forward(arrived, 0)
    real, imaginary = conjugate_factors(transfer)
    power = real * real + imaginary * imaginary
    spectrum = product(real, imaginary, observed)
    right = lateral.inverse(spectrum)
    image = lateral.inverse(spectrum * power)
    for i in range(8):
        out_ref[:, i, :] = right[i]
        out_ref[:, 8 + i, :] = image[i]
        after, before = halo_rows(right[i])
        image_after, image_before = halo_rows(image[i])
        image_after, image_before = pltpu.roll(image_after, 8, 1), pltpu.roll(image_before, 120, 1)
        out_ref[:, 16 + i, :] = after + before + image_after + image_before
    bank_ref[0] = transfer
    bank_ref[1] = spectrum


def second_filter_kernel(table, arrived, bank_ref, out_ref, image_ref, row_ref):
    lateral = Lateral(table)
    real, imaginary = conjugate_factors(bank_ref[0])
    power = real * real + imaginary * imaginary
    image = power * bank_ref[1] + lateral.forward(arrived, 0)
    filtered = power * image
    blocks = lateral.inverse(filtered)
    for i in range(8):
        out_ref[:, i, :] = blocks[i]
        after, before = halo_rows(blocks[i])
        out_ref[:, 8 + i, :] = after + before
    image_ref[...] = image
    row_ref[...] = jnp.where(lanes((1, 128)) == 3, lateral.weighted_sum(image * filtered), 0.0)


def last_filter_kernel(
    factors_ref, table, arrived, bank_ref, image_ref, terms, out_ref
):
    lateral = Lateral(table)
    factor_ref = [factors_ref[27 + k] for k in range(6)]
    real, imaginary = conjugate_factors(bank_ref[0])
    power = real * real + imaginary * imaginary
    image = image_ref[...]
    total = factor_ref[4] * image + factor_ref[5] * (power * image) + lateral.forward(arrived, 8)
    total = power * total + factor_ref[2] * bank_ref[1] + factor_ref[3] * image
    total = total + lateral.forward(arrived, 0)
    blocks = lateral.inverse(product(real, -imaginary, total))
    for i in range(8):
        out_ref[:, i, :] = blocks[i]
        out_ref[:, 8 + i, :] = jnp.broadcast_to(terms[...], (32, 128))


def gather_two_kernel(table_ref, arrived, right_ref, image_ref):
    tiles = [arrived[:, 8 * f : 8 * f + 8, :].reshape(256, 128) for f in range(3)]
    value = x_inverse(tiles, table_ref)
    right_ref[0:8, :] = value[88:96]
    right_ref[8:40, :] = value[0:32]
    right_ref[40:48, :] = value[64:72]
    image_ref[0:8, :] = value[80:88]
    image_ref[8:40, :] = value[32:64]
    image_ref[40:48, :] = value[72:80]


def gather_sum_kernel(table_ref, arrived, base, out_ref, row_ref):
    row = pltpu.roll(jnp.broadcast_to(jnp.sum(arrived[:, 8, :], 0, keepdims=True), (8, 128)), 120, 1)
    row_ref[...] = jnp.where(lanes((1, 128)) < 6, row[0:1], 0.0)
    tiles = [arrived[:, 8 * f : 8 * f + 8, :].reshape(256, 128) for f in range(2)]
    value = x_inverse(tiles, table_ref)
    out_ref[0:8, :] = base[0:8, :] + value[56:64]
    out_ref[8:40, :] = base[8:40, :] + value[0:32]
    out_ref[40:48, :] = base[40:48, :] + value[32:40]


def final_kernel(table_ref, arrived, out_ref, row_ref):
    out_ref[...] = x_inverse([arrived[:, 0:8, :].reshape(256, 128)], table_ref)
    row_ref[...] = jnp.sum(arrived[:, 8, :], 0, keepdims=True)


def shifted_columns(value):
    column = lanes(value.shape)
    left = jnp.where(column >= 1, pltpu.roll(value, 1, 1), 0.0)
    right = jnp.where(column < COLS - 1, pltpu.roll(value, COLS - 1, 1), 0.0)
    return left, right


def stencil_sum(weight, source, start, cols):
    total = None
    for b in range(3):
        part = None
        for a in range(3):
            for c in range(3):
                term = weight(a, b, c) * source[c, start + a, :, cols]
                part = term if part is None else part + term
        if b == 0:
            part = pltpu.roll(part, 1, 0)
        elif b == 2:
            part = pltpu.roll(part, FRAME - 1, 0)
        total = part if total is None else total + part
    return total


def load_planes(parts, source):
    for p, ref in enumerate(parts):
        value = ref[...]
        source[1, p] = value
        source[0, p], source[2, p] = shifted_columns(value)


def row_bounds():
    device, plane, planes = lax.axis_index(GY), lax.axis_index(GZ), lax.axis_size(GZ)
    lowest = jnp.where(device > 0, 0, 8)
    highest = jnp.where(device < 31, FRAME, 40)

    def highest_at(here):
        return jnp.where((here >= 0) & (here < planes), highest, 0)

    return sublanes((FRAME, 128)), lowest, highest, lambda p: highest_at(plane + p)


def weight_of(weights_ref):
    return lambda a, b, c: weights_ref[9 * a + 3 * b + c]


def flipped_of(weights_ref):
    return lambda a, b, c: weights_ref[26 - 9 * a - 3 * b - c]


def apply_stencils(weights_ref, source, middle, back_ref):
    row, lowest, highest, highest_at = row_bounds()
    for p in range(3):
        valid = (row >= lowest) & (row < highest_at(p - 1))
        for k in range(8):
            cols = slice(128 * k, 128 * k + 128)
            value = stencil_sum(weight_of(weights_ref), source, p, cols)
            middle[1, p, :, cols] = jnp.where(valid, value, 0.0)
    for p in range(3):
        middle[0, p], middle[2, p] = shifted_columns(middle[1, p])
    inside = (row >= lowest) & (row < highest)
    for k in range(8):
        cols = slice(128 * k, 128 * k + 128)
        back_ref[:, cols] = jnp.where(inside, stencil_sum(flipped_of(weights_ref), middle, 0, cols), 0.0)


def row_of(values):
    lane = lanes((1, 128))
    out = jnp.zeros((1, 128), F32)
    for k, value in values:
        out = jnp.where(lane == k, jnp.sum(value), out)
    return out


def image_kernel(weights, table, blurred, upstream, u2, u1, o, d1, d2, image_ref, mapped_ref, out_ref, row_ref, *scratch):
    source, middle, back = scratch
    load_planes((u2, u1, o, d1, d2), source)
    apply_stencils(weights, source, middle, back)
    out_ref[...] = x_forward(back[8:40, :], table).reshape(32, 8, 128)
    mapped_ref[...] = middle[1, 1, 8:40, :]
    image_ref[...] = blurred[...] + back[...]
    b, ab, u = source[1, 2, 8:40, :], image_ref[8:40, :], upstream[...]
    row_ref[...] = row_of(((0, b * b), (1, b * ab), (2, ab * ab), (4, u * b), (5, u * ab)))


def map_kernel(weights, row_b, row_f, further, u1, o, d1, mapped_ref, out_ref, source):
    load_planes((u1, o, d1), source)
    row, lowest, highest, _ = row_bounds()
    inside = (row >= lowest) & (row < highest)
    for k in range(8):
        cols = slice(128 * k, 128 * k + 128)
        mapped_ref[:, cols] = jnp.where(inside, stencil_sum(weight_of(weights), source, 0, cols), 0.0)
    mapped = mapped_ref[8:40, :]
    sums = row_b[...] + row_f[...] + row_of(((3, mapped * mapped),))
    out_ref[...] = further[...]
    out_ref[:, 8, :] = further[:, 8, :] + pltpu.roll(jnp.broadcast_to(sums, (32, 128)), 8, 1)


def further_kernel(weights, u1, o, d1, back_ref, middle):
    load_planes((u1, o, d1), middle)
    row, lowest, highest, _ = row_bounds()
    inside = (row >= lowest) & (row < highest)
    for k in range(8):
        cols = slice(128 * k, 128 * k + 128)
        back_ref[:, cols] = jnp.where(inside, stencil_sum(flipped_of(weights), middle, 0, cols), 0.0)


def last_kernel(
    weights, table, image_back, upstream, u2, u1, o, d1, d2, mapped_ref, out_ref, source, middle, back
):
    load_planes((u2, u1, o, d1, d2), source)
    apply_stencils(weights, source, middle, back)
    mapped_ref[...] = middle[1, 1, 8:40, :]
    alpha, gamma, twice_g2, twice_g3 = weights[27], weights[28], weights[31], weights[32]
    u, again = upstream[...], image_back[8:40, :]
    first = alpha * u + twice_g2 * again + back[8:40, :]
    second = gamma * u + twice_g3 * again
    out_ref[:, 0:8, :] = x_forward(first, table).reshape(32, 8, 128)
    out_ref[:, 8:16, :] = x_forward(second, table).reshape(32, 8, 128)


def correlate_kernel(factor_ref, *refs):
    out_ref, scaled, mapped = refs[-3:]
    right, image, mixed = refs[0:3], refs[3:6], refs[6:9]
    right_map, image_map, mixed_map = refs[9:12]
    g1, twice_g2, twice_g3 = (factor_ref[k] for k in (33, 31, 32))
    for p in range(3):
        scaled[p] = mixed[p][...] + g1 * right[p][...] + twice_g2 * image[p][...]
    mapped[0] = mixed_map[...] + g1 * right_map[...] + twice_g2 * image_map[8:40, :]
    mapped[1] = right_map[...]
    mapped[2] = twice_g3 * image_map[8:40, :]
    lane = lanes((1, 128))
    out = jnp.zeros((1, 128), F32)
    column = lanes((ROWS, COLS))
    left_edge, right_edge = column < COLS - 1, column >= 1
    for c in range(3):
        parts = []
        for k in range(3):
            value = mapped[k]
            if c == 0:
                value = jnp.where(left_edge, pltpu.roll(value, COLS - 1, 1), 0.0)
            elif c == 2:
                value = jnp.where(right_edge, pltpu.roll(value, 1, 1), 0.0)
            parts.append(value)
        for a in range(3):
            for b in range(3):
                rows = slice(7 + b, 39 + b)
                total = parts[0] * right[a][rows, :] + parts[1] * scaled[a, rows, :] + parts[2] * image[a][rows, :]
                out = jnp.where(lane == 9 * a + 3 * b + c, jnp.sum(total), out)
    out_ref[...] = out


def shape(*dims):
    return jax.ShapeDtypeStruct(dims, F32)


STENCIL_SCRATCH = (
    pltpu.VMEM((3, 5, FRAME, COLS), F32),
    pltpu.VMEM((3, 3, FRAME, COLS), F32),
)
BACK_SCRATCH = (pltpu.VMEM((FRAME, COLS), F32),)


def call(body, out_shape, scalars, operands, scratch=(), far=(), planes=(), limit=VMEM, flops=400_000_000):
    operands = [*operands, *planes]
    smem, vmem, hbm = (pl.BlockSpec(memory_space=m) for m in (pltpu.SMEM, pltpu.VMEM, pltpu.HBM))
    outs = out_shape if isinstance(out_shape, tuple) else (out_shape,)
    first, count = len(scalars), len(scalars) + len(operands)
    buffers = [pltpu.VMEM(operands[i].shape, operands[i].dtype) for i in far]
    extra = [*buffers, pltpu.SemaphoreType.DMA((len(buffers),))] if buffers else []

    def whole(*refs):
        ins, results = list(refs[:count]), list(refs[count : count + len(outs)])
        own = refs[count + len(outs) :]
        held, sems, own = own[: len(buffers)], own[len(buffers)] if buffers else None, own[len(extra) :]
        copies = []
        for k, i in enumerate(far):
            copies.append(pltpu.make_async_copy(ins[first + i], held[k], sems.at[k]))
            ins[first + i] = held[k]
        for copy in copies:
            copy.start()
        for copy in copies:
            copy.wait()
        body(*ins, *results, *own)

    spec_in = [smem] * len(scalars) + [hbm if i in far else vmem for i in range(len(operands))]
    spec_out = (vmem,) * len(outs)
    return pl.pallas_call(
        whole,
        out_shape=out_shape,
        in_specs=spec_in,
        out_specs=spec_out if isinstance(out_shape, tuple) else spec_out[0],
        scratch_shapes=[*extra, *scratch],
        compiler_params=pltpu.CompilerParams(vmem_limit_bytes=limit),
        cost_estimate=pl.CostEstimate(flops=flops, bytes_accessed=4_000_000, transcendentals=0),
    )(*scalars, *operands)


def exchange(value):
    return lax.all_to_all(value, GY, 0, 0, tiled=True)


def moved(value, by):
    size = lax.axis_size(GZ)
    return lax.ppermute(value, GZ, [(i, i + by) for i in range(size) if 0 <= i + by < size])


def neighbours(value):
    return moved(value, 2), moved(value, 1), value, moved(value, -1), moved(value, -2)


def with_rows(value):
    size = lax.axis_size(GY)
    below = lax.ppermute(value[24:32], GY, [(i, i + 1) for i in range(size - 1)])
    above = lax.ppermute(value[0:8], GY, [(i + 1, i) for i in range(size - 1)])
    return jnp.concatenate([below, value, above], 0)


def from_all(row):
    size = lax.axis_size(GZ)
    return lax.all_to_all(jnp.broadcast_to(row[None], (size, 1, 128)), GZ, 0, 0, tiled=True)


def factors_of(m0, m1, m2, m3, u0, u1):
    def pair(m0, m1, m2, m3):
        step0 = m0 / m1
        norm1 = m0 - 2.0 * step0 * m1 + step0 * step0 * m2
        ratio = norm1 / m0
        keep = 1.0 + ratio
        curvature = keep * keep * m1 - 2.0 * keep * step0 * m2 + step0 * step0 * m3
        step1 = norm1 / curvature
        return step0 + step1 * keep, -step1 * step0

    (alpha, gamma), back = jax.vjp(pair, m0, m1, m2, m3)
    return (alpha, gamma, *back((u0, u1)))


def factors_kernel(weights_ref, rows, further, grown, out_ref, mixed_ref):
    total = jnp.sum(rows[...], 0)
    lane = lanes((1, 128))
    moments = [jnp.sum(jnp.where(lane == k, total, 0.0), axis=1, keepdims=True) for k in range(6)]
    alpha, gamma, g0, g1, g2, g3 = factors_of(*moments)
    for k in range(27):
        out_ref[k] = weights_ref[k]
    for k, value in enumerate((alpha, gamma, 2.0 * g0, 2.0 * g1, 2.0 * g2, 2.0 * g3, g1)):
        out_ref[27 + k] = value[0, 0]
    mixed_ref[...] = gamma * grown[...] + (2.0 * g3) * further[...]


def local(measured, point_spread, stencil_weights, upstream):
    cells = measured.size * lax.axis_size(GY) * lax.axis_size(GZ)
    weights = stencil_weights.reshape(27)
    table, along_y = jnp.asarray(X_TABLE), jnp.asarray(Y_TABLE)
    measured, upstream = measured[0], upstream[0]
    tile, tiles, three = shape(32, 8, 128), shape(32, 16, 128), shape(32, 24, 128)
    spectral, frame, rows, row = shape(32 * BLOCKS, 128), shape(FRAME, COLS), shape(ROWS, COLS), shape(1, 128)

    first = exchange(
        call(spread_kernel, tiles, [], [table, measured, point_spread], far=(0, 1, 2), limit=ALL_VMEM)
    )
    first, grown = lax.optimization_barrier((first, with_rows(upstream)))

    right_out, bank = call(first_filter_kernel, (three, shape(2, 32 * BLOCKS, 128)), [], [along_y, first])
    right, blurred = call(gather_two_kernel, (frame, frame), [], [table, exchange(right_out)])

    right_parts = neighbours(right)
    image, right_map, image_send, row_b = call(
        image_kernel,
        (frame, rows, tile, row),
        [weights],
        [table, blurred, upstream],
        STENCIL_SCRATCH + BACK_SCRATCH,
        planes=right_parts,
    )
    image_arrived = exchange(image_send)
    image_parts = (moved(image, 1), image, moved(image, -1))
    plane_scratch = (pltpu.VMEM((3, 3, FRAME, COLS), F32),)
    further_out, image_spectrum, row_f = call(
        second_filter_kernel, (tiles, spectral, row), [], [along_y, image_arrived, bank]
    )
    image_map, further_out = call(
        map_kernel, (frame, tiles), [weights], [row_b, row_f, further_out], plane_scratch, planes=image_parts
    )
    further_arrived = exchange(further_out)
    map_parts = (moved(image_map, 1), image_map, moved(image_map, -1))
    image_back = call(further_kernel, frame, [weights], [], plane_scratch, planes=map_parts)
    further_arrived, image_back = lax.optimization_barrier((further_arrived, image_back))

    further, row_sum = call(gather_sum_kernel, (frame, row), [], [table, further_arrived, image_back])
    smem, vmem = (pl.BlockSpec(memory_space=m) for m in (pltpu.SMEM, pltpu.VMEM))
    factors, mixed = pl.pallas_call(
        factors_kernel,
        out_shape=(shape(34), frame),
        in_specs=[smem, vmem, vmem, vmem],
        out_specs=(smem, vmem),
        compiler_params=pltpu.CompilerParams(vmem_limit_bytes=VMEM),
    )(weights, from_all(row_sum), further, grown)

    mixed_parts = neighbours(mixed)
    mixed_map, last_send = call(
        last_kernel,
        (rows, tiles),
        [factors],
        [table, image_back, upstream],
        STENCIL_SCRATCH + BACK_SCRATCH,
        planes=mixed_parts,
    )
    operands = [*right_parts[1:4], *image_parts, *mixed_parts[1:4], right_map, image_map, mixed_map]
    scratch = (pltpu.VMEM((3, FRAME, COLS), F32), pltpu.VMEM((3, ROWS, COLS), F32))
    terms = call(correlate_kernel, row, [factors], operands, scratch, far=tuple(range(12)), limit=ALL_VMEM)
    terms = lax.psum(terms, "gz_1")
    last_arrived = exchange(last_send)
    result_out = call(last_filter_kernel, tiles, [factors], [along_y, last_arrived, bank, image_spectrum, terms])
    grad_measured, terms = call(final_kernel, (rows, row), [], [table, exchange(result_out)])
    grad_stencil = lax.psum(terms, "gz_0")[0, :27].reshape(3, 3, 3) / math.sqrt(cells)
    return grad_measured[None], grad_stencil


def solution(mesh):
    groups, planes = mesh.devices.shape
    finer = Mesh(mesh.devices.reshape(groups, 4, planes // 4), (GY, *GZ))
    return jax.shard_map(
        local,
        mesh=finer,
        in_specs=(P(GZ, GY, None), P(GY, None), P(), P(GZ, GY, None)),
        out_specs=(P(GZ, GY, None), P()),
        check_vma=False,
    )
```

```python
import functools
import math

import jax
import jax.numpy as jnp
import ml_dtypes
import numpy as np
from jax import lax
from jax.experimental import pallas as pl
from jax.experimental.pallas import tpu as pltpu
from jax.sharding import Mesh
from jax.sharding import PartitionSpec as P

GY = "gy"
GZ = ("gz_0", "gz_1")
ROWS = 32
COLS = 1024
FRAME = 48
BLOCKS = 9
F32 = jnp.float32
BF16 = jnp.bfloat16
VMEM = 14 * 1024 * 1024
ALL_VMEM = 60 * 1024 * 1024


def split_table(table):
    high = table.astype(ml_dtypes.bfloat16)
    low = (table - high.astype(np.float64)).astype(ml_dtypes.bfloat16)
    return high, low


def x_table():
    part, half, device, i = np.meshgrid(
        np.arange(2), np.arange(2), np.arange(32), np.arange(8), indexing="ij"
    )
    kx = 2 * (16 * (device % 16) + 8 * half + i) + device // 16
    part, kx = part.reshape(-1, 1), kx.reshape(-1, 1)
    x = np.arange(COLS // 2)[None, :]
    angle = 2.0 * np.pi * ((kx * x) % COLS) / COLS
    flip = 1.0 - 2.0 * (x % 2)
    wave = np.where(part == 0, np.cos(angle), -np.sin(angle))
    return np.where((kx == 0) & (part == 1), flip, wave)


def y_tables():
    q = np.arange(32)[:, None]
    s = np.arange(32)[None, :]
    angle = 2.0 * np.pi * ((q * s) % 32) / 32
    first = np.concatenate([np.cos(angle), np.sin(angle)], 0)
    lane = np.arange(128)
    part, half, t = lane // 64, lane // 32 % 2, lane % 32
    turn = 2.0 * np.pi * q * t[None, :] / 1024
    sign = np.where(part == 0, 1.0, -1.0)[None, :]
    turn_cos, turn_sin = np.cos(turn), np.sin(turn) * sign
    angle = 2.0 * np.pi * ((t[:, None] * t[None, :]) % 32) / 32
    pi, po = part[:, None], part[None, :]
    block = np.where(pi == po, np.cos(angle), np.where(pi > po, np.sin(angle), -np.sin(angle)))
    second = np.where(half[:, None] == half[None, :], block, 0.0)
    return first, turn_cos, turn_sin, second


def packed_tables():
    first, turn_cos, turn_sin, second = y_tables()
    first = np.pad(first, ((0, 0), (0, 96)))
    return np.concatenate([second, first, turn_cos, turn_sin], 0).astype(np.float32)


X_TABLE = np.concatenate(split_table(x_table()), 0)
Y_TABLE = packed_tables()
SCALE = 2.0 / (COLS * 1024.0)


def halves(value):
    high = value.astype(BF16)
    return high, (value - high.astype(F32)).astype(BF16)


def dot(left, right):
    return lax.dot_general(left, right, (((1,), (0,)), ((), ())), preferred_element_type=F32)


def dot_nt(left, right):
    return lax.dot_general(left, right, (((1,), (1,)), ((), ())), preferred_element_type=F32)


def swap(value):
    return pltpu.roll(value, 64, 1)


def lanes(shape):
    return lax.broadcasted_iota(jnp.int32, shape, 1)


def sublanes(shape):
    return lax.broadcasted_iota(jnp.int32, shape, 0)


def x_forward(value, table_ref):
    left, right = value[:, : COLS // 2], value[:, COLS // 2 :]
    group = lanes((128, 128)) // 32
    outs = []
    for parity, folded in enumerate((left + right, left - right)):
        high, low = halves(folded)
        both = jnp.concatenate([high] * 4 + [low] * 4, 0)
        out = None
        for h in range(4):
            start = 256 * h + 128 * parity
            first = dot_nt(table_ref[start : start + 128, :], both)
            piece = first[:, :128] + first[:, 128:]
            piece = piece + dot_nt(table_ref[1024 + start : 1152 + start, :], both[:128])
            out = piece if out is None else jnp.where(group == h, piece, out)
        outs.append(out)
    return jnp.concatenate(outs, 0)


def x_inverse(spectra, table_ref):
    turned = [value.T for value in spectra]
    sums = []
    for parity in range(2):
        cols = slice(128 * parity, 128 * parity + 128)
        rows = [jnp.concatenate([v[32 * h : 32 * h + 32, cols] for h in range(4)], 1) for v in turned]
        left = rows[0] if len(rows) == 1 else jnp.concatenate(rows, 0)
        count = left.shape[0]
        high, low = halves(left)
        both = jnp.concatenate([high, low], 0)
        total = None
        for h in range(4):
            start = 256 * h + 128 * parity
            k = slice(128 * h, 128 * h + 128)
            first = dot(both[:, k], table_ref[start : start + 128, :])
            piece = first[:count] + first[count:] + dot(high[:, k], table_ref[1024 + start : 1152 + start, :])
            total = piece if total is None else total + piece
        sums.append(total)
    return jnp.concatenate([sums[0] + sums[1], sums[0] - sums[1]], 1)


class Lateral:
    def __init__(self, table):
        second = table[0:128, :]
        self.second = halves(second)
        self.back = halves(second.T)
        self.first = halves(table[128:192, :][:, 0:32])
        self.cos, self.sin = table[192:224, :], table[224:256, :]
        self.is_first = jnp.where(lax.axis_index(GY) == 0, 1.0, 0.0).astype(F32)
        self.sign = jnp.where(lanes((32, 128)) < 64, 1.0, -1.0)

    def over_s(self, blocks, direction):
        high, low = halves(jnp.concatenate(blocks, 1))
        both = dot(self.first[0], high) + dot(self.first[0], low) + dot(self.first[1], high)
        out = []
        for i in range(len(blocks)):
            cols = slice(128 * i, 128 * i + 128)
            out.append(both[:32, cols] + direction * self.sign * swap(both[32:, cols]))
        return out

    def over_t(self, value, tables):
        high, low = halves(value)
        return dot(high, tables[0]) + dot(low, tables[0]) + dot(high, tables[1])

    def forward(self, ref, offset):
        blocks = [ref[:, offset + i, :] for i in range(8)]
        lane = lanes((32, 128))
        nyquist = (lane >= 64) & (lane < 96)
        blocks.append(jnp.where(lane < 32, swap(blocks[0]), 0.0) * self.is_first)
        blocks[0] = jnp.where(nyquist, blocks[0] * (1.0 - self.is_first), blocks[0])
        blocks = self.over_s(blocks, 1.0)
        blocks = [z * self.cos + swap(z) * self.sin for z in blocks]
        return self.over_t(jnp.concatenate(blocks, 0), self.second)

    def inverse(self, spectrum):
        all_rows = self.over_t(spectrum, self.back)
        blocks = [all_rows[32 * i : 32 * i + 32] for i in range(BLOCKS)]
        blocks = [z * self.cos - swap(z) * self.sin for z in blocks]
        blocks = self.over_s(blocks, -1.0)
        lane = lanes((32, 128))
        nyquist = (lane >= 64) & (lane < 96)
        own = jnp.where(lane // 32 % 2 == 0, SCALE * (1.0 - 0.5 * self.is_first), SCALE)
        blocks[0] = (blocks[0] + jnp.where(nyquist, swap(blocks[8]), 0.0)) * own
        return [blocks[0]] + [z * SCALE for z in blocks[1:8]]

    def weighted_sum(self, value):
        lane, row = lanes(value.shape), sublanes(value.shape)
        weight = jnp.where((row < 32) & (lane // 32 % 2 == 0), 2.0 - self.is_first, 2.0)
        weight = jnp.where(row >= 256, 1.0, weight)
        return jnp.sum(value * weight) * (1.0 / (COLS * 1024.0))


def halo_rows(block):
    lane, row = lanes((32, 128)) % 32, sublanes((32, 128))
    after = jnp.where((lane < 8) & (row < 31), pltpu.roll(block, 31, 0), 0.0)
    before = jnp.where((lane >= 24) & (row > 0), pltpu.roll(block, 1, 0), 0.0)
    return after, before


def product(real, imaginary, value):
    return real * value + imaginary * swap(value)


def conjugate_factors(transfer):
    turned, left = swap(transfer), lanes(transfer.shape) < 64
    return jnp.where(left, transfer, turned), jnp.where(left, turned, -transfer)


def spread_kernel(table_ref, measured, point_spread, out_ref):
    for f, ref in enumerate((measured, point_spread)):
        out_ref[:, 8 * f : 8 * f + 8, :] = x_forward(ref[...], table_ref).reshape(32, 8, 128)


def first_filter_kernel(table, arrived, out_ref, bank_ref):
    lateral = Lateral(table)
    transfer = lateral.forward(arrived, 8)
    observed = lateral.forward(arrived, 0)
    real, imaginary = conjugate_factors(transfer)
    power = real * real + imaginary * imaginary
    spectrum = product(real, imaginary, observed)
    right = lateral.inverse(spectrum)
    image = lateral.inverse(spectrum * power)
    for i in range(8):
        out_ref[:, i, :] = right[i]
        out_ref[:, 8 + i, :] = image[i]
        after, before = halo_rows(right[i])
        image_after, image_before = halo_rows(image[i])
        image_after, image_before = pltpu.roll(image_after, 8, 1), pltpu.roll(image_before, 120, 1)
        out_ref[:, 16 + i, :] = after + before + image_after + image_before
    bank_ref[0] = transfer
    bank_ref[1] = spectrum


def second_filter_kernel(table, arrived, bank_ref, out_ref, image_ref, row_ref):
    lateral = Lateral(table)
    real, imaginary = conjugate_factors(bank_ref[0])
    power = real * real + imaginary * imaginary
    image = power * bank_ref[1] + lateral.forward(arrived, 0)
    filtered = power * image
    blocks = lateral.inverse(filtered)
    for i in range(8):
        out_ref[:, i, :] = blocks[i]
        after, before = halo_rows(blocks[i])
        out_ref[:, 8 + i, :] = after + before
    image_ref[...] = image
    row_ref[...] = jnp.where(lanes((1, 128)) == 3, lateral.weighted_sum(image * filtered), 0.0)


def last_filter_kernel(
    factors_ref, table, arrived, bank_ref, image_ref, terms, out_ref
):
    lateral = Lateral(table)
    factor_ref = [factors_ref[27 + k] for k in range(6)]
    real, imaginary = conjugate_factors(bank_ref[0])
    power = real * real + imaginary * imaginary
    image = image_ref[...]
    total = factor_ref[4] * image + factor_ref[5] * (power * image) + lateral.forward(arrived, 8)
    total = power * total + factor_ref[2] * bank_ref[1] + factor_ref[3] * image
    total = total + lateral.forward(arrived, 0)
    blocks = lateral.inverse(product(real, -imaginary, total))
    for i in range(8):
        out_ref[:, i, :] = blocks[i]
        out_ref[:, 8 + i, :] = jnp.broadcast_to(terms[...], (32, 128))


def gather_two_kernel(table_ref, arrived, right_ref, image_ref):
    tiles = [arrived[:, 8 * f : 8 * f + 8, :].reshape(256, 128) for f in range(3)]
    value = x_inverse(tiles, table_ref)
    right_ref[0:8, :] = value[88:96]
    right_ref[8:40, :] = value[0:32]
    right_ref[40:48, :] = value[64:72]
    image_ref[0:8, :] = value[80:88]
    image_ref[8:40, :] = value[32:64]
    image_ref[40:48, :] = value[72:80]


def gather_sum_kernel(table_ref, arrived, base, out_ref, row_ref):
    row = pltpu.roll(jnp.broadcast_to(jnp.sum(arrived[:, 8, :], 0, keepdims=True), (8, 128)), 120, 1)
    row_ref[...] = jnp.where(lanes((1, 128)) < 6, row[0:1], 0.0)
    tiles = [arrived[:, 8 * f : 8 * f + 8, :].reshape(256, 128) for f in range(2)]
    value = x_inverse(tiles, table_ref)
    out_ref[0:8, :] = base[0:8, :] + value[56:64]
    out_ref[8:40, :] = base[8:40, :] + value[0:32]
    out_ref[40:48, :] = base[40:48, :] + value[32:40]


def final_kernel(table_ref, arrived, out_ref, row_ref):
    out_ref[...] = x_inverse([arrived[:, 0:8, :].reshape(256, 128)], table_ref)
    row_ref[...] = jnp.sum(arrived[:, 8, :], 0, keepdims=True)


def shifted_columns(value):
    column = lanes(value.shape)
    left = jnp.where(column >= 1, pltpu.roll(value, 1, 1), 0.0)
    right = jnp.where(column < COLS - 1, pltpu.roll(value, COLS - 1, 1), 0.0)
    return left, right


def stencil_sum(weight, source, start, cols):
    total = None
    for b in range(3):
        part = None
        for a in range(3):
            for c in range(3):
                term = weight(a, b, c) * source[c, start + a, :, cols]
                part = term if part is None else part + term
        if b == 0:
            part = pltpu.roll(part, 1, 0)
        elif b == 2:
            part = pltpu.roll(part, FRAME - 1, 0)
        total = part if total is None else total + part
    return total


def load_planes(parts, source):
    for p, ref in enumerate(parts):
        value = ref[...]
        source[1, p] = value
        source[0, p], source[2, p] = shifted_columns(value)


def row_bounds():
    device, plane, planes = lax.axis_index(GY), lax.axis_index(GZ), lax.axis_size(GZ)
    lowest = jnp.where(device > 0, 0, 8)
    highest = jnp.where(device < 31, FRAME, 40)

    def highest_at(here):
        return jnp.where((here >= 0) & (here < planes), highest, 0)

    return sublanes((FRAME, 128)), lowest, highest, lambda p: highest_at(plane + p)


def weight_of(weights_ref):
    return lambda a, b, c: weights_ref[9 * a + 3 * b + c]


def flipped_of(weights_ref):
    return lambda a, b, c: weights_ref[26 - 9 * a - 3 * b - c]


def apply_stencils(weights_ref, source, middle, back_ref):
    row, lowest, highest, highest_at = row_bounds()
    for p in range(3):
        valid = (row >= lowest) & (row < highest_at(p - 1))
        for k in range(8):
            cols = slice(128 * k, 128 * k + 128)
            value = stencil_sum(weight_of(weights_ref), source, p, cols)
            middle[1, p, :, cols] = jnp.where(valid, value, 0.0)
    for p in range(3):
        middle[0, p], middle[2, p] = shifted_columns(middle[1, p])
    inside = (row >= lowest) & (row < highest)
    for k in range(8):
        cols = slice(128 * k, 128 * k + 128)
        back_ref[:, cols] = jnp.where(inside, stencil_sum(flipped_of(weights_ref), middle, 0, cols), 0.0)


def row_of(values):
    lane = lanes((1, 128))
    out = jnp.zeros((1, 128), F32)
    for k, value in values:
        out = jnp.where(lane == k, jnp.sum(value), out)
    return out


def image_kernel(weights, table, blurred, upstream, u2, u1, o, d1, d2, image_ref, mapped_ref, out_ref, row_ref, *scratch):
    source, middle, back = scratch
    load_planes((u2, u1, o, d1, d2), source)
    apply_stencils(weights, source, middle, back)
    out_ref[...] = x_forward(back[8:40, :], table).reshape(32, 8, 128)
    mapped_ref[...] = middle[1, 1, 8:40, :]
    image_ref[...] = blurred[...] + back[...]
    b, ab, u = source[1, 2, 8:40, :], image_ref[8:40, :], upstream[...]
    row_ref[...] = row_of(((0, b * b), (1, b * ab), (2, ab * ab), (4, u * b), (5, u * ab)))


def map_kernel(weights, row_b, row_f, further, u1, o, d1, mapped_ref, out_ref, source):
    load_planes((u1, o, d1), source)
    row, lowest, highest, _ = row_bounds()
    inside = (row >= lowest) & (row < highest)
    for k in range(8):
        cols = slice(128 * k, 128 * k + 128)
        mapped_ref[:, cols] = jnp.where(inside, stencil_sum(weight_of(weights), source, 0, cols), 0.0)
    mapped = mapped_ref[8:40, :]
    sums = row_b[...] + row_f[...] + row_of(((3, mapped * mapped),))
    out_ref[...] = further[...]
    out_ref[:, 8, :] = further[:, 8, :] + pltpu.roll(jnp.broadcast_to(sums, (32, 128)), 8, 1)


def further_kernel(weights, u1, o, d1, back_ref, middle):
    load_planes((u1, o, d1), middle)
    row, lowest, highest, _ = row_bounds()
    inside = (row >= lowest) & (row < highest)
    for k in range(8):
        cols = slice(128 * k, 128 * k + 128)
        back_ref[:, cols] = jnp.where(inside, stencil_sum(flipped_of(weights), middle, 0, cols), 0.0)


def last_kernel(
    weights, table, image_back, upstream, u2, u1, o, d1, d2, mapped_ref, out_ref, source, middle, back
):
    load_planes((u2, u1, o, d1, d2), source)
    apply_stencils(weights, source, middle, back)
    mapped_ref[...] = middle[1, 1, 8:40, :]
    alpha, gamma, twice_g2, twice_g3 = weights[27], weights[28], weights[31], weights[32]
    u, again = upstream[...], image_back[8:40, :]
    first = alpha * u + twice_g2 * again + back[8:40, :]
    second = gamma * u + twice_g3 * again
    out_ref[:, 0:8, :] = x_forward(first, table).reshape(32, 8, 128)
    out_ref[:, 8:16, :] = x_forward(second, table).reshape(32, 8, 128)


def correlate_kernel(factor_ref, *refs):
    out_ref, scaled, mapped = refs[-3:]
    right, image, mixed = refs[0:3], refs[3:6], refs[6:9]
    right_map, image_map, mixed_map = refs[9:12]
    g1, twice_g2, twice_g3 = (factor_ref[k] for k in (33, 31, 32))
    for p in range(3):
        scaled[p] = mixed[p][...] + g1 * right[p][...] + twice_g2 * image[p][...]
    mapped[0] = mixed_map[...] + g1 * right_map[...] + twice_g2 * image_map[8:40, :]
    mapped[1] = right_map[...]
    mapped[2] = twice_g3 * image_map[8:40, :]
    lane = lanes((1, 128))
    out = jnp.zeros((1, 128), F32)
    column = lanes((ROWS, COLS))
    left_edge, right_edge = column < COLS - 1, column >= 1
    for c in range(3):
        parts = []
        for k in range(3):
            value = mapped[k]
            if c == 0:
                value = jnp.where(left_edge, pltpu.roll(value, COLS - 1, 1), 0.0)
            elif c == 2:
                value = jnp.where(right_edge, pltpu.roll(value, 1, 1), 0.0)
            parts.append(value)
        for a in range(3):
            for b in range(3):
                rows = slice(7 + b, 39 + b)
                total = parts[0] * right[a][rows, :] + parts[1] * scaled[a, rows, :] + parts[2] * image[a][rows, :]
                out = jnp.where(lane == 9 * a + 3 * b + c, jnp.sum(total), out)
    out_ref[...] = out


def shape(*dims):
    return jax.ShapeDtypeStruct(dims, F32)


STENCIL_SCRATCH = (
    pltpu.VMEM((3, 5, FRAME, COLS), F32),
    pltpu.VMEM((3, 3, FRAME, COLS), F32),
)
BACK_SCRATCH = (pltpu.VMEM((FRAME, COLS), F32),)


def call(body, out_shape, scalars, operands, scratch=(), far=(), planes=(), limit=VMEM, flops=400_000_000):
    operands = [*operands, *planes]
    smem, vmem, hbm = (pl.BlockSpec(memory_space=m) for m in (pltpu.SMEM, pltpu.VMEM, pltpu.HBM))
    outs = out_shape if isinstance(out_shape, tuple) else (out_shape,)
    first, count = len(scalars), len(scalars) + len(operands)
    buffers = [pltpu.VMEM(operands[i].shape, operands[i].dtype) for i in far]
    extra = [*buffers, pltpu.SemaphoreType.DMA((len(buffers),))] if buffers else []

    def whole(*refs):
        ins, results = list(refs[:count]), list(refs[count : count + len(outs)])
        own = refs[count + len(outs) :]
        held, sems, own = own[: len(buffers)], own[len(buffers)] if buffers else None, own[len(extra) :]
        copies = []
        for k, i in enumerate(far):
            copies.append(pltpu.make_async_copy(ins[first + i], held[k], sems.at[k]))
            ins[first + i] = held[k]
        for copy in copies:
            copy.start()
        for copy in copies:
            copy.wait()
        body(*ins, *results, *own)

    spec_in = [smem] * len(scalars) + [hbm if i in far else vmem for i in range(len(operands))]
    spec_out = (vmem,) * len(outs)
    return pl.pallas_call(
        whole,
        out_shape=out_shape,
        in_specs=spec_in,
        out_specs=spec_out if isinstance(out_shape, tuple) else spec_out[0],
        scratch_shapes=[*extra, *scratch],
        compiler_params=pltpu.CompilerParams(vmem_limit_bytes=limit),
        cost_estimate=pl.CostEstimate(flops=flops, bytes_accessed=4_000_000, transcendentals=0),
    )(*scalars, *operands)


def exchange(value):
    return lax.all_to_all(value, GY, 0, 0, tiled=True)


def moved(value, by):
    size = lax.axis_size(GZ)
    return lax.ppermute(value, GZ, [(i, i + by) for i in range(size) if 0 <= i + by < size])


def neighbours(value):
    return moved(value, 2), moved(value, 1), value, moved(value, -1), moved(value, -2)


def with_rows(value):
    size = lax.axis_size(GY)
    below = lax.ppermute(value[24:32], GY, [(i, i + 1) for i in range(size - 1)])
    above = lax.ppermute(value[0:8], GY, [(i + 1, i) for i in range(size - 1)])
    return jnp.concatenate([below, value, above], 0)


def from_all(row):
    size = lax.axis_size(GZ)
    return lax.all_to_all(jnp.broadcast_to(row[None], (size, 1, 128)), GZ, 0, 0, tiled=True)


def factors_of(m0, m1, m2, m3, u0, u1):
    def pair(m0, m1, m2, m3):
        step0 = m0 / m1
        norm1 = m0 - 2.0 * step0 * m1 + step0 * step0 * m2
        ratio = norm1 / m0
        keep = 1.0 + ratio
        curvature = keep * keep * m1 - 2.0 * keep * step0 * m2 + step0 * step0 * m3
        step1 = norm1 / curvature
        return step0 + step1 * keep, -step1 * step0

    (alpha, gamma), back = jax.vjp(pair, m0, m1, m2, m3)
    return (alpha, gamma, *back((u0, u1)))


def factors_kernel(weights_ref, rows, further, grown, out_ref, mixed_ref):
    total = jnp.sum(rows[...], 0)
    lane = lanes((1, 128))
    moments = [jnp.sum(jnp.where(lane == k, total, 0.0), axis=1, keepdims=True) for k in range(6)]
    alpha, gamma, g0, g1, g2, g3 = factors_of(*moments)
    for k in range(27):
        out_ref[k] = weights_ref[k]
    for k, value in enumerate((alpha, gamma, 2.0 * g0, 2.0 * g1, 2.0 * g2, 2.0 * g3, g1)):
        out_ref[27 + k] = value[0, 0]
    mixed_ref[...] = gamma * grown[...] + (2.0 * g3) * further[...]


def local(measured, point_spread, stencil_weights, upstream):
    cells = measured.size * lax.axis_size(GY) * lax.axis_size(GZ)
    weights = stencil_weights.reshape(27)
    table, along_y = jnp.asarray(X_TABLE), jnp.asarray(Y_TABLE)
    measured, upstream = measured[0], upstream[0]
    tile, tiles, three = shape(32, 8, 128), shape(32, 16, 128), shape(32, 24, 128)
    spectral, frame, rows, row = shape(32 * BLOCKS, 128), shape(FRAME, COLS), shape(ROWS, COLS), shape(1, 128)

    first = exchange(
        call(spread_kernel, tiles, [], [table, measured, point_spread], far=(0, 1, 2), limit=ALL_VMEM)
    )
    first, grown = lax.optimization_barrier((first, with_rows(upstream)))

    right_out, bank = call(first_filter_kernel, (three, shape(2, 32 * BLOCKS, 128)), [], [along_y, first])
    right, blurred = call(gather_two_kernel, (frame, frame), [], [table, exchange(right_out)])

    right_parts = neighbours(right)
    image, right_map, image_send, row_b = call(
        image_kernel,
        (frame, rows, tile, row),
        [weights],
        [table, blurred, upstream],
        STENCIL_SCRATCH + BACK_SCRATCH,
        planes=right_parts,
    )
    image_arrived = exchange(image_send)
    image_parts = (moved(image, 1), image, moved(image, -1))
    plane_scratch = (pltpu.VMEM((3, 3, FRAME, COLS), F32),)
    further_out, image_spectrum, row_f = call(
        second_filter_kernel, (tiles, spectral, row), [], [along_y, image_arrived, bank]
    )
    image_map, further_out = call(
        map_kernel, (frame, tiles), [weights], [row_b, row_f, further_out], plane_scratch, planes=image_parts
    )
    further_arrived = exchange(further_out)
    map_parts = (moved(image_map, 1), image_map, moved(image_map, -1))
    image_back = call(further_kernel, frame, [weights], [], plane_scratch, planes=map_parts)
    further_arrived, image_back = lax.optimization_barrier((further_arrived, image_back))

    further, row_sum = call(gather_sum_kernel, (frame, row), [], [table, further_arrived, image_back])
    smem, vmem = (pl.BlockSpec(memory_space=m) for m in (pltpu.SMEM, pltpu.VMEM))
    factors, mixed = pl.pallas_call(
        factors_kernel,
        out_shape=(shape(34), frame),
        in_specs=[smem, vmem, vmem, vmem],
        out_specs=(smem, vmem),
        compiler_params=pltpu.CompilerParams(vmem_limit_bytes=VMEM),
    )(weights, from_all(row_sum), further, grown)

    mixed_parts = neighbours(mixed)
    mixed_map, last_send = call(
        last_kernel,
        (rows, tiles),
        [factors],
        [table, image_back, upstream],
        STENCIL_SCRATCH + BACK_SCRATCH,
        planes=mixed_parts,
    )
    operands = [*right_parts[1:4], *image_parts, *mixed_parts[1:4], right_map, image_map, mixed_map]
    scratch = (pltpu.VMEM((3, FRAME, COLS), F32), pltpu.VMEM((3, ROWS, COLS), F32))
    terms = call(correlate_kernel, row, [factors], operands, scratch, far=tuple(range(12)), limit=ALL_VMEM)
    terms = lax.psum(lax.psum(terms, "gz_1"), "gz_0")
    last_arrived = exchange(last_send)
    result_out = call(last_filter_kernel, tiles, [factors], [along_y, last_arrived, bank, image_spectrum, terms])
    grad_measured, terms = call(final_kernel, (rows, row), [], [table, exchange(result_out)])
    grad_stencil = terms[0, :27].reshape(3, 3, 3) / math.sqrt(cells)
    return grad_measured[None], grad_stencil


def solution(mesh):
    groups, planes = mesh.devices.shape
    finer = Mesh(mesh.devices.reshape(groups, 4, planes // 4), (GY, *GZ))
    return jax.shard_map(
        local,
        mesh=finer,
        in_specs=(P(GZ, GY, None), P(GY, None), P(), P(GZ, GY, None)),
        out_specs=(P(GZ, GY, None), P()),
        check_vma=False,
    )
```

```python
import functools
import math

import jax
import jax.numpy as jnp
import ml_dtypes
import numpy as np
from jax import lax
from jax.experimental import pallas as pl
from jax.experimental.pallas import tpu as pltpu
from jax.sharding import Mesh
from jax.sharding import PartitionSpec as P

GY = "gy"
GZ = ("gz_0", "gz_1")
ROWS = 32
COLS = 1024
FRAME = 48
BLOCKS = 9
F32 = jnp.float32
BF16 = jnp.bfloat16
VMEM = 14 * 1024 * 1024
ALL_VMEM = 60 * 1024 * 1024


def split_table(table):
    high = table.astype(ml_dtypes.bfloat16)
    low = (table - high.astype(np.float64)).astype(ml_dtypes.bfloat16)
    return high, low


def x_table():
    part, half, device, i = np.meshgrid(
        np.arange(2), np.arange(2), np.arange(32), np.arange(8), indexing="ij"
    )
    kx = 2 * (16 * (device % 16) + 8 * half + i) + device // 16
    part, kx = part.reshape(-1, 1), kx.reshape(-1, 1)
    x = np.arange(COLS // 2)[None, :]
    angle = 2.0 * np.pi * ((kx * x) % COLS) / COLS
    flip = 1.0 - 2.0 * (x % 2)
    wave = np.where(part == 0, np.cos(angle), -np.sin(angle))
    return np.where((kx == 0) & (part == 1), flip, wave)


def y_tables():
    q = np.arange(32)[:, None]
    s = np.arange(32)[None, :]
    angle = 2.0 * np.pi * ((q * s) % 32) / 32
    first = np.concatenate([np.cos(angle), np.sin(angle)], 0)
    lane = np.arange(128)
    part, half, t = lane // 64, lane // 32 % 2, lane % 32
    turn = 2.0 * np.pi * q * t[None, :] / 1024
    sign = np.where(part == 0, 1.0, -1.0)[None, :]
    turn_cos, turn_sin = np.cos(turn), np.sin(turn) * sign
    angle = 2.0 * np.pi * ((t[:, None] * t[None, :]) % 32) / 32
    pi, po = part[:, None], part[None, :]
    block = np.where(pi == po, np.cos(angle), np.where(pi > po, np.sin(angle), -np.sin(angle)))
    second = np.where(half[:, None] == half[None, :], block, 0.0)
    return first, turn_cos, turn_sin, second


def packed_tables():
    first, turn_cos, turn_sin, second = y_tables()
    first = np.pad(first, ((0, 0), (0, 96)))
    return np.concatenate([second, first, turn_cos, turn_sin], 0).astype(np.float32)


X_TABLE = np.concatenate(split_table(x_table()), 0)
Y_TABLE = packed_tables()
SCALE = 2.0 / (COLS * 1024.0)


def halves(value):
    high = value.astype(BF16)
    return high, (value - high.astype(F32)).astype(BF16)


def dot(left, right):
    return lax.dot_general(left, right, (((1,), (0,)), ((), ())), preferred_element_type=F32)


def dot_nt(left, right):
    return lax.dot_general(left, right, (((1,), (1,)), ((), ())), preferred_element_type=F32)


def swap(value):
    return pltpu.roll(value, 64, 1)


def lanes(shape):
    return lax.broadcasted_iota(jnp.int32, shape, 1)


def sublanes(shape):
    return lax.broadcasted_iota(jnp.int32, shape, 0)


def x_forward(value, table_ref):
    left, right = value[:, : COLS // 2], value[:, COLS // 2 :]
    group = lanes((128, 128)) // 32
    outs = []
    for parity, folded in enumerate((left + right, left - right)):
        high, low = halves(folded)
        both = jnp.concatenate([high] * 4 + [low] * 4, 0)
        out = None
        for h in range(4):
            start = 256 * h + 128 * parity
            first = dot_nt(table_ref[start : start + 128, :], both)
            piece = first[:, :128] + first[:, 128:]
            piece = piece + dot_nt(table_ref[1024 + start : 1152 + start, :], both[:128])
            out = piece if out is None else jnp.where(group == h, piece, out)
        outs.append(out)
    return jnp.concatenate(outs, 0)


def x_inverse(spectra, table_ref):
    turned = [value.T for value in spectra]
    sums = []
    for parity in range(2):
        cols = slice(128 * parity, 128 * parity + 128)
        rows = [jnp.concatenate([v[32 * h : 32 * h + 32, cols] for h in range(4)], 1) for v in turned]
        left = rows[0] if len(rows) == 1 else jnp.concatenate(rows, 0)
        count = left.shape[0]
        high, low = halves(left)
        both = jnp.concatenate([high, low], 0)
        total = None
        for h in range(4):
            start = 256 * h + 128 * parity
            k = slice(128 * h, 128 * h + 128)
            first = dot(both[:, k], table_ref[start : start + 128, :])
            piece = first[:count] + first[count:] + dot(high[:, k], table_ref[1024 + start : 1152 + start, :])
            total = piece if total is None else total + piece
        sums.append(total)
    return jnp.concatenate([sums[0] + sums[1], sums[0] - sums[1]], 1)


class Lateral:
    def __init__(self, table):
        second = table[0:128, :]
        self.second = halves(second)
        self.back = halves(second.T)
        self.first = halves(table[128:192, :][:, 0:32])
        self.cos, self.sin = table[192:224, :], table[224:256, :]
        self.is_first = jnp.where(lax.axis_index(GY) == 0, 1.0, 0.0).astype(F32)
        self.sign = jnp.where(lanes((32, 128)) < 64, 1.0, -1.0)

    def over_s(self, blocks, direction):
        high, low = halves(jnp.concatenate(blocks, 1))
        both = dot(self.first[0], high) + dot(self.first[0], low) + dot(self.first[1], high)
        out = []
        for i in range(len(blocks)):
            cols = slice(128 * i, 128 * i + 128)
            out.append(both[:32, cols] + direction * self.sign * swap(both[32:, cols]))
        return out

    def over_t(self, value, tables):
        high, low = halves(value)
        return dot(high, tables[0]) + dot(low, tables[0]) + dot(high, tables[1])

    def forward(self, ref, offset):
        blocks = [ref[:, offset + i, :] for i in range(8)]
        lane = lanes((32, 128))
        nyquist = (lane >= 64) & (lane < 96)
        blocks.append(jnp.where(lane < 32, swap(blocks[0]), 0.0) * self.is_first)
        blocks[0] = jnp.where(nyquist, blocks[0] * (1.0 - self.is_first), blocks[0])
        blocks = self.over_s(blocks, 1.0)
        blocks = [z * self.cos + swap(z) * self.sin for z in blocks]
        return self.over_t(jnp.concatenate(blocks, 0), self.second)

    def inverse(self, spectrum):
        all_rows = self.over_t(spectrum, self.back)
        blocks = [all_rows[32 * i : 32 * i + 32] for i in range(BLOCKS)]
        blocks = [z * self.cos - swap(z) * self.sin for z in blocks]
        blocks = self.over_s(blocks, -1.0)
        lane = lanes((32, 128))
        nyquist = (lane >= 64) & (lane < 96)
        own = jnp.where(lane // 32 % 2 == 0, SCALE * (1.0 - 0.5 * self.is_first), SCALE)
        blocks[0] = (blocks[0] + jnp.where(nyquist, swap(blocks[8]), 0.0)) * own
        return [blocks[0]] + [z * SCALE for z in blocks[1:8]]

    def weighted_sum(self, value):
        lane, row = lanes(value.shape), sublanes(value.shape)
        weight = jnp.where((row < 32) & (lane // 32 % 2 == 0), 2.0 - self.is_first, 2.0)
        weight = jnp.where(row >= 256, 1.0, weight)
        return jnp.sum(value * weight) * (1.0 / (COLS * 1024.0))


def halo_rows(block):
    lane, row = lanes((32, 128)) % 32, sublanes((32, 128))
    after = jnp.where((lane < 8) & (row < 31), pltpu.roll(block, 31, 0), 0.0)
    before = jnp.where((lane >= 24) & (row > 0), pltpu.roll(block, 1, 0), 0.0)
    return after, before


def product(real, imaginary, value):
    return real * value + imaginary * swap(value)


def conjugate_factors(transfer):
    turned, left = swap(transfer), lanes(transfer.shape) < 64
    return jnp.where(left, transfer, turned), jnp.where(left, turned, -transfer)


def spread_kernel(table_ref, measured, point_spread, out_ref):
    for f, ref in enumerate((measured, point_spread)):
        out_ref[:, 8 * f : 8 * f + 8, :] = x_forward(ref[...], table_ref).reshape(32, 8, 128)


def first_filter_kernel(table, arrived, out_ref, bank_ref):
    lateral = Lateral(table)
    transfer = lateral.forward(arrived, 8)
    observed = lateral.forward(arrived, 0)
    real, imaginary = conjugate_factors(transfer)
    power = real * real + imaginary * imaginary
    spectrum = product(real, imaginary, observed)
    right = lateral.inverse(spectrum)
    image = lateral.inverse(spectrum * power)
    for i in range(8):
        out_ref[:, i, :] = right[i]
        out_ref[:, 8 + i, :] = image[i]
        after, before = halo_rows(right[i])
        image_after, image_before = halo_rows(image[i])
        image_after, image_before = pltpu.roll(image_after, 8, 1), pltpu.roll(image_before, 120, 1)
        out_ref[:, 16 + i, :] = after + before + image_after + image_before
    bank_ref[0] = transfer
    bank_ref[1] = spectrum


def second_filter_kernel(table, arrived, bank_ref, out_ref, image_ref, row_ref):
    lateral = Lateral(table)
    real, imaginary = conjugate_factors(bank_ref[0])
    power = real * real + imaginary * imaginary
    image = power * bank_ref[1] + lateral.forward(arrived, 0)
    filtered = power * image
    blocks = lateral.inverse(filtered)
    for i in range(8):
        out_ref[:, i, :] = blocks[i]
        after, before = halo_rows(blocks[i])
        out_ref[:, 8 + i, :] = after + before
    image_ref[...] = image
    row_ref[...] = jnp.where(lanes((1, 128)) == 3, lateral.weighted_sum(image * filtered), 0.0)


def last_filter_kernel(
    factors_ref, table, arrived, bank_ref, image_ref, terms, out_ref
):
    lateral = Lateral(table)
    factor_ref = [factors_ref[27 + k] for k in range(6)]
    real, imaginary = conjugate_factors(bank_ref[0])
    power = real * real + imaginary * imaginary
    image = image_ref[...]
    total = factor_ref[4] * image + factor_ref[5] * (power * image) + lateral.forward(arrived, 8)
    total = power * total + factor_ref[2] * bank_ref[1] + factor_ref[3] * image
    total = total + lateral.forward(arrived, 0)
    blocks = lateral.inverse(product(real, -imaginary, total))
    for i in range(8):
        out_ref[:, i, :] = blocks[i]
        out_ref[:, 8 + i, :] = jnp.broadcast_to(terms[...], (32, 128))


def gather_two_kernel(table_ref, arrived, right_ref, image_ref):
    tiles = [arrived[:, 8 * f : 8 * f + 8, :].reshape(256, 128) for f in range(3)]
    value = x_inverse(tiles, table_ref)
    right_ref[0:8, :] = value[88:96]
    right_ref[8:40, :] = value[0:32]
    right_ref[40:48, :] = value[64:72]
    image_ref[0:8, :] = value[80:88]
    image_ref[8:40, :] = value[32:64]
    image_ref[40:48, :] = value[72:80]


def gather_sum_kernel(table_ref, arrived, base, out_ref, row_ref):
    row = pltpu.roll(jnp.broadcast_to(jnp.sum(arrived[:, 8, :], 0, keepdims=True), (8, 128)), 120, 1)
    row_ref[...] = jnp.where(lanes((1, 128)) < 6, row[0:1], 0.0)
    tiles = [arrived[:, 8 * f : 8 * f + 8, :].reshape(256, 128) for f in range(2)]
    value = x_inverse(tiles, table_ref)
    out_ref[0:8, :] = base[0:8, :] + value[56:64]
    out_ref[8:40, :] = base[8:40, :] + value[0:32]
    out_ref[40:48, :] = base[40:48, :] + value[32:40]


def final_kernel(table_ref, arrived, out_ref, row_ref):
    out_ref[...] = x_inverse([arrived[:, 0:8, :].reshape(256, 128)], table_ref)
    row_ref[...] = jnp.sum(arrived[:, 8, :], 0, keepdims=True)


def shifted_columns(value):
    column = lanes(value.shape)
    left = jnp.where(column >= 1, pltpu.roll(value, 1, 1), 0.0)
    right = jnp.where(column < COLS - 1, pltpu.roll(value, COLS - 1, 1), 0.0)
    return left, right


def stencil_sum(weight, source, start, cols):
    total = None
    for b in range(3):
        part = None
        for a in range(3):
            for c in range(3):
                term = weight(a, b, c) * source[c, start + a, :, cols]
                part = term if part is None else part + term
        if b == 0:
            part = pltpu.roll(part, 1, 0)
        elif b == 2:
            part = pltpu.roll(part, FRAME - 1, 0)
        total = part if total is None else total + part
    return total


def load_planes(parts, source):
    for p, ref in enumerate(parts):
        value = ref[...]
        source[1, p] = value
        source[0, p], source[2, p] = shifted_columns(value)


def row_bounds():
    device, plane, planes = lax.axis_index(GY), lax.axis_index(GZ), lax.axis_size(GZ)
    lowest = jnp.where(device > 0, 0, 8)
    highest = jnp.where(device < 31, FRAME, 40)

    def highest_at(here):
        return jnp.where((here >= 0) & (here < planes), highest, 0)

    return sublanes((FRAME, 128)), lowest, highest, lambda p: highest_at(plane + p)


def weight_of(weights_ref):
    return lambda a, b, c: weights_ref[9 * a + 3 * b + c]


def flipped_of(weights_ref):
    return lambda a, b, c: weights_ref[26 - 9 * a - 3 * b - c]


def apply_stencils(weights_ref, source, middle, back_ref):
    row, lowest, highest, highest_at = row_bounds()
    for p in range(3):
        valid = (row >= lowest) & (row < highest_at(p - 1))
        for k in range(8):
            cols = slice(128 * k, 128 * k + 128)
            value = stencil_sum(weight_of(weights_ref), source, p, cols)
            middle[1, p, :, cols] = jnp.where(valid, value, 0.0)
    for p in range(3):
        middle[0, p], middle[2, p] = shifted_columns(middle[1, p])
    inside = (row >= lowest) & (row < highest)
    for k in range(8):
        cols = slice(128 * k, 128 * k + 128)
        back_ref[:, cols] = jnp.where(inside, stencil_sum(flipped_of(weights_ref), middle, 0, cols), 0.0)


def row_of(values):
    lane = lanes((1, 128))
    out = jnp.zeros((1, 128), F32)
    for k, value in values:
        out = jnp.where(lane == k, jnp.sum(value), out)
    return out


def image_kernel(weights, table, blurred, upstream, u2, u1, o, d1, d2, image_ref, mapped_ref, out_ref, row_ref, *scratch):
    source, middle, back = scratch
    load_planes((u2, u1, o, d1, d2), source)
    apply_stencils(weights, source, middle, back)
    out_ref[...] = x_forward(back[8:40, :], table).reshape(32, 8, 128)
    mapped_ref[...] = middle[1, 1, 8:40, :]
    image_ref[...] = blurred[...] + back[...]
    b, ab, u = source[1, 2, 8:40, :], image_ref[8:40, :], upstream[...]
    row_ref[...] = row_of(((0, b * b), (1, b * ab), (2, ab * ab), (4, u * b), (5, u * ab)))


def map_kernel(weights, row_b, row_f, further, u1, o, d1, mapped_ref, out_ref, source):
    load_planes((u1, o, d1), source)
    row, lowest, highest, _ = row_bounds()
    inside = (row >= lowest) & (row < highest)
    for k in range(8):
        cols = slice(128 * k, 128 * k + 128)
        mapped_ref[:, cols] = jnp.where(inside, stencil_sum(weight_of(weights), source, 0, cols), 0.0)
    mapped = mapped_ref[8:40, :]
    sums = row_b[...] + row_f[...] + row_of(((3, mapped * mapped),))
    out_ref[...] = further[...]
    out_ref[:, 8, :] = further[:, 8, :] + pltpu.roll(jnp.broadcast_to(sums, (32, 128)), 8, 1)


def further_kernel(weights, u1, o, d1, back_ref, middle):
    load_planes((u1, o, d1), middle)
    row, lowest, highest, _ = row_bounds()
    inside = (row >= lowest) & (row < highest)
    for k in range(8):
        cols = slice(128 * k, 128 * k + 128)
        back_ref[:, cols] = jnp.where(inside, stencil_sum(flipped_of(weights), middle, 0, cols), 0.0)


def last_kernel(
    weights, table, image_back, upstream, u2, u1, o, d1, d2, mapped_ref, out_ref, source, middle, back
):
    load_planes((u2, u1, o, d1, d2), source)
    apply_stencils(weights, source, middle, back)
    mapped_ref[...] = middle[1, 1, 8:40, :]
    alpha, gamma, twice_g2, twice_g3 = weights[27], weights[28], weights[31], weights[32]
    u, again = upstream[...], image_back[8:40, :]
    first = alpha * u + twice_g2 * again + back[8:40, :]
    second = gamma * u + twice_g3 * again
    out_ref[:, 0:8, :] = x_forward(first, table).reshape(32, 8, 128)
    out_ref[:, 8:16, :] = x_forward(second, table).reshape(32, 8, 128)


def correlate_kernel(factor_ref, *refs):
    out_ref, scaled, mapped = refs[-3:]
    right, image, mixed = refs[0:3], refs[3:6], refs[6:9]
    right_map, image_map, mixed_map = refs[9:12]
    g1, twice_g2, twice_g3 = (factor_ref[k] for k in (33, 31, 32))
    for p in range(3):
        scaled[p] = mixed[p][...] + g1 * right[p][...] + twice_g2 * image[p][...]
    mapped[0] = mixed_map[...] + g1 * right_map[...] + twice_g2 * image_map[8:40, :]
    mapped[1] = right_map[...]
    mapped[2] = twice_g3 * image_map[8:40, :]
    lane = lanes((1, 128))
    out = jnp.zeros((1, 128), F32)
    column = lanes((ROWS, COLS))
    left_edge, right_edge = column < COLS - 1, column >= 1
    for c in range(3):
        parts = []
        for k in range(3):
            value = mapped[k]
            if c == 0:
                value = jnp.where(left_edge, pltpu.roll(value, COLS - 1, 1), 0.0)
            elif c == 2:
                value = jnp.where(right_edge, pltpu.roll(value, 1, 1), 0.0)
            parts.append(value)
        for a in range(3):
            for b in range(3):
                rows = slice(7 + b, 39 + b)
                total = parts[0] * right[a][rows, :] + parts[1] * scaled[a, rows, :] + parts[2] * image[a][rows, :]
                out = jnp.where(lane == 9 * a + 3 * b + c, jnp.sum(total), out)
    out_ref[...] = out


def shape(*dims):
    return jax.ShapeDtypeStruct(dims, F32)


STENCIL_SCRATCH = (
    pltpu.VMEM((3, 5, FRAME, COLS), F32),
    pltpu.VMEM((3, 3, FRAME, COLS), F32),
)
BACK_SCRATCH = (pltpu.VMEM((FRAME, COLS), F32),)


def call(body, out_shape, scalars, operands, scratch=(), far=(), planes=(), limit=VMEM, flops=400_000_000):
    operands = [*operands, *planes]
    smem, vmem, hbm = (pl.BlockSpec(memory_space=m) for m in (pltpu.SMEM, pltpu.VMEM, pltpu.HBM))
    outs = out_shape if isinstance(out_shape, tuple) else (out_shape,)
    first, count = len(scalars), len(scalars) + len(operands)
    buffers = [pltpu.VMEM(operands[i].shape, operands[i].dtype) for i in far]
    extra = [*buffers, pltpu.SemaphoreType.DMA((len(buffers),))] if buffers else []

    def whole(*refs):
        ins, results = list(refs[:count]), list(refs[count : count + len(outs)])
        own = refs[count + len(outs) :]
        held, sems, own = own[: len(buffers)], own[len(buffers)] if buffers else None, own[len(extra) :]
        copies = []
        for k, i in enumerate(far):
            copies.append(pltpu.make_async_copy(ins[first + i], held[k], sems.at[k]))
            ins[first + i] = held[k]
        for copy in copies:
            copy.start()
        for copy in copies:
            copy.wait()
        body(*ins, *results, *own)

    spec_in = [smem] * len(scalars) + [hbm if i in far else vmem for i in range(len(operands))]
    spec_out = (vmem,) * len(outs)
    return pl.pallas_call(
        whole,
        out_shape=out_shape,
        in_specs=spec_in,
        out_specs=spec_out if isinstance(out_shape, tuple) else spec_out[0],
        scratch_shapes=[*extra, *scratch],
        compiler_params=pltpu.CompilerParams(vmem_limit_bytes=limit),
        cost_estimate=pl.CostEstimate(flops=flops, bytes_accessed=4_000_000, transcendentals=0),
    )(*scalars, *operands)


def exchange(value):
    return lax.all_to_all(value, GY, 0, 0, tiled=True)


def moved(value, by):
    size = lax.axis_size(GZ)
    return lax.ppermute(value, GZ, [(i, i + by) for i in range(size) if 0 <= i + by < size])


def neighbours(value):
    return moved(value, 2), moved(value, 1), value, moved(value, -1), moved(value, -2)


def with_rows(value):
    size = lax.axis_size(GY)
    below = lax.ppermute(value[24:32], GY, [(i, i + 1) for i in range(size - 1)])
    above = lax.ppermute(value[0:8], GY, [(i + 1, i) for i in range(size - 1)])
    return jnp.concatenate([below, value, above], 0)


def from_all(row):
    size = lax.axis_size(GZ)
    return lax.all_to_all(jnp.broadcast_to(row[None], (size, 1, 128)), GZ, 0, 0, tiled=True)


def factors_of(m0, m1, m2, m3, u0, u1):
    def pair(m0, m1, m2, m3):
        step0 = m0 / m1
        norm1 = m0 - 2.0 * step0 * m1 + step0 * step0 * m2
        ratio = norm1 / m0
        keep = 1.0 + ratio
        curvature = keep * keep * m1 - 2.0 * keep * step0 * m2 + step0 * step0 * m3
        step1 = norm1 / curvature
        return step0 + step1 * keep, -step1 * step0

    (alpha, gamma), back = jax.vjp(pair, m0, m1, m2, m3)
    return (alpha, gamma, *back((u0, u1)))


def factors_kernel(weights_ref, rows, further, grown, out_ref, mixed_ref):
    total = jnp.sum(rows[...], 0)
    lane = lanes((1, 128))
    moments = [jnp.sum(jnp.where(lane == k, total, 0.0), axis=1, keepdims=True) for k in range(6)]
    alpha, gamma, g0, g1, g2, g3 = factors_of(*moments)
    for k in range(27):
        out_ref[k] = weights_ref[k]
    for k, value in enumerate((alpha, gamma, 2.0 * g0, 2.0 * g1, 2.0 * g2, 2.0 * g3, g1)):
        out_ref[27 + k] = value[0, 0]
    mixed_ref[...] = gamma * grown[...] + (2.0 * g3) * further[...]


def local(measured, point_spread, stencil_weights, upstream):
    cells = measured.size * lax.axis_size(GY) * lax.axis_size(GZ)
    weights = stencil_weights.reshape(27)
    table, along_y = jnp.asarray(X_TABLE), jnp.asarray(Y_TABLE)
    measured, upstream = measured[0], upstream[0]
    tile, tiles, three = shape(32, 8, 128), shape(32, 16, 128), shape(32, 24, 128)
    spectral, frame, rows, row = shape(32 * BLOCKS, 128), shape(FRAME, COLS), shape(ROWS, COLS), shape(1, 128)

    first = exchange(
        call(spread_kernel, tiles, [], [table, measured, point_spread], far=(0, 1, 2), limit=ALL_VMEM)
    )
    first, grown = lax.optimization_barrier((first, with_rows(upstream)))

    right_out, bank = call(first_filter_kernel, (three, shape(2, 32 * BLOCKS, 128)), [], [along_y, first])
    right, blurred = call(gather_two_kernel, (frame, frame), [], [table, exchange(right_out)])

    right_parts = neighbours(right)
    image, right_map, image_send, row_b = call(
        image_kernel,
        (frame, rows, tile, row),
        [weights],
        [table, blurred, upstream],
        STENCIL_SCRATCH + BACK_SCRATCH,
        planes=right_parts,
    )
    image_arrived = exchange(image_send)
    image_parts = (moved(image, 1), image, moved(image, -1))
    plane_scratch = (pltpu.VMEM((3, 3, FRAME, COLS), F32),)
    further_out, image_spectrum, row_f = call(
        second_filter_kernel, (tiles, spectral, row), [], [along_y, image_arrived, bank]
    )
    image_map, further_out = call(
        map_kernel, (frame, tiles), [weights], [row_b, row_f, further_out], plane_scratch, planes=image_parts
    )
    further_arrived = exchange(further_out)
    map_parts = (moved(image_map, 1), image_map, moved(image_map, -1))
    image_back = call(further_kernel, frame, [weights], [], plane_scratch, planes=map_parts)
    further_arrived, image_back = lax.optimization_barrier((further_arrived, image_back))

    further, row_sum = call(gather_sum_kernel, (frame, row), [], [table, further_arrived, image_back])
    smem, vmem = (pl.BlockSpec(memory_space=m) for m in (pltpu.SMEM, pltpu.VMEM))
    factors, mixed = pl.pallas_call(
        factors_kernel,
        out_shape=(shape(34), frame),
        in_specs=[smem, vmem, vmem, vmem],
        out_specs=(smem, vmem),
        compiler_params=pltpu.CompilerParams(vmem_limit_bytes=VMEM),
    )(weights, from_all(row_sum), further, grown)

    mixed_parts = neighbours(mixed)
    mixed_map, last_send = call(
        last_kernel,
        (rows, tiles),
        [factors],
        [table, image_back, upstream],
        STENCIL_SCRATCH + BACK_SCRATCH,
        planes=mixed_parts,
    )
    operands = [*right_parts[1:4], *image_parts, *mixed_parts[1:4], right_map, image_map, mixed_map]
    scratch = (pltpu.VMEM((3, FRAME, COLS), F32), pltpu.VMEM((3, ROWS, COLS), F32))
    terms = call(correlate_kernel, row, [factors], operands, scratch, far=tuple(range(12)), limit=ALL_VMEM)
    terms = lax.psum(terms, "gz_1")
    last_arrived = exchange(last_send)
    result_out = call(
        last_filter_kernel,
        tiles,
        [factors],
        [along_y, last_arrived, bank, image_spectrum, terms],
        far=(0, 2, 3, 4),
        limit=ALL_VMEM,
    )
    grad_measured, terms = call(final_kernel, (rows, row), [], [table, exchange(result_out)])
    grad_stencil = lax.psum(terms, "gz_0")[0, :27].reshape(3, 3, 3) / math.sqrt(cells)
    return grad_measured[None], grad_stencil


def solution(mesh):
    groups, planes = mesh.devices.shape
    finer = Mesh(mesh.devices.reshape(groups, 4, planes // 4), (GY, *GZ))
    return jax.shard_map(
        local,
        mesh=finer,
        in_specs=(P(GZ, GY, None), P(GY, None), P(), P(GZ, GY, None)),
        out_specs=(P(GZ, GY, None), P()),
        check_vma=False,
    )
```
